32 devices in a mesh: row: 8 (over z, x), col: 4 (over y, core).
Axes of the slice: x: 2, y: 2, z: 4, core: 2. Of those that a mesh axis runs over, the one named last changes fastest.
Arguments:
- inverse_set: float32 [1, 8, 128, 2, 4, 128], P(None, 'row', None, None, 'col'), may hold values from -6 to 6
- presence: int32 [1, 8, 2, 4], P(None, 'row', None, 'col'), may hold values 0 or 1
- factor: float32 [1, 8, 128, 512], P(None, 'row'), may hold values from -0.1875 to 0.1875
- dinv: float32 [512, 512], P('row', 'col'), may hold values from -6 to 6
Outputs:
- off_diag: float32 [1, 8, 128, 512], P(None, 'row', 'col')
- diag_block: float32 [512, 512], P('row', 'col')
The draws below stay inside these ranges and needn't reach their ends.
All inputs are finite; a program needn't handle non-finite values. No bound on the sum of `presence` on one device may be relied on, other than what follows from the above.
Results may differ from the reference program's by a relative error of at most 0.00007.
Values sent between devices are 32-bit elements; how exact they have to be, the bound alone decides.
No kernel may reach another device: no remote copies, remote signals or barrier semaphores. Data moves between devices by JAX's collectives and lax.ppermute only.
A program may use at most 64 MiB of HBM per device.

```python
import jax
import jax.numpy as jnp
from jax import lax

BR = 1
BS = 128
GR = 8
GC = 4
BC = 2
ORDER = 1024
PW = 512


def touch_ends(entries, own_key, least, largest):
    longest = entries.shape.index(max(entries.shape))
    spots = []
    for shift in (0, 1):
        where = [jax.random.randint(jax.random.fold_in(own_key, axis), (), 0, length) for axis, length in enumerate(entries.shape)]
        where[longest] = (where[longest] + shift) % entries.shape[longest]
        spots.append(tuple(where))
    return entries.at[spots[0]].set(least).at[spots[1]].set(largest)


def block_scale(own_key, shape, split, low, high):
    gain, own = 1.0, jax.random.fold_in(own_key, 6)
    for axis_at, shards_of in split:
        draws = jnp.exp(jax.random.uniform(jax.random.fold_in(own, axis_at), (shards_of,), jnp.float32, low / len(split), high / len(split)))
        gain = gain * jnp.repeat(draws, shape[axis_at] // shards_of).reshape([-1 if axis == axis_at else 1 for axis in range(len(shape))])
    return gain


def bell_draw(key, extent, spread, bound, cuts=(), held_as=jnp.bfloat16):
    entries = spread * jax.random.normal(key, extent, jnp.float32)
    if cuts:
        entries = entries * block_scale(key, extent, cuts, -0.22, 0.18)
    return jnp.clip(entries, -bound, bound).astype(held_as)


def setup_inputs(seed: int = 0) -> dict:
    streams_of = jax.random.split(jax.random.key(seed), 5)
    inverse_set = bell_draw(streams_of[0], (BR, GR, BS, BC, GC, BS), 1.0, 6.0, ((1, 8), (4, 4)), jnp.float32)
    presence = touch_ends((jax.random.randint(streams_of[1], (BR, GR, BC, GC), 0, 20) < 17).astype(jnp.int32), jax.random.fold_in(streams_of[1], 1), 0, 1)
    factor = bell_draw(streams_of[2], (BR, GR, BS, PW), ORDER ** -0.5, 0.1875, ((1, 8),), jnp.float32)
    dinv = bell_draw(streams_of[3], (PW, PW), 1.0, 6.0, ((0, 8), (1, 4)), jnp.float32)
    return dict(inverse_set=inverse_set, presence=presence, factor=factor, dinv=dinv)


def reference(inverse_set, presence, factor, dinv):
    flat = factor.reshape(BR * GR * BS, PW)
    weights = presence.astype(inverse_set.dtype)

    def one_row(args):
        blocks, marks = args
        masked = blocks * marks[:, None, :, :, None]
        return jnp.dot(masked.reshape(GR * BS, BR * GR * BS), flat, precision=lax.Precision.HIGHEST, preferred_element_type=jnp.float32)

    update = lax.map(one_row, (inverse_set, weights))
    update = update.reshape(BR, GR, BS, PW)
    off_diag = -update
    diag_block = dinv + jnp.dot(flat.T, update.reshape(BR * GR * BS, PW), precision=lax.Precision.HIGHEST, preferred_element_type=jnp.float32)
    return (off_diag, diag_block)
```

```python
import jax
import jax.numpy as jnp
from jax import lax
from jax.sharding import PartitionSpec as P

HI = lax.Precision.HIGHEST


def to_all(value, axis):
    copies = jnp.broadcast_to(value[None], (lax.axis_size(axis),) + value.shape)
    return lax.all_to_all(copies, axis, 0, 0)


def local(inverse_set, presence, factor, dinv):
    groups_row = lax.axis_size("row")
    groups_col = lax.axis_size("col")
    col_index = lax.axis_index("col")
    block_rows, _, order, width = factor.shape
    block_cols = inverse_set.shape[3]
    total = block_cols * groups_col * order
    span = width // groups_col
    share = order // groups_col
    rows = block_rows * order

    own = factor[:, 0]
    masked = (
        inverse_set[:, 0, :, :, 0, :] * presence[:, 0, :, 0].astype(jnp.float32)[:, None, :, None]
    )
    columns = to_all(lax.dynamic_slice_in_dim(own, col_index * span, span, 2), "row")
    columns = columns.transpose(1, 0, 2, 3).reshape(total, span)
    wide = to_all(masked, "col")
    wide = wide.transpose(1, 2, 3, 0, 4).reshape(rows, total)
    update = jnp.dot(wide, columns, precision=HI)

    parts = update.reshape(block_rows, groups_col, share, span).transpose(1, 0, 2, 3)
    parts = lax.all_to_all(-parts, "col", 0, 0)
    off_diag = parts.transpose(1, 2, 0, 3).reshape(block_rows, 1, share, width)

    terms = jnp.dot(own.reshape(rows, width).T, update, precision=HI)
    terms = terms.reshape(groups_row, width // groups_row, span)
    terms = lax.all_to_all(terms, "row", 0, 0)
    diag_block = dinv + terms.sum(axis=0)
    return (off_diag, diag_block)


def solution(mesh):
    in_specs = (
        P(None, "row", None, None, "col", None),
        P(None, "row", None, "col"),
        P(None, "row", None, None),
        P("row", "col"),
    )
    out_specs = (P(None, "row", "col", None), P("row", "col"))
    return jax.shard_map(local, mesh=mesh, in_specs=in_specs, out_specs=out_specs, check_vma=False)
```

```python
import jax
import jax.numpy as jnp
from jax import lax
from jax.sharding import PartitionSpec as P

HI = lax.Precision.HIGHEST


def shifted(value, axis, step):
    size = lax.axis_size(axis)
    return lax.ppermute(value, axis, [(i, (i + step) % size) for i in range(size)])


def to_all(value, axis):
    size = lax.axis_size(axis)
    return jnp.stack([shifted(value, axis, step) for step in range(size - 1, 0, -1)] + [value])


def turned(values, axis_at, first, size):
    twice = jnp.concatenate([values, values], axis=axis_at)
    return lax.dynamic_slice_in_dim(twice, first, size, axis_at)


def swap(values, axis):
    size = lax.axis_size(axis)
    me = lax.axis_index(axis)
    pieces = []
    for step in range(size):
        piece = lax.dynamic_index_in_dim(values, (me + step) % size, 0, keepdims=False)
        pieces.append(shifted(piece, axis, step) if step else piece)
    return pieces


def local(inverse_set, presence, factor, dinv):
    groups_row = lax.axis_size("row")
    groups_col = lax.axis_size("col")
    row_index = lax.axis_index("row")
    col_index = lax.axis_index("col")
    block_rows, _, order, width = factor.shape
    block_cols = inverse_set.shape[3]
    total = block_cols * groups_col * order
    span = width // groups_col
    share = order // groups_col
    rows = block_rows * order

    own = factor[:, 0]
    columns = to_all(lax.dynamic_slice_in_dim(own, col_index * span, span, 2), "row")
    columns = columns.transpose(1, 0, 2, 3).reshape(total, span)
    masked = (
        inverse_set[:, 0, :, :, 0, :] * presence[:, 0, :, 0].astype(jnp.float32)[:, None, :, None]
    )
    wide = to_all(masked, "col")
    wide = turned(wide, 0, (groups_col - 1 - col_index) % groups_col, groups_col)
    wide = wide.transpose(1, 2, 3, 0, 4).reshape(rows, block_rows, groups_row, order)
    wide = turned(wide, 2, (row_index + 1) % groups_row, groups_row).reshape(rows, total)
    update = jnp.dot(wide, columns, precision=HI)

    parts = update.reshape(block_rows, groups_col, share, span).transpose(1, 0, 2, 3)
    parts = jnp.stack(swap(-parts, "col")[::-1])
    parts = turned(parts, 0, (groups_col - 1 - col_index) % groups_col, groups_col)
    off_diag = parts.transpose(1, 2, 0, 3).reshape(block_rows, 1, share, width)

    terms = jnp.dot(own.reshape(rows, width).T, update, precision=HI)
    terms = terms.reshape(groups_row, width // groups_row, span)
    diag_block = dinv + sum(swap(terms, "row"))
    return (off_diag, diag_block)


def solution(mesh):
    in_specs = (
        P(None, "row", None, None, "col", None),
        P(None, "row", None, "col"),
        P(None, "row", None, None),
        P("row", "col"),
    )
    out_specs = (P(None, "row", "col", None), P("row", "col"))
    return jax.shard_map(local, mesh=mesh, in_specs=in_specs, out_specs=out_specs, check_vma=False)
```

```python
import jax
import jax.numpy as jnp
from jax import lax
from jax.sharding import PartitionSpec as P

HI = lax.Precision.HIGHEST


def flipped(value, axis, flip):
    return lax.ppermute(value, axis, [(i, i ^ flip) for i in range(lax.axis_size(axis))])


def to_all(value, axis):
    copies = jnp.broadcast_to(value[None], (lax.axis_size(axis),) + value.shape)
    return lax.all_to_all(copies, axis, 0, 0)


def doubled(value, axis):
    me = lax.axis_index(axis)
    held = value[None]
    bit = 1
    while bit < lax.axis_size(axis):
        other = flipped(held, axis, bit)
        upper = (me & bit) != 0
        held = jnp.concatenate([jnp.where(upper, other, held), jnp.where(upper, held, other)])
        bit *= 2
    return held


def swap(values, axis):
    size = lax.axis_size(axis)
    me = lax.axis_index(axis)
    pieces = []
    for flip in range(size):
        piece = lax.dynamic_index_in_dim(values, me ^ flip, 0, keepdims=False)
        pieces.append(flipped(piece, axis, flip) if flip else piece)
    held = [piece[None] for piece in pieces]
    bit = 1
    while bit < size:
        upper = (me & bit) != 0
        held = [
            jnp.concatenate([jnp.where(upper, b, a), jnp.where(upper, a, b)])
            for a, b in zip(held[::2], held[1::2])
        ]
        bit *= 2
    return held[0]


def local(inverse_set, presence, factor, dinv):
    groups_row = lax.axis_size("row")
    groups_col = lax.axis_size("col")
    col_index = lax.axis_index("col")
    block_rows, _, order, width = factor.shape
    block_cols = inverse_set.shape[3]
    total = block_cols * groups_col * order
    span = width // groups_col
    share = order // groups_col
    rows = block_rows * order

    own = factor[:, 0]
    columns = to_all(lax.dynamic_slice_in_dim(own, col_index * span, span, 2), "row")
    columns = columns.transpose(1, 0, 2, 3).reshape(total, span)
    masked = (
        inverse_set[:, 0, :, :, 0, :] * presence[:, 0, :, 0].astype(jnp.float32)[:, None, :, None]
    )
    wide = doubled(masked, "col")
    wide = wide.transpose(1, 2, 3, 0, 4).reshape(rows, total)
    update = jnp.dot(wide, columns, precision=HI)

    terms = jnp.dot(own.reshape(rows, width).T, update, precision=HI)
    terms = terms.reshape(groups_row, width // groups_row, span)
    diag_block = dinv + lax.all_to_all(terms, "row", 0, 0).sum(axis=0)

    parts = update.reshape(block_rows, groups_col, share, span).transpose(1, 0, 2, 3)
    parts = swap(-parts, "col")
    off_diag = parts.transpose(1, 2, 0, 3).reshape(block_rows, 1, share, width)
    return (off_diag, diag_block)


def solution(mesh):
    in_specs = (
        P(None, "row", None, None, "col", None),
        P(None, "row", None, "col"),
        P(None, "row", None, None),
        P("row", "col"),
    )
    out_specs = (P(None, "row", "col", None), P("row", "col"))
    return jax.shard_map(local, mesh=mesh, in_specs=in_specs, out_specs=out_specs, check_vma=False)
```

```python
import jax
import jax.numpy as jnp
from jax import lax
from jax.sharding import PartitionSpec as P

HI = lax.Precision.HIGHEST


def flipped(value, axis, flip):
    return lax.ppermute(value, axis, [(i, i ^ flip) for i in range(lax.axis_size(axis))])


def ordered(lower_first, first, second):
    return jnp.stack([jnp.where(lower_first, first, second), jnp.where(lower_first, second, first)])


def swap(values, axis):
    size = lax.axis_size(axis)
    me = lax.axis_index(axis)
    held = []
    for flip in range(size):
        piece = lax.dynamic_index_in_dim(values, me ^ flip, 0, keepdims=True)
        held.append(flipped(piece, axis, flip) if flip else piece)
    bit = 1
    while bit < size:
        lower = (me & bit) == 0
        held = [
            ordered(lower, a, b).reshape((2 * a.shape[0],) + a.shape[1:])
            for a, b in zip(held[::2], held[1::2])
        ]
        bit *= 2
    return held[0]


def pair_rows(masked):
    groups_row = lax.axis_size("row")
    groups_col = lax.axis_size("col")
    row_bit = lax.axis_index("row") & 1
    col_index = lax.axis_index("col")
    col_bit = col_index & 1
    cross = [
        (r * groups_col + c, (r ^ 1) * groups_col + (c ^ 1))
        for r in range(groups_row)
        for c in range(groups_col)
        if (r ^ c) & 1
    ]
    held = jnp.where(row_bit == col_bit, masked, lax.ppermute(masked, ("row", "col"), cross))[None]
    bit = 2
    while bit < groups_col:
        other = flipped(held, "col", bit)
        lower = (col_index & bit) == 0
        held = ordered(lower, held, other).reshape((2 * held.shape[0],) + held.shape[1:])
        bit *= 2
    return ordered(col_bit == 0, held, flipped(held, "col", 1))


def local(inverse_set, presence, factor, dinv):
    groups_row = lax.axis_size("row")
    groups_col = lax.axis_size("col")
    row_bit = lax.axis_index("row") & 1
    col_index = lax.axis_index("col")
    block_rows, _, order, width = factor.shape
    block_cols = inverse_set.shape[3]
    half = block_cols * (groups_col // 2) * order
    span = width // groups_col
    share = order // groups_col
    rows = block_rows * order

    own = factor[:, 0]
    mine = lax.dynamic_slice_in_dim(own, col_index * span, span, 2)
    lines = [list(range(bit, groups_row, 2)) for bit in range(2)]
    copies = jnp.broadcast_to(mine[None], (groups_row // 2,) + mine.shape)
    columns = lax.all_to_all(copies, "row", 0, 0, axis_index_groups=lines)
    columns = columns.transpose(1, 0, 2, 3).reshape(half, span)

    masked = (
        inverse_set[:, 0, :, :, 0, :] * presence[:, 0, :, 0].astype(jnp.float32)[:, None, :, None]
    )
    wide = pair_rows(masked).transpose(0, 2, 3, 4, 1, 5).reshape(2 * rows, half)
    pair_factor = ordered(row_bit == 0, own, flipped(own, "row", 1)).reshape(2 * rows, width)

    partial_pair = jnp.dot(wide, columns, precision=HI)
    terms = jnp.dot(pair_factor.T, partial_pair, precision=HI)
    terms = terms.reshape(groups_row, width // groups_row, span)
    diag_block = dinv + lax.all_to_all(terms, "row", 0, 0).sum(axis=0)

    partial_pair = -partial_pair.reshape(2, rows, span)
    kept = lax.dynamic_index_in_dim(partial_pair, row_bit, 0, keepdims=False)
    sent = lax.dynamic_index_in_dim(partial_pair, 1 - row_bit, 0, keepdims=False)
    parts = (kept + flipped(sent, "row", 1)).reshape(block_rows, groups_col, share, span)
    parts = swap(parts.transpose(1, 0, 2, 3), "col")
    off_diag = parts.transpose(1, 2, 0, 3).reshape(block_rows, 1, share, width)
    return (off_diag, diag_block)


def solution(mesh):
    in_specs = (
        P(None, "row", None, None, "col", None),
        P(None, "row", None, "col"),
        P(None, "row", None, None),
        P("row", "col"),
    )
    out_specs = (P(None, "row", "col", None), P("row", "col"))
    return jax.shard_map(local, mesh=mesh, in_specs=in_specs, out_specs=out_specs, check_vma=False)
```

```python
import functools

import jax
import jax.numpy as jnp
from jax import lax
from jax.experimental import pallas as pl
from jax.experimental.pallas import tpu as pltpu
from jax.sharding import PartitionSpec as P

LANES = 128
WHOLE = pl.BlockSpec(memory_space=pltpu.VMEM)
LIGHT = pl.CostEstimate(flops=1000, bytes_accessed=1000, transcendentals=0)


def flipped(value, axis, flip):
    return lax.ppermute(value, axis, [(i, i ^ flip) for i in range(lax.axis_size(axis))])


def two_parts(value):
    high = value.astype(jnp.bfloat16)
    return high, (value - high.astype(jnp.float32)).astype(jnp.bfloat16)


def product(left, right, contract):
    left_high, left_low = two_parts(left)
    right_high, right_low = two_parts(right)

    def once(a, b):
        return lax.dot_general(a, b, (contract, ((), ())), preferred_element_type=jnp.float32)

    return once(left_high, right_high) + (once(left_high, right_low) + once(left_low, right_high))


def prepare_kernel(presence, blocks, factor, masked, copies, sems):
    count, rows, span = copies.shape
    first = pl.multiple_of(lax.axis_index("col") * span, LANES)
    sends = [
        pltpu.make_async_copy(factor.at[:, pl.ds(first, span)], copies.at[i], sems.at[i])
        for i in range(count)
    ]
    for send in sends:
        send.start()
    block_cols, _, order = masked.shape
    block_rows = rows // order
    for a in range(block_rows):
        for b in range(block_cols):
            weight = presence[a * block_cols + b].astype(jnp.float32)
            picked = blocks[pl.ds(a * order * block_cols + b, order, stride=block_cols), :]
            masked[b, pl.ds(a * order, order), :] = picked * weight
    for send in sends:
        send.wait()


def prepare(presence, blocks, own, receivers, span):
    rows, width = own.shape
    block_cols = blocks.shape[0] // rows
    order = blocks.shape[1]
    if span % LANES:
        first = lax.axis_index("col") * span
        mine = lax.dynamic_slice_in_dim(own, first, span, 1)
        weights = presence.reshape(-1, 1, block_cols, 1).astype(jnp.float32)
        picked = blocks.reshape(-1, order, block_cols, order) * weights
        masked = picked.transpose(2, 0, 1, 3).reshape(block_cols, rows, order)
        return masked, jnp.broadcast_to(mine[None], (receivers, rows, span))
    return pl.pallas_call(
        prepare_kernel,
        out_shape=(
            jax.ShapeDtypeStruct((block_cols, rows, order), jnp.float32),
            jax.ShapeDtypeStruct((receivers, rows, span), jnp.float32),
        ),
        in_specs=[pl.BlockSpec(memory_space=pltpu.SMEM), WHOLE, pl.BlockSpec(memory_space=pl.ANY)],
        out_specs=(WHOLE, pl.BlockSpec(memory_space=pl.ANY)),
        scratch_shapes=[pltpu.SemaphoreType.DMA((receivers,))],
        cost_estimate=LIGHT,
    )(presence, blocks, own)


def middle_kernel(count, *refs):
    pieces = refs[: 2 * count]
    columns, own, near, terms, kept, sent = refs[2 * count :]
    block_cols, rows, _ = pieces[0].shape
    col_index = lax.axis_index("col")
    left, right = [], []
    for t in range(count):
        for b in range(block_cols):
            left.append(jnp.concatenate([pieces[t][b], pieces[count + t][b]], axis=0))
            right.append(columns[b * count + ((col_index >> 1) ^ t)])
    both = product(jnp.concatenate(left, axis=1), jnp.concatenate(right, axis=0), ((1,), (0,)))
    first, second = both[:rows], both[rows:]
    same = (lax.axis_index("row") & 1) == (col_index & 1)
    mine = jnp.where(same, first, second)
    other = jnp.where(same, second, first)
    kept[...] = -mine
    sent[...] = -other
    factors = jnp.concatenate([own[...], near[...]], axis=0)
    terms[...] = product(factors, jnp.concatenate([mine, other], axis=0), ((0,), (0,)))


def middle(pieces, columns, own, near):
    rows, width = own.shape
    span = columns.shape[2]
    part = jax.ShapeDtypeStruct((rows, span), jnp.float32)
    return pl.pallas_call(
        functools.partial(middle_kernel, len(pieces) // 2),
        out_shape=(jax.ShapeDtypeStruct((width, span), jnp.float32), part, part),
        in_specs=[WHOLE] * (len(pieces) + 3),
        out_specs=(WHOLE,) * 3,
        cost_estimate=LIGHT,
        compiler_params=pltpu.CompilerParams(vmem_limit_bytes=32 * 1024 * 1024),
    )(*pieces, columns, own, near)


def collect_kernel(*refs):
    out = refs[-1]
    span = refs[0].shape[1]
    for flip, piece in enumerate(refs[:-1]):
        first = pl.multiple_of((lax.axis_index("col") ^ flip) * span, LANES)
        out[:, pl.ds(first, span)] = piece[...]


def collect(held):
    share, span = held[0].shape
    if span % LANES:
        me = lax.axis_index("col")
        stacked = jnp.stack(held)
        return jnp.concatenate(
            [lax.dynamic_index_in_dim(stacked, me ^ j, 0, keepdims=False) for j in range(len(held))],
            axis=1,
        )
    return pl.pallas_call(
        collect_kernel,
        out_shape=jax.ShapeDtypeStruct((share, span * len(held)), jnp.float32),
        in_specs=[WHOLE] * len(held),
        out_specs=WHOLE,
        cost_estimate=LIGHT,
    )(*held)


def pair_rows(masked):
    groups_row = lax.axis_size("row")
    groups_col = lax.axis_size("col")
    cross = []
    for r in range(groups_row):
        for c in range(groups_col):
            odd = (r ^ c) & 1
            cross.append((r * groups_col + c, (r ^ odd) * groups_col + (c ^ odd)))
    held = lax.ppermute(masked, ("row", "col"), cross)
    held = [held] + [flipped(held, "col", flip) for flip in range(2, groups_col, 2)]
    return held + [flipped(piece, "col", 1) for piece in held]


def local(inverse_set, presence, factor, dinv):
    groups_row = lax.axis_size("row")
    groups_col = lax.axis_size("col")
    col_index = lax.axis_index("col")
    block_rows, _, order, width = factor.shape
    block_cols = inverse_set.shape[3]
    span = width // groups_col
    rows = block_rows * order
    share = order // groups_col

    own = factor.reshape(rows, width)
    blocks = inverse_set.reshape(rows * block_cols, order)
    masked, copies = prepare(presence.reshape(-1), blocks, own, groups_row // 2, span)
    lines = [list(range(bit, groups_row, 2)) for bit in range(2)]
    columns = lax.all_to_all(copies, "row", 0, 0, axis_index_groups=lines)
    columns = columns.reshape(groups_row // 2, block_rows, order, span).transpose(1, 0, 2, 3)
    columns = columns.reshape(-1, order, span)
    pieces = pair_rows(masked)
    near = flipped(own, "row", 1)

    terms, kept, sent = middle(pieces, columns, own, near)
    terms = lax.all_to_all(terms.reshape(groups_row, width // groups_row, span), "row", 0, 0)
    diag_block = dinv + terms.sum(axis=0)

    update = (kept + flipped(sent, "row", 1)).reshape(block_rows, groups_col, share, span)
    held = []
    for flip in range(groups_col):
        piece = lax.dynamic_index_in_dim(update, col_index ^ flip, 1, keepdims=False)
        piece = piece.reshape(block_rows * share, span)
        held.append(flipped(piece, "col", flip) if flip else piece)
    off_diag = collect(held).reshape(block_rows, 1, share, width)
    return (off_diag, diag_block)


def solution(mesh):
    in_specs = (
        P(None, "row", None, None, "col", None),
        P(None, "row", None, "col"),
        P(None, "row", None, None),
        P("row", "col"),
    )
    out_specs = (P(None, "row", "col", None), P("row", "col"))
    return jax.shard_map(local, mesh=mesh, in_specs=in_specs, out_specs=out_specs, check_vma=False)
```

```python
import functools

import jax
import jax.numpy as jnp
from jax import lax
from jax.experimental import pallas as pl
from jax.experimental.pallas import tpu as pltpu
from jax.sharding import PartitionSpec as P

LANES = 128
WHOLE = pl.BlockSpec(memory_space=pltpu.VMEM)
LIGHT = pl.CostEstimate(flops=1000, bytes_accessed=1000, transcendentals=0)


def flipped(value, axis, flip):
    return lax.ppermute(value, axis, [(i, i ^ flip) for i in range(lax.axis_size(axis))])


def two_parts(value):
    high = value.astype(jnp.bfloat16)
    return high, (value - high.astype(jnp.float32)).astype(jnp.bfloat16)


def product(left, right, contract):
    left_high, left_low = two_parts(left)
    right_high, right_low = two_parts(right)

    def once(a, b):
        return lax.dot_general(a, b, (contract, ((), ())), preferred_element_type=jnp.float32)

    return once(left_high, right_high) + (once(left_high, right_low) + once(left_low, right_high))


def prepare_kernel(presence, blocks, factor, masked, copies):
    count, rows, span = copies.shape
    first = pl.multiple_of(lax.axis_index("col") * span, LANES)
    mine = factor[:, pl.ds(first, span)]
    for i in range(count):
        copies[i] = mine
    block_cols, _, order = masked.shape
    for a in range(rows // order):
        for b in range(block_cols):
            weight = presence[a * block_cols + b].astype(jnp.float32)
            picked = blocks[pl.ds(a * order * block_cols + b, order, stride=block_cols), :]
            masked[b, pl.ds(a * order, order), :] = picked * weight


def prepare(presence, blocks, own, receivers, span):
    rows, width = own.shape
    block_cols = blocks.shape[0] // rows
    order = blocks.shape[1]
    if span % LANES:
        first = lax.axis_index("col") * span
        mine = lax.dynamic_slice_in_dim(own, first, span, 1)
        weights = presence.reshape(-1, 1, block_cols, 1).astype(jnp.float32)
        picked = blocks.reshape(-1, order, block_cols, order) * weights
        masked = picked.transpose(2, 0, 1, 3).reshape(block_cols, rows, order)
        return masked, jnp.broadcast_to(mine[None], (receivers, rows, span))
    return pl.pallas_call(
        prepare_kernel,
        out_shape=(
            jax.ShapeDtypeStruct((block_cols, rows, order), jnp.float32),
            jax.ShapeDtypeStruct((receivers, rows, span), jnp.float32),
        ),
        in_specs=[pl.BlockSpec(memory_space=pltpu.SMEM), WHOLE, WHOLE],
        out_specs=(WHOLE, WHOLE),
        cost_estimate=LIGHT,
    )(presence, blocks, own)


def middle_kernel(count, *refs):
    pieces = refs[: 2 * count]
    columns, own, near, dinv, terms = refs[2 * count : 2 * count + 5]
    outward = refs[2 * count + 5 :]
    block_cols, rows, order = pieces[0].shape
    col_index = lax.axis_index("col")
    row_index = lax.axis_index("row")
    left, right = [], []
    for t in range(count):
        for b in range(block_cols):
            left.append(jnp.concatenate([pieces[t][b], pieces[count + t][b]], axis=0))
            right.append(columns[b * count + ((col_index >> 1) ^ t)])
    both = product(jnp.concatenate(left, axis=1), jnp.concatenate(right, axis=0), ((1,), (0,)))
    first, second = both[:rows], both[rows:]
    same = (row_index & 1) == (col_index & 1)
    mine = jnp.where(same, first, second)
    other = jnp.where(same, second, first)
    factors = jnp.concatenate([own[...], near[...]], axis=0)
    terms[...] = product(factors, jnp.concatenate([mine, other], axis=0), ((0,), (0,)))
    tall = dinv.shape[0]
    here = pl.ds(pl.multiple_of(row_index * tall, 8), tall)
    terms[here, :] = terms[here, :] + dinv[...]

    scratch = outward[-1]
    flips = len(outward[:-1]) // 2
    share = order // flips
    for near_row, value in enumerate((mine, other)):
        scratch[...] = -value
        for flip in range(flips):
            start = (col_index ^ flip) * share
            for a in range(rows // order):
                picked = scratch[pl.ds(pl.multiple_of(a * order + start, 8), share), :]
                outward[near_row * flips + flip][pl.ds(a * share, share), :] = picked


def middle(pieces, columns, own, near, dinv, flips):
    rows, width = own.shape
    span = columns.shape[2]
    part = jax.ShapeDtypeStruct((rows // flips, span), jnp.float32)
    return pl.pallas_call(
        functools.partial(middle_kernel, len(pieces) // 2),
        out_shape=(jax.ShapeDtypeStruct((width, span), jnp.float32),) + (part,) * (2 * flips),
        in_specs=[WHOLE] * (len(pieces) + 4),
        out_specs=(WHOLE,) * (1 + 2 * flips),
        scratch_shapes=[pltpu.VMEM((rows, span), jnp.float32)],
        cost_estimate=LIGHT,
        compiler_params=pltpu.CompilerParams(vmem_limit_bytes=32 * 1024 * 1024),
    )(*pieces, columns, own, near, dinv)


def exchange(outward, flips):
    groups_row = lax.axis_size("row")
    groups_col = lax.axis_size("col")
    arrived = []
    for index, piece in enumerate(outward):
        near_row, flip = divmod(index, flips)
        pairs = [
            (r * groups_col + c, (r ^ near_row) * groups_col + (c ^ flip))
            for r in range(groups_row)
            for c in range(groups_col)
        ]
        arrived.append(lax.ppermute(piece, ("row", "col"), pairs) if index else piece)
    return [arrived[flip] + arrived[flips + flip] for flip in range(flips)]


def side_by_side(held):
    me = lax.axis_index("col")
    size = len(held)
    return jnp.concatenate([lax.select_n(me ^ j, *held) for j in range(size)], axis=1)


def pair_rows(masked):
    groups_row = lax.axis_size("row")
    groups_col = lax.axis_size("col")
    cross = []
    for r in range(groups_row):
        for c in range(groups_col):
            odd = (r ^ c) & 1
            cross.append((r * groups_col + c, (r ^ odd) * groups_col + (c ^ odd)))
    held = lax.ppermute(masked, ("row", "col"), cross)
    held = [held] + [flipped(held, "col", flip) for flip in range(2, groups_col, 2)]
    return held + [flipped(piece, "col", 1) for piece in held]


def local(inverse_set, presence, factor, dinv):
    groups_row = lax.axis_size("row")
    groups_col = lax.axis_size("col")
    block_rows, _, order, width = factor.shape
    block_cols = inverse_set.shape[3]
    span = width // groups_col
    rows = block_rows * order
    share = order // groups_col

    own = factor.reshape(rows, width)
    blocks = inverse_set.reshape(rows * block_cols, order)
    masked, copies = prepare(presence.reshape(-1), blocks, own, groups_row // 2, span)
    lines = [list(range(bit, groups_row, 2)) for bit in range(2)]
    columns = lax.all_to_all(copies, "row", 0, 0, axis_index_groups=lines)
    columns = columns.reshape(groups_row // 2, block_rows, order, span).transpose(1, 0, 2, 3)
    columns = columns.reshape(-1, order, span)
    pieces = pair_rows(masked)
    near = flipped(own, "row", 1)

    terms, *outward = middle(pieces, columns, own, near, dinv, groups_col)
    terms = lax.all_to_all(terms.reshape(groups_row, width // groups_row, span), "row", 0, 0)
    diag_block = terms.sum(axis=0)

    off_diag = side_by_side(exchange(outward, groups_col))
    return (off_diag.reshape(block_rows, 1, share, width), diag_block)


def solution(mesh):
    in_specs = (
        P(None, "row", None, None, "col", None),
        P(None, "row", None, "col"),
        P(None, "row", None, None),
        P("row", "col"),
    )
    out_specs = (P(None, "row", "col", None), P("row", "col"))
    return jax.shard_map(local, mesh=mesh, in_specs=in_specs, out_specs=out_specs, check_vma=False)
```

```python
import functools

import jax
import jax.numpy as jnp
from jax import lax
from jax.experimental import pallas as pl
from jax.experimental.pallas import tpu as pltpu
from jax.sharding import PartitionSpec as P

LANES = 128
WHOLE = pl.BlockSpec(memory_space=pltpu.VMEM)
LIGHT = pl.CostEstimate(flops=1000, bytes_accessed=1000, transcendentals=0)


def flipped(value, axis, flip):
    return lax.ppermute(value, axis, [(i, i ^ flip) for i in range(lax.axis_size(axis))])


def two_parts(value):
    high = value.astype(jnp.bfloat16)
    return high, (value - high.astype(jnp.float32)).astype(jnp.bfloat16)


def product(left, right, contract):
    left_high, left_low = two_parts(left)
    right_high, right_low = two_parts(right)

    def once(a, b):
        return lax.dot_general(a, b, (contract, ((), ())), preferred_element_type=jnp.float32)

    return once(left_high, right_high) + (once(left_high, right_low) + once(left_low, right_high))


def prepare_kernel(presence, blocks, factor, masked, copies):
    count, rows, span = copies.shape
    first = pl.multiple_of(lax.axis_index("col") * span, LANES)
    mine = factor[:, pl.ds(first, span)]
    for i in range(count):
        copies[i] = mine
    block_cols, _, order = masked.shape
    for a in range(rows // order):
        for b in range(block_cols):
            weight = presence[a * block_cols + b].astype(jnp.float32)
            picked = blocks[pl.ds(a * order * block_cols + b, order, stride=block_cols), :]
            masked[b, pl.ds(a * order, order), :] = picked * weight


def prepare(presence, blocks, own, receivers, span):
    rows, width = own.shape
    block_cols = blocks.shape[0] // rows
    order = blocks.shape[1]
    if span % LANES:
        first = lax.axis_index("col") * span
        mine = lax.dynamic_slice_in_dim(own, first, span, 1)
        weights = presence.reshape(-1, 1, block_cols, 1).astype(jnp.float32)
        picked = blocks.reshape(-1, order, block_cols, order) * weights
        masked = picked.transpose(2, 0, 1, 3).reshape(block_cols, rows, order)
        return masked, jnp.broadcast_to(mine[None], (receivers, rows, span))
    return pl.pallas_call(
        prepare_kernel,
        out_shape=(
            jax.ShapeDtypeStruct((block_cols, rows, order), jnp.float32),
            jax.ShapeDtypeStruct((receivers, rows, span), jnp.float32),
        ),
        in_specs=[pl.BlockSpec(memory_space=pltpu.SMEM), WHOLE, WHOLE],
        out_specs=(WHOLE, WHOLE),
        cost_estimate=LIGHT,
    )(presence, blocks, own)


def middle_kernel(count, *refs):
    pieces = refs[: 2 * count]
    columns, own, near, dinv, terms = refs[2 * count : 2 * count + 5]
    outward = refs[2 * count + 5 :]
    block_cols, rows, order = pieces[0].shape
    col_index = lax.axis_index("col")
    row_index = lax.axis_index("row")
    left, right = [], []
    for t in range(count):
        for b in range(block_cols):
            left.append(jnp.concatenate([pieces[t][b], pieces[count + t][b]], axis=0))
            right.append(columns[b * count + ((col_index >> 1) ^ t)])
    both = product(jnp.concatenate(left, axis=1), jnp.concatenate(right, axis=0), ((1,), (0,)))
    first, second = both[:rows], both[rows:]
    same = (row_index & 1) == (col_index & 1)
    mine = jnp.where(same, first, second)
    other = jnp.where(same, second, first)
    factors = jnp.concatenate([own[...], near[...]], axis=0)
    terms[...] = product(factors, jnp.concatenate([mine, other], axis=0), ((0,), (0,)))
    tall = dinv.shape[0]
    here = pl.ds(pl.multiple_of(row_index * tall, 8), tall)
    terms[here, :] = terms[here, :] + dinv[...]

    scratch = outward[-1]
    flips = len(outward[:-1]) // 2
    share = order // flips
    for near_row, value in enumerate((mine, other)):
        scratch[...] = -value
        for flip in range(flips):
            start = (col_index ^ flip) * share
            for a in range(rows // order):
                picked = scratch[pl.ds(pl.multiple_of(a * order + start, 8), share), :]
                outward[near_row * flips + flip][pl.ds(a * share, share), :] = picked


def middle(pieces, columns, own, near, dinv, flips):
    rows, width = own.shape
    span = columns.shape[2]
    part = jax.ShapeDtypeStruct((rows // flips, span), jnp.float32)
    return pl.pallas_call(
        functools.partial(middle_kernel, len(pieces) // 2),
        out_shape=(jax.ShapeDtypeStruct((width, span), jnp.float32),) + (part,) * (2 * flips),
        in_specs=[WHOLE] * (len(pieces) + 4),
        out_specs=(WHOLE,) * (1 + 2 * flips),
        scratch_shapes=[pltpu.VMEM((rows, span), jnp.float32)],
        cost_estimate=LIGHT,
        compiler_params=pltpu.CompilerParams(vmem_limit_bytes=32 * 1024 * 1024),
    )(*pieces, columns, own, near, dinv)


def exchange(outward, flips):
    groups_row = lax.axis_size("row")
    groups_col = lax.axis_size("col")
    arrived = []
    for index, piece in enumerate(outward):
        near_row, flip = divmod(index, flips)
        pairs = [
            (r * groups_col + c, (r ^ near_row) * groups_col + (c ^ flip))
            for r in range(groups_row)
            for c in range(groups_col)
        ]
        arrived.append(lax.ppermute(piece, ("row", "col"), pairs) if index else piece)
    return arrived


def collect_kernel(*refs):
    out = refs[-1]
    flips = len(refs) // 2
    span = refs[0].shape[1]
    for flip in range(flips):
        first = pl.multiple_of((lax.axis_index("col") ^ flip) * span, LANES)
        out[:, pl.ds(first, span)] = refs[flip][...] + refs[flips + flip][...]


def collect(arrived):
    flips = len(arrived) // 2
    share, span = arrived[0].shape
    if span % LANES:
        me = lax.axis_index("col")
        held = [arrived[flip] + arrived[flips + flip] for flip in range(flips)]
        return jnp.concatenate([lax.select_n(me ^ j, *held) for j in range(flips)], axis=1)
    return pl.pallas_call(
        collect_kernel,
        out_shape=jax.ShapeDtypeStruct((share, span * flips), jnp.float32),
        in_specs=[WHOLE] * len(arrived),
        out_specs=WHOLE,
        cost_estimate=LIGHT,
    )(*arrived)


def pair_rows(masked):
    groups_row = lax.axis_size("row")
    groups_col = lax.axis_size("col")
    cross = []
    for r in range(groups_row):
        for c in range(groups_col):
            odd = (r ^ c) & 1
            cross.append((r * groups_col + c, (r ^ odd) * groups_col + (c ^ odd)))
    held = lax.ppermute(masked, ("row", "col"), cross)
    held = [held] + [flipped(held, "col", flip) for flip in range(2, groups_col, 2)]
    return held + [flipped(piece, "col", 1) for piece in held]


def local(inverse_set, presence, factor, dinv):
    groups_row = lax.axis_size("row")
    groups_col = lax.axis_size("col")
    block_rows, _, order, width = factor.shape
    block_cols = inverse_set.shape[3]
    span = width // groups_col
    rows = block_rows * order
    share = order // groups_col

    own = factor.reshape(rows, width)
    blocks = inverse_set.reshape(rows * block_cols, order)
    masked, copies = prepare(presence.reshape(-1), blocks, own, groups_row // 2, span)
    lines = [list(range(bit, groups_row, 2)) for bit in range(2)]
    columns = lax.all_to_all(copies, "row", 0, 0, axis_index_groups=lines)
    columns = columns.reshape(groups_row // 2, block_rows, order, span).transpose(1, 0, 2, 3)
    columns = columns.reshape(-1, order, span)
    pieces = pair_rows(masked)
    near = flipped(own, "row", 1)

    terms, *outward = middle(pieces, columns, own, near, dinv, groups_col)
    terms = lax.all_to_all(terms.reshape(groups_row, width // groups_row, span), "row", 0, 0)
    diag_block = terms.sum(axis=0)

    off_diag = collect(exchange(outward, groups_col))
    return (off_diag.reshape(block_rows, 1, share, width), diag_block)


def solution(mesh):
    in_specs = (
        P(None, "row", None, None, "col", None),
        P(None, "row", None, "col"),
        P(None, "row", None, None),
        P("row", "col"),
    )
    out_specs = (P(None, "row", "col", None), P("row", "col"))
    return jax.shard_map(local, mesh=mesh, in_specs=in_specs, out_specs=out_specs, check_vma=False)
```

```python
import functools

import jax
import jax.numpy as jnp
from jax import lax
from jax.experimental import pallas as pl
from jax.experimental.pallas import tpu as pltpu
from jax.sharding import PartitionSpec as P

LANES = 128
WHOLE = pl.BlockSpec(memory_space=pltpu.VMEM)
ROOM = pltpu.CompilerParams(vmem_limit_bytes=16 * 1024 * 1024)
LIGHT = pl.CostEstimate(flops=1000, bytes_accessed=1000, transcendentals=0)


def flipped(value, axis, flip):
    return lax.ppermute(value, axis, [(i, i ^ flip) for i in range(lax.axis_size(axis))])


def two_parts(value):
    high = value.astype(jnp.bfloat16)
    return high, (value - high.astype(jnp.float32)).astype(jnp.bfloat16)


def product(left, right, contract):
    left_high, left_low = two_parts(left)
    right_high, right_low = two_parts(right)

    def once(a, b):
        return lax.dot_general(a, b, (contract, ((), ())), preferred_element_type=jnp.float32)

    return once(left_high, right_high) + (once(left_high, right_low) + once(left_low, right_high))


def prepare_kernel(presence, blocks, factor, masked, mine):
    rows, span = mine.shape
    mine[...] = factor[:, pl.ds(pl.multiple_of(lax.axis_index("col") * span, LANES), span)]
    block_cols, _, order = masked.shape
    for a in range(rows // order):
        for b in range(block_cols):
            weight = presence[a * block_cols + b].astype(jnp.float32)
            picked = blocks[pl.ds(a * order * block_cols + b, order, stride=block_cols), :]
            masked[b, pl.ds(a * order, order), :] = picked * weight


def prepare(presence, blocks, own, span):
    rows, width = own.shape
    block_cols = blocks.shape[0] // rows
    order = blocks.shape[1]
    if span % LANES:
        first = lax.axis_index("col") * span
        mine = lax.dynamic_slice_in_dim(own, first, span, 1)
        weights = presence.reshape(-1, 1, block_cols, 1).astype(jnp.float32)
        picked = blocks.reshape(-1, order, block_cols, order) * weights
        return picked.transpose(2, 0, 1, 3).reshape(block_cols, rows, order), mine
    return pl.pallas_call(
        prepare_kernel,
        out_shape=(
            jax.ShapeDtypeStruct((block_cols, rows, order), jnp.float32),
            jax.ShapeDtypeStruct((rows, span), jnp.float32),
        ),
        in_specs=[pl.BlockSpec(memory_space=pltpu.SMEM), WHOLE, WHOLE],
        out_specs=(WHOLE, WHOLE),
        cost_estimate=LIGHT,
        compiler_params=ROOM,
    )(presence, blocks, own)


def middle_kernel(count, lines, *refs):
    pieces, refs = refs[: 2 * count], refs[2 * count :]
    strips, refs = refs[:lines], refs[lines:]
    own, near, dinv, terms = refs[:4]
    outward, columns, scratch = refs[4:-2], refs[-2], refs[-1]
    block_cols, rows, order = pieces[0].shape
    col_index = lax.axis_index("col")
    row_index = lax.axis_index("row")
    for line in range(lines):
        for a in range(rows // order):
            at = a * lines + ((row_index >> 1) ^ line)
            columns[at] = strips[line][pl.ds(a * order, order), :]
    left, right = [], []
    for t in range(count):
        for b in range(block_cols):
            left.append(jnp.concatenate([pieces[t][b], pieces[count + t][b]], axis=0))
            right.append(columns[b * count + ((col_index >> 1) ^ t)])
    both = product(jnp.concatenate(left, axis=1), jnp.concatenate(right, axis=0), ((1,), (0,)))
    first, second = both[:rows], both[rows:]
    same = (row_index & 1) == (col_index & 1)
    mine = jnp.where(same, first, second)
    other = jnp.where(same, second, first)
    factors = jnp.concatenate([own[...], near[...]], axis=0)
    terms[...] = product(factors, jnp.concatenate([mine, other], axis=0), ((0,), (0,)))
    tall = dinv.shape[0]
    here = pl.ds(pl.multiple_of(row_index * tall, 8), tall)
    terms[here, :] = terms[here, :] + dinv[...]

    flips = len(outward) // 2
    share = order // flips
    for near_row, value in enumerate((mine, other)):
        scratch[...] = -value
        for flip in range(flips):
            start = (col_index ^ flip) * share
            for a in range(rows // order):
                picked = scratch[pl.ds(pl.multiple_of(a * order + start, 8), share), :]
                outward[near_row * flips + flip][pl.ds(a * share, share), :] = picked


def middle(pieces, strips, own, near, dinv, flips):
    rows, width = own.shape
    order = pieces[0].shape[2]
    span = strips[0].shape[1]
    operands = (*pieces, *strips, own, near, dinv)
    part = jax.ShapeDtypeStruct((rows // flips, span), jnp.float32)
    return pl.pallas_call(
        functools.partial(middle_kernel, len(pieces) // 2, len(strips)),
        out_shape=(jax.ShapeDtypeStruct((width, span), jnp.float32),) + (part,) * (2 * flips),
        in_specs=[WHOLE] * len(operands),
        out_specs=(WHOLE,) * (1 + 2 * flips),
        scratch_shapes=[
            pltpu.VMEM((rows // order * len(strips), order, span), jnp.float32),
            pltpu.VMEM((rows, span), jnp.float32),
        ],
        cost_estimate=LIGHT,
        compiler_params=ROOM,
    )(*operands)


def exchange(outward, flips):
    groups_row = lax.axis_size("row")
    groups_col = lax.axis_size("col")
    arrived = []
    for index, piece in enumerate(outward):
        near_row, flip = divmod(index, flips)
        pairs = [
            (r * groups_col + c, (r ^ near_row) * groups_col + (c ^ flip))
            for r in range(groups_row)
            for c in range(groups_col)
        ]
        arrived.append(lax.ppermute(piece, ("row", "col"), pairs) if index else piece)
    return arrived


def collect_kernel(*refs):
    out = refs[-1]
    flips = len(refs) // 2
    span = refs[0].shape[1]
    for flip in range(flips):
        first = pl.multiple_of((lax.axis_index("col") ^ flip) * span, LANES)
        out[:, pl.ds(first, span)] = refs[flip][...] + refs[flips + flip][...]


def collect(arrived):
    flips = len(arrived) // 2
    share, span = arrived[0].shape
    if span % LANES:
        me = lax.axis_index("col")
        held = [arrived[flip] + arrived[flips + flip] for flip in range(flips)]
        return jnp.concatenate([lax.select_n(me ^ j, *held) for j in range(flips)], axis=1)
    return pl.pallas_call(
        collect_kernel,
        out_shape=jax.ShapeDtypeStruct((share, span * flips), jnp.float32),
        in_specs=[WHOLE] * len(arrived),
        out_specs=WHOLE,
        cost_estimate=LIGHT,
        compiler_params=ROOM,
    )(*arrived)


def pair_rows(masked):
    groups_row = lax.axis_size("row")
    groups_col = lax.axis_size("col")
    cross = []
    for r in range(groups_row):
        for c in range(groups_col):
            odd = (r ^ c) & 1
            cross.append((r * groups_col + c, (r ^ odd) * groups_col + (c ^ odd)))
    held = lax.ppermute(masked, ("row", "col"), cross)
    held = [held] + [flipped(held, "col", flip) for flip in range(2, groups_col, 2)]
    return held + [flipped(piece, "col", 1) for piece in held]


def local(inverse_set, presence, factor, dinv):
    groups_row = lax.axis_size("row")
    groups_col = lax.axis_size("col")
    block_rows, _, order, width = factor.shape
    block_cols = inverse_set.shape[3]
    span = width // groups_col
    rows = block_rows * order
    share = order // groups_col

    own = factor.reshape(rows, width)
    blocks = inverse_set.reshape(rows * block_cols, order)
    masked, mine = prepare(presence.reshape(-1), blocks, own, span)
    strips = [mine] + [flipped(mine, "row", flip) for flip in range(2, groups_row, 2)]
    pieces = pair_rows(masked)
    near = flipped(own, "row", 1)

    terms, *outward = middle(pieces, strips, own, near, dinv, groups_col)
    terms = lax.all_to_all(terms.reshape(groups_row, width // groups_row, span), "row", 0, 0)
    diag_block = terms.sum(axis=0)

    off_diag = collect(exchange(outward, groups_col))
    return (off_diag.reshape(block_rows, 1, share, width), diag_block)


def solution(mesh):
    in_specs = (
        P(None, "row", None, None, "col", None),
        P(None, "row", None, "col"),
        P(None, "row", None, None),
        P("row", "col"),
    )
    out_specs = (P(None, "row", "col", None), P("row", "col"))
    return jax.shard_map(local, mesh=mesh, in_specs=in_specs, out_specs=out_specs, check_vma=False)
```

```python
import functools

import jax
import jax.numpy as jnp
from jax import lax
from jax.experimental import pallas as pl
from jax.experimental.pallas import tpu as pltpu
from jax.sharding import PartitionSpec as P

LANES = 128
WHOLE = pl.BlockSpec(memory_space=pltpu.VMEM)
ROOM = pltpu.CompilerParams(vmem_limit_bytes=16 * 1024 * 1024)
LIGHT = pl.CostEstimate(flops=1000, bytes_accessed=1000, transcendentals=0)


def flipped(value, axis, flip):
    return lax.ppermute(value, axis, [(i, i ^ flip) for i in range(lax.axis_size(axis))])


def two_parts(value):
    high = value.astype(jnp.bfloat16)
    return high, (value - high.astype(jnp.float32)).astype(jnp.bfloat16)


def product(left, right, contract):
    left_high, left_low = two_parts(left)
    right_high, right_low = two_parts(right)

    def once(a, b):
        return lax.dot_general(a, b, (contract, ((), ())), preferred_element_type=jnp.float32)

    return once(left_high, right_high) + (once(left_high, right_low) + once(left_low, right_high))


def prepare_kernel(presence, blocks, factor, masked, copies):
    count, rows, span = copies.shape
    mine = factor[:, pl.ds(pl.multiple_of(lax.axis_index("col") * span, LANES), span)]
    for i in range(count):
        copies[i] = mine
    block_cols, _, order = masked.shape
    for a in range(rows // order):
        for b in range(block_cols):
            weight = presence[a * block_cols + b].astype(jnp.float32)
            picked = blocks[pl.ds(a * order * block_cols + b, order, stride=block_cols), :]
            masked[b, pl.ds(a * order, order), :] = picked * weight


def prepare(presence, blocks, own, receivers, span):
    rows, width = own.shape
    block_cols = blocks.shape[0] // rows
    order = blocks.shape[1]
    if span % LANES:
        first = lax.axis_index("col") * span
        mine = lax.dynamic_slice_in_dim(own, first, span, 1)
        weights = presence.reshape(-1, 1, block_cols, 1).astype(jnp.float32)
        picked = blocks.reshape(-1, order, block_cols, order) * weights
        masked = picked.transpose(2, 0, 1, 3).reshape(block_cols, rows, order)
        return masked, jnp.broadcast_to(mine[None], (receivers, rows, span))
    return pl.pallas_call(
        prepare_kernel,
        out_shape=(
            jax.ShapeDtypeStruct((block_cols, rows, order), jnp.float32),
            jax.ShapeDtypeStruct((receivers, rows, span), jnp.float32),
        ),
        in_specs=[pl.BlockSpec(memory_space=pltpu.SMEM), WHOLE, WHOLE],
        out_specs=(WHOLE, WHOLE),
        cost_estimate=LIGHT,
    )(presence, blocks, own)


def partials_kernel(count, *refs):
    pieces = refs[: 2 * count]
    columns, kept, sent = refs[2 * count :]
    block_cols, rows, _ = pieces[0].shape
    col_index = lax.axis_index("col")
    left, right = [], []
    for t in range(count):
        for b in range(block_cols):
            left.append(jnp.concatenate([pieces[t][b], pieces[count + t][b]], axis=0))
            right.append(columns[b * count + ((col_index >> 1) ^ t)])
    both = product(jnp.concatenate(left, axis=1), jnp.concatenate(right, axis=0), ((1,), (0,)))
    first, second = both[:rows], both[rows:]
    same = (lax.axis_index("row") & 1) == (col_index & 1)
    kept[...] = jnp.where(same, first, second)
    sent[...] = jnp.where(same, second, first)


def partials(pieces, columns):
    part = jax.ShapeDtypeStruct((pieces[0].shape[1], columns.shape[2]), jnp.float32)
    return pl.pallas_call(
        functools.partial(partials_kernel, len(pieces) // 2),
        out_shape=(part, part),
        in_specs=[WHOLE] * (len(pieces) + 1),
        out_specs=(WHOLE, WHOLE),
        cost_estimate=LIGHT,
        compiler_params=ROOM,
    )(*pieces, columns)


def finish_kernel(order, kept, got, own, dinv, terms, *refs):
    outward, update = refs[:-1], refs[-1]
    rows = kept.shape[0]
    update[...] = kept[...] + got[...]
    terms[...] = product(own[...], update[...], ((0,), (0,)))
    tall = dinv.shape[0]
    here = pl.ds(pl.multiple_of(lax.axis_index("row") * tall, 8), tall)
    terms[here, :] = terms[here, :] + dinv[...]
    share = order // len(outward)
    for flip, piece in enumerate(outward):
        start = (lax.axis_index("col") ^ flip) * share
        for a in range(rows // order):
            picked = update[pl.ds(pl.multiple_of(a * order + start, 8), share), :]
            piece[pl.ds(a * share, share), :] = -picked


def finish(kept, got, own, dinv, order, flips):
    rows, width = own.shape
    span = kept.shape[1]
    part = jax.ShapeDtypeStruct((rows // flips, span), jnp.float32)
    return pl.pallas_call(
        functools.partial(finish_kernel, order),
        out_shape=(jax.ShapeDtypeStruct((width, span), jnp.float32),) + (part,) * flips,
        in_specs=[WHOLE] * 4,
        out_specs=(WHOLE,) * (1 + flips),
        scratch_shapes=[pltpu.VMEM((rows, span), jnp.float32)],
        cost_estimate=LIGHT,
        compiler_params=ROOM,
    )(kept, got, own, dinv)


def collect_kernel(*refs):
    out = refs[-1]
    span = refs[0].shape[1]
    for flip, piece in enumerate(refs[:-1]):
        first = pl.multiple_of((lax.axis_index("col") ^ flip) * span, LANES)
        out[:, pl.ds(first, span)] = piece[...]


def collect(arrived):
    flips = len(arrived)
    share, span = arrived[0].shape
    if span % LANES:
        me = lax.axis_index("col")
        return jnp.concatenate([lax.select_n(me ^ j, *arrived) for j in range(flips)], axis=1)
    return pl.pallas_call(
        collect_kernel,
        out_shape=jax.ShapeDtypeStruct((share, span * flips), jnp.float32),
        in_specs=[WHOLE] * flips,
        out_specs=WHOLE,
        cost_estimate=LIGHT,
        compiler_params=ROOM,
    )(*arrived)


def pair_rows(masked):
    groups_row = lax.axis_size("row")
    groups_col = lax.axis_size("col")
    cross = []
    for r in range(groups_row):
        for c in range(groups_col):
            odd = (r ^ c) & 1
            cross.append((r * groups_col + c, (r ^ odd) * groups_col + (c ^ odd)))
    held = lax.ppermute(masked, ("row", "col"), cross)
    held = [held] + [flipped(held, "col", flip) for flip in range(2, groups_col, 2)]
    return held + [flipped(piece, "col", 1) for piece in held]


def local(inverse_set, presence, factor, dinv):
    groups_row = lax.axis_size("row")
    groups_col = lax.axis_size("col")
    block_rows, _, order, width = factor.shape
    block_cols = inverse_set.shape[3]
    span = width // groups_col
    rows = block_rows * order
    share = order // groups_col

    own = factor.reshape(rows, width)
    blocks = inverse_set.reshape(rows * block_cols, order)
    masked, copies = prepare(presence.reshape(-1), blocks, own, groups_row // 2, span)
    lines = [list(range(bit, groups_row, 2)) for bit in range(2)]
    columns = lax.all_to_all(copies, "row", 0, 0, axis_index_groups=lines)
    columns = columns.reshape(groups_row // 2, block_rows, order, span).transpose(1, 0, 2, 3)
    pieces = pair_rows(masked)

    kept, sent = partials(pieces, columns.reshape(-1, order, span))
    got = flipped(sent, "row", 1)
    terms, *outward = finish(kept, got, own, dinv, order, groups_col)
    terms = lax.all_to_all(terms.reshape(groups_row, width // groups_row, span), "row", 0, 0)
    diag_block = terms.sum(axis=0)

    arrived = [outward[0]] + [flipped(outward[f], "col", f) for f in range(1, groups_col)]
    return (collect(arrived).reshape(block_rows, 1, share, width), diag_block)


def solution(mesh):
    in_specs = (
        P(None, "row", None, None, "col", None),
        P(None, "row", None, "col"),
        P(None, "row", None, None),
        P("row", "col"),
    )
    out_specs = (P(None, "row", "col", None), P("row", "col"))
    return jax.shard_map(local, mesh=mesh, in_specs=in_specs, out_specs=out_specs, check_vma=False)
```

```python
import functools

import jax
import jax.numpy as jnp
from jax import lax
from jax.experimental import pallas as pl
from jax.experimental.pallas import tpu as pltpu
from jax.sharding import PartitionSpec as P

LANES = 128
WHOLE = pl.BlockSpec(memory_space=pltpu.VMEM)
ROOM = pltpu.CompilerParams(vmem_limit_bytes=16 * 1024 * 1024)
LIGHT = pl.CostEstimate(flops=1000, bytes_accessed=1000, transcendentals=0)


def flipped(value, axis, flip):
    return lax.ppermute(value, axis, [(i, i ^ flip) for i in range(lax.axis_size(axis))])


def two_parts(value):
    high = value.astype(jnp.bfloat16)
    return high, (value - high.astype(jnp.float32)).astype(jnp.bfloat16)


def product(left, right, contract):
    left_high, left_low = two_parts(left)
    right_high, right_low = two_parts(right)

    def once(a, b):
        return lax.dot_general(a, b, (contract, ((), ())), preferred_element_type=jnp.float32)

    return once(left_high, right_high) + (once(left_high, right_low) + once(left_low, right_high))


def prepare_kernel(presence, blocks, factor, masked, mine):
    rows, span = mine.shape
    mine[...] = factor[:, pl.ds(pl.multiple_of(lax.axis_index("col") * span, LANES), span)]
    block_cols, _, order = masked.shape
    for a in range(rows // order):
        for b in range(block_cols):
            weight = presence[a * block_cols + b].astype(jnp.float32)
            picked = blocks[pl.ds(a * order * block_cols + b, order, stride=block_cols), :]
            masked[b, pl.ds(a * order, order), :] = picked * weight


def prepare(presence, blocks, own, span):
    rows, width = own.shape
    block_cols = blocks.shape[0] // rows
    order = blocks.shape[1]
    if span % LANES:
        first = lax.axis_index("col") * span
        mine = lax.dynamic_slice_in_dim(own, first, span, 1)
        weights = presence.reshape(-1, 1, block_cols, 1).astype(jnp.float32)
        picked = blocks.reshape(-1, order, block_cols, order) * weights
        return picked.transpose(2, 0, 1, 3).reshape(block_cols, rows, order), mine
    return pl.pallas_call(
        prepare_kernel,
        out_shape=(
            jax.ShapeDtypeStruct((block_cols, rows, order), jnp.float32),
            jax.ShapeDtypeStruct((rows, span), jnp.float32),
        ),
        in_specs=[pl.BlockSpec(memory_space=pltpu.SMEM), WHOLE, WHOLE],
        out_specs=(WHOLE, WHOLE),
        cost_estimate=LIGHT,
    )(presence, blocks, own)


def partials_kernel(count, flips, *refs):
    pieces, refs = refs[: 2 * count], refs[2 * count :]
    strips = refs[: len(flips)]
    kept, sent, columns = refs[len(flips) :]
    block_cols, rows, order = pieces[0].shape
    col_index = lax.axis_index("col")
    row_index = lax.axis_index("row")
    for flip, strip in zip(flips, strips):
        for a in range(rows // order):
            at = a * len(flips) + ((row_index ^ flip) >> 1)
            columns[at] = strip[pl.ds(a * order, order), :]
    left, right = [], []
    for t in range(count):
        for b in range(block_cols):
            left.append(jnp.concatenate([pieces[t][b], pieces[count + t][b]], axis=0))
            right.append(columns[b * count + ((col_index >> 1) ^ t)])
    both = product(jnp.concatenate(left, axis=1), jnp.concatenate(right, axis=0), ((1,), (0,)))
    first, second = both[:rows], both[rows:]
    same = (row_index & 1) == (col_index & 1)
    kept[...] = jnp.where(same, first, second)
    sent[...] = jnp.where(same, second, first)


def partials(pieces, strips, flips):
    _, rows, order = pieces[0].shape
    span = strips[0].shape[1]
    part = jax.ShapeDtypeStruct((rows, span), jnp.float32)
    return pl.pallas_call(
        functools.partial(partials_kernel, len(pieces) // 2, flips),
        out_shape=(part, part),
        in_specs=[WHOLE] * (len(pieces) + len(strips)),
        out_specs=(WHOLE, WHOLE),
        scratch_shapes=[pltpu.VMEM((rows // order * len(strips), order, span), jnp.float32)],
        cost_estimate=LIGHT,
        compiler_params=ROOM,
    )(*pieces, *strips)


def finish_kernel(order, kept, got, own, dinv, terms, *refs):
    outward, update = refs[:-1], refs[-1]
    rows = kept.shape[0]
    update[...] = kept[...] + got[...]
    terms[...] = product(own[...], update[...], ((0,), (0,)))
    tall = dinv.shape[0]
    here = pl.ds(pl.multiple_of(lax.axis_index("row") * tall, 8), tall)
    terms[here, :] = terms[here, :] + dinv[...]
    share = order // len(outward)
    for flip, piece in enumerate(outward):
        start = (lax.axis_index("col") ^ flip) * share
        for a in range(rows // order):
            picked = update[pl.ds(pl.multiple_of(a * order + start, 8), share), :]
            piece[pl.ds(a * share, share), :] = -picked


def finish(kept, got, own, dinv, order, flips):
    rows, width = own.shape
    span = kept.shape[1]
    part = jax.ShapeDtypeStruct((rows // flips, span), jnp.float32)
    return pl.pallas_call(
        functools.partial(finish_kernel, order),
        out_shape=(jax.ShapeDtypeStruct((width, span), jnp.float32),) + (part,) * flips,
        in_specs=[WHOLE] * 4,
        out_specs=(WHOLE,) * (1 + flips),
        scratch_shapes=[pltpu.VMEM((rows, span), jnp.float32)],
        cost_estimate=LIGHT,
        compiler_params=ROOM,
    )(kept, got, own, dinv)


def collect_kernel(*refs):
    out = refs[-1]
    span = refs[0].shape[1]
    for flip, piece in enumerate(refs[:-1]):
        first = pl.multiple_of((lax.axis_index("col") ^ flip) * span, LANES)
        out[:, pl.ds(first, span)] = piece[...]


def collect(arrived):
    flips = len(arrived)
    share, span = arrived[0].shape
    if span % LANES:
        me = lax.axis_index("col")
        return jnp.concatenate([lax.select_n(me ^ j, *arrived) for j in range(flips)], axis=1)
    return pl.pallas_call(
        collect_kernel,
        out_shape=jax.ShapeDtypeStruct((share, span * flips), jnp.float32),
        in_specs=[WHOLE] * flips,
        out_specs=WHOLE,
        cost_estimate=LIGHT,
        compiler_params=ROOM,
    )(*arrived)


def along_line(mine):
    strips, flips = [mine], [0]
    bit = lax.axis_size("row") // 2
    while bit > 1:
        strips = strips + [flipped(strip, "row", bit) for strip in strips]
        flips = flips + [flip ^ bit for flip in flips]
        bit //= 2
    return strips, tuple(flips)


def pair_rows(masked):
    groups_row = lax.axis_size("row")
    groups_col = lax.axis_size("col")
    cross = []
    for r in range(groups_row):
        for c in range(groups_col):
            odd = (r ^ c) & 1
            cross.append((r * groups_col + c, (r ^ odd) * groups_col + (c ^ odd)))
    held = lax.ppermute(masked, ("row", "col"), cross)
    held = [held] + [flipped(held, "col", flip) for flip in range(2, groups_col, 2)]
    return held + [flipped(piece, "col", 1) for piece in held]


def local(inverse_set, presence, factor, dinv):
    groups_row = lax.axis_size("row")
    groups_col = lax.axis_size("col")
    block_rows, _, order, width = factor.shape
    block_cols = inverse_set.shape[3]
    span = width // groups_col
    rows = block_rows * order
    share = order // groups_col

    own = factor.reshape(rows, width)
    blocks = inverse_set.reshape(rows * block_cols, order)
    masked, mine = prepare(presence.reshape(-1), blocks, own, span)
    strips, flips = along_line(mine)
    kept, sent = partials(pair_rows(masked), strips, flips)
    got = flipped(sent, "row", 1)
    terms, *outward = finish(kept, got, own, dinv, order, groups_col)
    terms = lax.all_to_all(terms.reshape(groups_row, width // groups_row, span), "row", 0, 0)
    diag_block = terms.sum(axis=0)

    arrived = [outward[0]] + [flipped(outward[f], "col", f) for f in range(1, groups_col)]
    return (collect(arrived).reshape(block_rows, 1, share, width), diag_block)


def solution(mesh):
    in_specs = (
        P(None, "row", None, None, "col", None),
        P(None, "row", None, "col"),
        P(None, "row", None, None),
        P("row", "col"),
    )
    out_specs = (P(None, "row", "col", None), P("row", "col"))
    return jax.shard_map(local, mesh=mesh, in_specs=in_specs, out_specs=out_specs, check_vma=False)
```

```python
import functools

import jax
import jax.numpy as jnp
from jax import lax
from jax.experimental import pallas as pl
from jax.experimental.pallas import tpu as pltpu
from jax.sharding import PartitionSpec as P

LANES = 128
WHOLE = pl.BlockSpec(memory_space=pltpu.VMEM)
ROOM = pltpu.CompilerParams(vmem_limit_bytes=16 * 1024 * 1024)
LIGHT = pl.CostEstimate(flops=1000, bytes_accessed=1000, transcendentals=0)


def flipped(value, axis, flip):
    return lax.ppermute(value, axis, [(i, i ^ flip) for i in range(lax.axis_size(axis))])


def two_parts(value):
    high = value.astype(jnp.bfloat16)
    return high, (value - high.astype(jnp.float32)).astype(jnp.bfloat16)


def product(left, right, contract):
    left_high, left_low = two_parts(left)
    right_high, right_low = two_parts(right)

    def once(a, b):
        return lax.dot_general(a, b, (contract, ((), ())), preferred_element_type=jnp.float32)

    return once(left_high, right_high) + (once(left_high, right_low) + once(left_low, right_high))


def prepare_kernel(presence, blocks, factor, masked, copies):
    count, rows, span = copies.shape
    mine = factor[:, pl.ds(pl.multiple_of(lax.axis_index("col") * span, LANES), span)]
    for i in range(count):
        copies[i] = mine
    block_cols, _, order = masked.shape
    for a in range(rows // order):
        for b in range(block_cols):
            weight = presence[a * block_cols + b].astype(jnp.float32)
            picked = blocks[pl.ds(a * order * block_cols + b, order, stride=block_cols), :]
            masked[b, pl.ds(a * order, order), :] = picked * weight


def prepare(presence, blocks, own, receivers, span):
    rows, width = own.shape
    block_cols = blocks.shape[0] // rows
    order = blocks.shape[1]
    if span % LANES:
        first = lax.axis_index("col") * span
        mine = lax.dynamic_slice_in_dim(own, first, span, 1)
        weights = presence.reshape(-1, 1, block_cols, 1).astype(jnp.float32)
        picked = blocks.reshape(-1, order, block_cols, order) * weights
        masked = picked.transpose(2, 0, 1, 3).reshape(block_cols, rows, order)
        return masked, jnp.broadcast_to(mine[None], (receivers, rows, span))
    return pl.pallas_call(
        prepare_kernel,
        out_shape=(
            jax.ShapeDtypeStruct((block_cols, rows, order), jnp.float32),
            jax.ShapeDtypeStruct((receivers, rows, span), jnp.float32),
        ),
        in_specs=[pl.BlockSpec(memory_space=pltpu.SMEM), WHOLE, WHOLE],
        out_specs=(WHOLE, WHOLE),
        cost_estimate=LIGHT,
    )(presence, blocks, own)


def partials_kernel(count, *refs):
    pieces = refs[: 2 * count]
    columns, both = refs[2 * count :]
    block_cols, rows, _ = pieces[0].shape
    col_index = lax.axis_index("col")
    left, right = [], []
    for t in range(count):
        for b in range(block_cols):
            left.append(jnp.concatenate([pieces[t][b], pieces[count + t][b]], axis=0))
            right.append(columns[b * count + ((col_index >> 1) ^ t)])
    summed = product(jnp.concatenate(left, axis=1), jnp.concatenate(right, axis=0), ((1,), (0,)))
    here = (col_index & 1) * rows
    both[pl.ds(pl.multiple_of(here, 8), rows), :] = summed[:rows]
    both[pl.ds(pl.multiple_of(rows - here, 8), rows), :] = summed[rows:]


def partials(pieces, columns):
    shape = (2 * pieces[0].shape[1], columns.shape[2])
    return pl.pallas_call(
        functools.partial(partials_kernel, len(pieces) // 2),
        out_shape=jax.ShapeDtypeStruct(shape, jnp.float32),
        in_specs=[WHOLE] * (len(pieces) + 1),
        out_specs=WHOLE,
        cost_estimate=LIGHT,
        compiler_params=ROOM,
    )(*pieces, columns)


def halves_kernel(tall, own, held, stay, go):
    even, odd = [
        jnp.concatenate([own[:, i : i + tall] for i in range(first, own.shape[1], 2 * tall)], axis=1)
        for first in (0, tall)
    ]
    upper = (lax.axis_index("row") & 1) == 1
    stay[...] = jnp.where(upper, odd, even)
    go[...] = jnp.where(upper, even, odd)


def halves(own, held, tall):
    rows, width = own.shape
    part = jax.ShapeDtypeStruct((rows, width // 2), jnp.float32)
    return pl.pallas_call(
        functools.partial(halves_kernel, tall),
        out_shape=(part, part),
        in_specs=[WHOLE, pl.BlockSpec(memory_space=pl.ANY)],
        out_specs=(WHOLE, WHOLE),
        cost_estimate=LIGHT,
        compiler_params=ROOM,
    )(own, held)


def finish_kernel(order, flips, both, got, stay, near, dinv, *refs):
    update, terms = refs[-2:]
    along, outward = refs[: len(flips)], refs[len(flips) : -2]
    rows = stay.shape[0]
    row_index = lax.axis_index("row")
    here = (row_index & 1) * rows
    update[...] = both[...] + got[...]
    mine = update[pl.ds(pl.multiple_of(here, 8), rows), :]
    other = update[pl.ds(pl.multiple_of(rows - here, 8), rows), :]
    factors = jnp.concatenate([stay[...], near[...]], axis=0)
    terms[...] = product(factors, jnp.concatenate([mine, other], axis=0), ((0,), (0,)))
    tall = dinv.shape[0]
    for flip, piece in zip(flips, along):
        slot = ((row_index ^ flip) >> 1) * tall
        piece[...] = terms[pl.ds(pl.multiple_of(slot, 8), tall), :]
    along[0][...] = along[0][...] + dinv[...]
    share = order // len(outward)
    for flip, piece in enumerate(outward):
        start = here + (lax.axis_index("col") ^ flip) * share
        for a in range(rows // order):
            picked = update[pl.ds(pl.multiple_of(a * order + start, 8), share), :]
            piece[pl.ds(a * share, share), :] = -picked


def finish(both, got, stay, near, dinv, order, flips, receivers):
    rows, half = stay.shape
    span = both.shape[1]
    along = (jax.ShapeDtypeStruct(dinv.shape, jnp.float32),) * len(flips)
    outward = (jax.ShapeDtypeStruct((rows // receivers, span), jnp.float32),) * receivers
    outs = pl.pallas_call(
        functools.partial(finish_kernel, order, flips),
        out_shape=along + outward,
        in_specs=[WHOLE] * 5,
        out_specs=(WHOLE,) * (len(flips) + receivers),
        scratch_shapes=[
            pltpu.VMEM((2 * rows, span), jnp.float32),
            pltpu.VMEM((half, span), jnp.float32),
        ],
        cost_estimate=LIGHT,
        compiler_params=ROOM,
    )(both, got, stay, near, dinv)
    return outs[: len(flips)], outs[len(flips) :]


def collect_kernel(*refs):
    out = refs[-1]
    span = refs[0].shape[1]
    for flip, piece in enumerate(refs[:-1]):
        first = pl.multiple_of((lax.axis_index("col") ^ flip) * span, LANES)
        out[:, pl.ds(first, span)] = piece[...]


def collect(arrived):
    flips = len(arrived)
    share, span = arrived[0].shape
    if span % LANES:
        me = lax.axis_index("col")
        return jnp.concatenate([lax.select_n(me ^ j, *arrived) for j in range(flips)], axis=1)
    return pl.pallas_call(
        collect_kernel,
        out_shape=jax.ShapeDtypeStruct((share, span * flips), jnp.float32),
        in_specs=[WHOLE] * flips,
        out_specs=WHOLE,
        cost_estimate=LIGHT,
        compiler_params=ROOM,
    )(*arrived)


def pair_rows(masked):
    groups_row = lax.axis_size("row")
    groups_col = lax.axis_size("col")
    cross = []
    for r in range(groups_row):
        for c in range(groups_col):
            odd = (r ^ c) & 1
            cross.append((r * groups_col + c, (r ^ odd) * groups_col + (c ^ odd)))
    held = lax.ppermute(masked, ("row", "col"), cross)
    held = [held] + [flipped(held, "col", flip) for flip in range(2, groups_col, 2)]
    return held + [flipped(piece, "col", 1) for piece in held]


def local(inverse_set, presence, factor, dinv):
    groups_row = lax.axis_size("row")
    groups_col = lax.axis_size("col")
    block_rows, _, order, width = factor.shape
    block_cols = inverse_set.shape[3]
    span = width // groups_col
    rows = block_rows * order
    share = order // groups_col

    own = factor.reshape(rows, width)
    blocks = inverse_set.reshape(rows * block_cols, order)
    masked, copies = prepare(presence.reshape(-1), blocks, own, groups_row // 2, span)
    lines = [list(range(bit, groups_row, 2)) for bit in range(2)]
    columns = lax.all_to_all(copies, "row", 0, 0, axis_index_groups=lines)
    columns = columns.reshape(groups_row // 2, block_rows, order, span).transpose(1, 0, 2, 3)
    pieces = pair_rows(masked)
    stay, go = halves(own, pieces[0], width // groups_row)
    near = flipped(go, "row", 1)

    both = partials(pieces, columns.reshape(-1, order, span))
    got = flipped(both, "row", 1)
    flips = tuple(range(0, groups_row, 2))
    along, outward = finish(both, got, stay, near, dinv, order, flips, groups_col)
    diag_block = along[0]
    for flip, piece in zip(flips[1:], along[1:]):
        diag_block = diag_block + flipped(piece, "row", flip)

    arrived = [outward[0]] + [flipped(outward[f], "col", f) for f in range(1, groups_col)]
    return (collect(arrived).reshape(block_rows, 1, share, width), diag_block)


def solution(mesh):
    in_specs = (
        P(None, "row", None, None, "col", None),
        P(None, "row", None, "col"),
        P(None, "row", None, None),
        P("row", "col"),
    )
    out_specs = (P(None, "row", "col", None), P("row", "col"))
    return jax.shard_map(local, mesh=mesh, in_specs=in_specs, out_specs=out_specs, check_vma=False)
```

```python
import functools

import jax
import jax.numpy as jnp
from jax import lax
from jax.experimental import pallas as pl
from jax.experimental.pallas import tpu as pltpu
from jax.sharding import PartitionSpec as P

LANES = 128
WHOLE = pl.BlockSpec(memory_space=pltpu.VMEM)
ROOM = pltpu.CompilerParams(vmem_limit_bytes=16 * 1024 * 1024)
LIGHT = pl.CostEstimate(flops=1000, bytes_accessed=1000, transcendentals=0)


def flipped(value, axis, flip):
    return lax.ppermute(value, axis, [(i, i ^ flip) for i in range(lax.axis_size(axis))])


def two_parts(value):
    high = value.astype(jnp.bfloat16)
    return high, (value - high.astype(jnp.float32)).astype(jnp.bfloat16)


def product(left, right, contract):
    left_high, left_low = two_parts(left)
    right_high, right_low = two_parts(right)

    def once(a, b):
        return lax.dot_general(a, b, (contract, ((), ())), preferred_element_type=jnp.float32)

    return once(left_high, right_high) + (once(left_high, right_low) + once(left_low, right_high))


def prepare_kernel(presence, blocks, factor, masked, copies):
    count, rows, span = copies.shape
    mine = factor[:, pl.ds(pl.multiple_of(lax.axis_index("col") * span, LANES), span)]
    for i in range(count):
        copies[i] = mine
    block_cols, _, order = masked.shape
    for a in range(rows // order):
        for b in range(block_cols):
            weight = presence[a * block_cols + b].astype(jnp.float32)
            picked = blocks[pl.ds(a * order * block_cols + b, order, stride=block_cols), :]
            masked[b, pl.ds(a * order, order), :] = picked * weight


def prepare(presence, blocks, own, receivers, span):
    rows, width = own.shape
    block_cols = blocks.shape[0] // rows
    order = blocks.shape[1]
    if span % LANES:
        first = lax.axis_index("col") * span
        mine = lax.dynamic_slice_in_dim(own, first, span, 1)
        weights = presence.reshape(-1, 1, block_cols, 1).astype(jnp.float32)
        picked = blocks.reshape(-1, order, block_cols, order) * weights
        masked = picked.transpose(2, 0, 1, 3).reshape(block_cols, rows, order)
        return masked, jnp.broadcast_to(mine[None], (receivers, rows, span))
    return pl.pallas_call(
        prepare_kernel,
        out_shape=(
            jax.ShapeDtypeStruct((block_cols, rows, order), jnp.float32),
            jax.ShapeDtypeStruct((receivers, rows, span), jnp.float32),
        ),
        in_specs=[pl.BlockSpec(memory_space=pltpu.SMEM), WHOLE, WHOLE],
        out_specs=(WHOLE, WHOLE),
        cost_estimate=LIGHT,
    )(presence, blocks, own)


def partials_kernel(count, *refs):
    pieces = refs[: 2 * count]
    columns, _, both = refs[2 * count :]
    block_cols, rows, _ = pieces[0].shape
    col_index = lax.axis_index("col")
    left, right = [], []
    for t in range(count):
        for b in range(block_cols):
            left.append(jnp.concatenate([pieces[t][b], pieces[count + t][b]], axis=0))
            right.append(columns[b * count + ((col_index >> 1) ^ t)])
    summed = product(jnp.concatenate(left, axis=1), jnp.concatenate(right, axis=0), ((1,), (0,)))
    here = (col_index & 1) * rows
    both[pl.ds(pl.multiple_of(here, 8), rows), :] = summed[:rows]
    both[pl.ds(pl.multiple_of(rows - here, 8), rows), :] = summed[rows:]


def partials(pieces, columns, near):
    shape = (2 * pieces[0].shape[1], columns.shape[2])
    return pl.pallas_call(
        functools.partial(partials_kernel, len(pieces) // 2),
        out_shape=jax.ShapeDtypeStruct(shape, jnp.float32),
        in_specs=[WHOLE] * (len(pieces) + 1) + [pl.BlockSpec(memory_space=pl.ANY)],
        out_specs=WHOLE,
        cost_estimate=LIGHT,
        compiler_params=ROOM,
    )(*pieces, columns, near)


def halves_kernel(tall, own, held, stay, go):
    even, odd = [
        jnp.concatenate([own[:, i : i + tall] for i in range(first, own.shape[1], 2 * tall)], axis=1)
        for first in (0, tall)
    ]
    upper = (lax.axis_index("row") & 1) == 1
    stay[...] = jnp.where(upper, odd, even)
    go[...] = jnp.where(upper, even, odd)


def halves(own, held, tall):
    rows, width = own.shape
    part = jax.ShapeDtypeStruct((rows, width // 2), jnp.float32)
    return pl.pallas_call(
        functools.partial(halves_kernel, tall),
        out_shape=(part, part),
        in_specs=[WHOLE, pl.BlockSpec(memory_space=pl.ANY)],
        out_specs=(WHOLE, WHOLE),
        cost_estimate=LIGHT,
        compiler_params=ROOM,
    )(own, held)


def finish_kernel(order, flips, both, got, stay, near, dinv, *refs):
    update, terms = refs[-2:]
    along, outward = refs[: len(flips)], refs[len(flips) : -2]
    rows = stay.shape[0]
    row_index = lax.axis_index("row")
    here = (row_index & 1) * rows
    update[...] = both[...] + got[...]
    mine = update[pl.ds(pl.multiple_of(here, 8), rows), :]
    other = update[pl.ds(pl.multiple_of(rows - here, 8), rows), :]
    factors = jnp.concatenate([stay[...], near[...]], axis=0)
    terms[...] = product(factors, jnp.concatenate([mine, other], axis=0), ((0,), (0,)))
    tall = dinv.shape[0]
    for flip, piece in zip(flips, along):
        slot = ((row_index ^ flip) >> 1) * tall
        piece[...] = terms[pl.ds(pl.multiple_of(slot, 8), tall), :]
    along[0][...] = along[0][...] + dinv[...]
    share = order // len(outward)
    for flip, piece in enumerate(outward):
        start = here + (lax.axis_index("col") ^ flip) * share
        for a in range(rows // order):
            picked = update[pl.ds(pl.multiple_of(a * order + start, 8), share), :]
            piece[pl.ds(a * share, share), :] = -picked


def finish(both, got, stay, near, dinv, order, flips, receivers):
    rows, half = stay.shape
    span = both.shape[1]
    along = (jax.ShapeDtypeStruct(dinv.shape, jnp.float32),) * len(flips)
    outward = (jax.ShapeDtypeStruct((rows // receivers, span), jnp.float32),) * receivers
    outs = pl.pallas_call(
        functools.partial(finish_kernel, order, flips),
        out_shape=along + outward,
        in_specs=[WHOLE] * 5,
        out_specs=(WHOLE,) * (len(flips) + receivers),
        scratch_shapes=[
            pltpu.VMEM((2 * rows, span), jnp.float32),
            pltpu.VMEM((half, span), jnp.float32),
        ],
        cost_estimate=LIGHT,
        compiler_params=ROOM,
    )(both, got, stay, near, dinv)
    return outs[: len(flips)], outs[len(flips) :]


def collect_kernel(*refs):
    out = refs[-1]
    span = refs[0].shape[1]
    for flip, piece in enumerate(refs[:-1]):
        first = pl.multiple_of((lax.axis_index("col") ^ flip) * span, LANES)
        out[:, pl.ds(first, span)] = piece[...]


def collect(arrived):
    flips = len(arrived)
    share, span = arrived[0].shape
    if span % LANES:
        me = lax.axis_index("col")
        return jnp.concatenate([lax.select_n(me ^ j, *arrived) for j in range(flips)], axis=1)
    return pl.pallas_call(
        collect_kernel,
        out_shape=jax.ShapeDtypeStruct((share, span * flips), jnp.float32),
        in_specs=[WHOLE] * flips,
        out_specs=WHOLE,
        cost_estimate=LIGHT,
        compiler_params=ROOM,
    )(*arrived)


def pair_rows(masked):
    groups_row = lax.axis_size("row")
    groups_col = lax.axis_size("col")
    cross = []
    for r in range(groups_row):
        for c in range(groups_col):
            odd = (r ^ c) & 1
            cross.append((r * groups_col + c, (r ^ odd) * groups_col + (c ^ odd)))
    held = lax.ppermute(masked, ("row", "col"), cross)
    held = [held] + [flipped(held, "col", flip) for flip in range(2, groups_col, 2)]
    return held + [flipped(piece, "col", 1) for piece in held]


def local(inverse_set, presence, factor, dinv):
    groups_row = lax.axis_size("row")
    groups_col = lax.axis_size("col")
    block_rows, _, order, width = factor.shape
    block_cols = inverse_set.shape[3]
    span = width // groups_col
    rows = block_rows * order
    share = order // groups_col

    own = factor.reshape(rows, width)
    blocks = inverse_set.reshape(rows * block_cols, order)
    masked, copies = prepare(presence.reshape(-1), blocks, own, groups_row // 2, span)
    lines = [list(range(bit, groups_row, 2)) for bit in range(2)]
    columns = lax.all_to_all(copies, "row", 0, 0, axis_index_groups=lines)
    columns = columns.reshape(groups_row // 2, block_rows, order, span).transpose(1, 0, 2, 3)
    pieces = pair_rows(masked)
    stay, go = halves(own, pieces[0], width // groups_row)
    near = flipped(go, "row", 1)

    both = partials(pieces, columns.reshape(-1, order, span), near)
    got = flipped(both, "row", 1)
    flips = tuple(range(0, groups_row, 2))
    along, outward = finish(both, got, stay, near, dinv, order, flips, groups_col)
    diag_block = along[0]
    for flip, piece in zip(flips[1:], along[1:]):
        diag_block = diag_block + flipped(piece, "row", flip)

    arrived = [outward[0]] + [flipped(outward[f], "col", f) for f in range(1, groups_col)]
    return (collect(arrived).reshape(block_rows, 1, share, width), diag_block)


def solution(mesh):
    in_specs = (
        P(None, "row", None, None, "col", None),
        P(None, "row", None, "col"),
        P(None, "row", None, None),
        P("row", "col"),
    )
    out_specs = (P(None, "row", "col", None), P("row", "col"))
    return jax.shard_map(local, mesh=mesh, in_specs=in_specs, out_specs=out_specs, check_vma=False)
```

```python
import functools

import jax
import jax.numpy as jnp
from jax import lax
from jax.experimental import pallas as pl
from jax.experimental.pallas import tpu as pltpu
from jax.sharding import PartitionSpec as P

LANES = 128
WHOLE = pl.BlockSpec(memory_space=pltpu.VMEM)
ROOM = pltpu.CompilerParams(vmem_limit_bytes=16 * 1024 * 1024)
HEAVY = 10**11
LIGHT = pl.CostEstimate(flops=1000, bytes_accessed=1000, transcendentals=0)


def flipped(value, axis, flip):
    return lax.ppermute(value, axis, [(i, i ^ flip) for i in range(lax.axis_size(axis))])


def two_parts(value):
    high = value.astype(jnp.bfloat16)
    return high, (value - high.astype(jnp.float32)).astype(jnp.bfloat16)


def product(left, right, contract):
    left_high, left_low = two_parts(left)
    right_high, right_low = two_parts(right)

    def once(a, b):
        return lax.dot_general(a, b, (contract, ((), ())), preferred_element_type=jnp.float32)

    return once(left_high, right_high) + (once(left_high, right_low) + once(left_low, right_high))


def prepare_kernel(presence, blocks, factor, masked, mine):
    rows, span = mine.shape
    mine[...] = factor[:, pl.ds(pl.multiple_of(lax.axis_index("col") * span, LANES), span)]
    block_cols, _, order = masked.shape
    for a in range(rows // order):
        for b in range(block_cols):
            weight = presence[a * block_cols + b].astype(jnp.float32)
            picked = blocks[pl.ds(a * order * block_cols + b, order, stride=block_cols), :]
            masked[b, pl.ds(a * order, order), :] = picked * weight


def prepare(presence, blocks, own, span):
    rows, width = own.shape
    block_cols = blocks.shape[0] // rows
    order = blocks.shape[1]
    if span % LANES:
        first = lax.axis_index("col") * span
        mine = lax.dynamic_slice_in_dim(own, first, span, 1)
        weights = presence.reshape(-1, 1, block_cols, 1).astype(jnp.float32)
        picked = blocks.reshape(-1, order, block_cols, order) * weights
        return picked.transpose(2, 0, 1, 3).reshape(block_cols, rows, order), mine
    return pl.pallas_call(
        prepare_kernel,
        out_shape=(
            jax.ShapeDtypeStruct((block_cols, rows, order), jnp.float32),
            jax.ShapeDtypeStruct((rows, span), jnp.float32),
        ),
        in_specs=[pl.BlockSpec(memory_space=pltpu.SMEM), WHOLE, WHOLE],
        out_specs=(WHOLE, WHOLE),
        cost_estimate=LIGHT,
    )(presence, blocks, own)


def joined_kernel(bit, first, second, out):
    here = jnp.where((lax.axis_index("row") & bit) == 0, 0, 1)
    out[:, here] = first[...]
    out[:, 1 - here] = second[...]


def joined(first, second, bit):
    count, rows, span = first.shape
    both = pl.pallas_call(
        functools.partial(joined_kernel, bit),
        out_shape=jax.ShapeDtypeStruct((count, 2, rows, span), jnp.float32),
        in_specs=[WHOLE, WHOLE],
        out_specs=WHOLE,
        cost_estimate=pl.CostEstimate(flops=HEAVY, bytes_accessed=1000, transcendentals=0),
        compiler_params=ROOM,
    )(first, second)
    return both.reshape(2 * count, rows, span)


def partials_kernel(count, *refs):
    pieces = refs[: 2 * count]
    columns, _, both = refs[2 * count :]
    block_cols, rows, _ = pieces[0].shape
    col_index = lax.axis_index("col")
    left, right = [], []
    for t in range(count):
        for b in range(block_cols):
            left.append(jnp.concatenate([pieces[t][b], pieces[count + t][b]], axis=0))
            right.append(columns[b * count + ((col_index >> 1) ^ t)])
    summed = product(jnp.concatenate(left, axis=1), jnp.concatenate(right, axis=0), ((1,), (0,)))
    here = (col_index & 1) * rows
    both[pl.ds(pl.multiple_of(here, 8), rows), :] = summed[:rows]
    both[pl.ds(pl.multiple_of(rows - here, 8), rows), :] = summed[rows:]


def partials(pieces, columns, near):
    shape = (2 * pieces[0].shape[1], columns.shape[2])
    return pl.pallas_call(
        functools.partial(partials_kernel, len(pieces) // 2),
        out_shape=jax.ShapeDtypeStruct(shape, jnp.float32),
        in_specs=[WHOLE] * (len(pieces) + 1) + [pl.BlockSpec(memory_space=pl.ANY)],
        out_specs=WHOLE,
        cost_estimate=LIGHT,
        compiler_params=ROOM,
    )(*pieces, columns, near)


def halves_kernel(tall, own, held, stay, go):
    even, odd = [
        jnp.concatenate([own[:, i : i + tall] for i in range(first, own.shape[1], 2 * tall)], axis=1)
        for first in (0, tall)
    ]
    upper = (lax.axis_index("row") & 1) == 1
    stay[...] = jnp.where(upper, odd, even)
    go[...] = jnp.where(upper, even, odd)


def halves(own, held, tall):
    rows, width = own.shape
    part = jax.ShapeDtypeStruct((rows, width // 2), jnp.float32)
    return pl.pallas_call(
        functools.partial(halves_kernel, tall),
        out_shape=(part, part),
        in_specs=[WHOLE, pl.BlockSpec(memory_space=pl.ANY)],
        out_specs=(WHOLE, WHOLE),
        cost_estimate=LIGHT,
        compiler_params=ROOM,
    )(own, held)


def finish_kernel(order, flips, both, got, stay, near, dinv, *refs):
    update, terms = refs[-2:]
    along, outward = refs[: len(flips)], refs[len(flips) : -2]
    rows = stay.shape[0]
    row_index = lax.axis_index("row")
    here = (row_index & 1) * rows
    update[...] = both[...] + got[...]
    mine = update[pl.ds(pl.multiple_of(here, 8), rows), :]
    other = update[pl.ds(pl.multiple_of(rows - here, 8), rows), :]
    factors = jnp.concatenate([stay[...], near[...]], axis=0)
    terms[...] = product(factors, jnp.concatenate([mine, other], axis=0), ((0,), (0,)))
    tall = dinv.shape[0]
    for flip, piece in zip(flips, along):
        slot = ((row_index ^ flip) >> 1) * tall
        piece[...] = terms[pl.ds(pl.multiple_of(slot, 8), tall), :]
    along[0][...] = along[0][...] + dinv[...]
    share = order // len(outward)
    for flip, piece in enumerate(outward):
        start = here + (lax.axis_index("col") ^ flip) * share
        for a in range(rows // order):
            picked = update[pl.ds(pl.multiple_of(a * order + start, 8), share), :]
            piece[pl.ds(a * share, share), :] = -picked


def finish(both, got, stay, near, dinv, order, flips, receivers):
    rows, half = stay.shape
    span = both.shape[1]
    along = (jax.ShapeDtypeStruct(dinv.shape, jnp.float32),) * len(flips)
    outward = (jax.ShapeDtypeStruct((rows // receivers, span), jnp.float32),) * receivers
    outs = pl.pallas_call(
        functools.partial(finish_kernel, order, flips),
        out_shape=along + outward,
        in_specs=[WHOLE] * 5,
        out_specs=(WHOLE,) * (len(flips) + receivers),
        scratch_shapes=[
            pltpu.VMEM((2 * rows, span), jnp.float32),
            pltpu.VMEM((half, span), jnp.float32),
        ],
        cost_estimate=LIGHT,
        compiler_params=ROOM,
    )(both, got, stay, near, dinv)
    return outs[: len(flips)], outs[len(flips) :]


def collect_kernel(*refs):
    out = refs[-1]
    span = refs[0].shape[1]
    for flip, piece in enumerate(refs[:-1]):
        first = pl.multiple_of((lax.axis_index("col") ^ flip) * span, LANES)
        out[:, pl.ds(first, span)] = piece[...]


def collect(arrived):
    flips = len(arrived)
    share, span = arrived[0].shape
    if span % LANES:
        me = lax.axis_index("col")
        return jnp.concatenate([lax.select_n(me ^ j, *arrived) for j in range(flips)], axis=1)
    return pl.pallas_call(
        collect_kernel,
        out_shape=jax.ShapeDtypeStruct((share, span * flips), jnp.float32),
        in_specs=[WHOLE] * flips,
        out_specs=WHOLE,
        cost_estimate=LIGHT,
        compiler_params=ROOM,
    )(*arrived)


def pair_rows(masked):
    groups_row = lax.axis_size("row")
    groups_col = lax.axis_size("col")
    cross = []
    for r in range(groups_row):
        for c in range(groups_col):
            odd = (r ^ c) & 1
            cross.append((r * groups_col + c, (r ^ odd) * groups_col + (c ^ odd)))
    held = lax.ppermute(masked, ("row", "col"), cross)
    held = [held] + [flipped(held, "col", flip) for flip in range(2, groups_col, 2)]
    return held + [flipped(piece, "col", 1) for piece in held]


def along_line(mine):
    strips = mine[None]
    bit = lax.axis_size("row") // 2
    while bit > 1:
        strips = joined(strips, flipped(strips, "row", bit), bit)
        bit //= 2
    return strips


def local(inverse_set, presence, factor, dinv):
    groups_row = lax.axis_size("row")
    groups_col = lax.axis_size("col")
    block_rows, _, order, width = factor.shape
    block_cols = inverse_set.shape[3]
    span = width // groups_col
    rows = block_rows * order
    share = order // groups_col

    own = factor.reshape(rows, width)
    blocks = inverse_set.reshape(rows * block_cols, order)
    masked, mine = prepare(presence.reshape(-1), blocks, own, span)
    columns = along_line(mine).reshape(-1, block_rows, order, span).transpose(1, 0, 2, 3)
    columns = columns.reshape(-1, order, span)
    pieces = pair_rows(masked)
    stay, go = halves(own, pieces[0], width // groups_row)
    near = flipped(go, "row", 1)

    both = partials(pieces, columns, near)
    got = flipped(both, "row", 1)
    flips = tuple(range(0, groups_row, 2))
    along, outward = finish(both, got, stay, near, dinv, order, flips, groups_col)
    diag_block = along[0]
    for flip, piece in zip(flips[1:], along[1:]):
        diag_block = diag_block + flipped(piece, "row", flip)

    arrived = [outward[0]] + [flipped(outward[f], "col", f) for f in range(1, groups_col)]
    return (collect(arrived).reshape(block_rows, 1, share, width), diag_block)


def solution(mesh):
    in_specs = (
        P(None, "row", None, None, "col", None),
        P(None, "row", None, "col"),
        P(None, "row", None, None),
        P("row", "col"),
    )
    out_specs = (P(None, "row", "col", None), P("row", "col"))
    return jax.shard_map(local, mesh=mesh, in_specs=in_specs, out_specs=out_specs, check_vma=False)
```

```python
import functools

import jax
import jax.numpy as jnp
from jax import lax
from jax.experimental import pallas as pl
from jax.experimental.pallas import tpu as pltpu
from jax.sharding import PartitionSpec as P

LANES = 128
WHOLE = pl.BlockSpec(memory_space=pltpu.VMEM)
ROOM = pltpu.CompilerParams(vmem_limit_bytes=16 * 1024 * 1024)
HEAVY = 10**11
LIGHT = pl.CostEstimate(flops=1000, bytes_accessed=1000, transcendentals=0)


def flipped(value, axis, flip):
    return lax.ppermute(value, axis, [(i, i ^ flip) for i in range(lax.axis_size(axis))])


def two_parts(value):
    high = value.astype(jnp.bfloat16)
    return high, (value - high.astype(jnp.float32)).astype(jnp.bfloat16)


def product(left, right, contract):
    left_high, left_low = two_parts(left)
    right_high, right_low = two_parts(right)

    def once(a, b):
        return lax.dot_general(a, b, (contract, ((), ())), preferred_element_type=jnp.float32)

    return once(left_high, right_high) + (once(left_high, right_low) + once(left_low, right_high))


def prepare_kernel(presence, blocks, factor, masked, mine):
    rows, span = mine.shape
    mine[...] = factor[:, pl.ds(pl.multiple_of(lax.axis_index("col") * span, LANES), span)]
    block_cols, _, order = masked.shape
    for a in range(rows // order):
        for b in range(block_cols):
            weight = presence[a * block_cols + b].astype(jnp.float32)
            picked = blocks[pl.ds(a * order * block_cols + b, order, stride=block_cols), :]
            masked[b, pl.ds(a * order, order), :] = picked * weight


def prepare(presence, blocks, own, span):
    rows, width = own.shape
    block_cols = blocks.shape[0] // rows
    order = blocks.shape[1]
    if span % LANES:
        first = lax.axis_index("col") * span
        mine = lax.dynamic_slice_in_dim(own, first, span, 1)
        weights = presence.reshape(-1, 1, block_cols, 1).astype(jnp.float32)
        picked = blocks.reshape(-1, order, block_cols, order) * weights
        return picked.transpose(2, 0, 1, 3).reshape(block_cols, rows, order), mine
    return pl.pallas_call(
        prepare_kernel,
        out_shape=(
            jax.ShapeDtypeStruct((block_cols, rows, order), jnp.float32),
            jax.ShapeDtypeStruct((rows, span), jnp.float32),
        ),
        in_specs=[pl.BlockSpec(memory_space=pltpu.SMEM), WHOLE, WHOLE],
        out_specs=(WHOLE, WHOLE),
        cost_estimate=LIGHT,
    )(presence, blocks, own)


def joined_kernel(bit, first, second, out):
    here = jnp.where((lax.axis_index("row") & bit) == 0, 0, 1)
    out[:, here] = first[...]
    out[:, 1 - here] = second[...]


def joined(first, second, bit):
    count, rows, span = first.shape
    both = pl.pallas_call(
        functools.partial(joined_kernel, bit),
        out_shape=jax.ShapeDtypeStruct((count, 2, rows, span), jnp.float32),
        in_specs=[WHOLE, WHOLE],
        out_specs=WHOLE,
        cost_estimate=pl.CostEstimate(flops=HEAVY, bytes_accessed=1000, transcendentals=0),
        compiler_params=ROOM,
    )(first, second)
    return both.reshape(2 * count, rows, span)


def partials_kernel(count, *refs):
    pieces = refs[: 2 * count]
    columns, _, both, *outward = refs[2 * count :]
    block_cols, rows, order = pieces[0].shape
    col_index = lax.axis_index("col")
    left, right = [], []
    for t in range(count):
        for b in range(block_cols):
            left.append(jnp.concatenate([pieces[t][b], pieces[count + t][b]], axis=0))
            right.append(columns[b * count + ((col_index >> 1) ^ t)])
    summed = product(jnp.concatenate(left, axis=1), jnp.concatenate(right, axis=0), ((1,), (0,)))
    here = (col_index & 1) * rows
    both[pl.ds(pl.multiple_of(here, 8), rows), :] = summed[:rows]
    both[pl.ds(pl.multiple_of(rows - here, 8), rows), :] = summed[rows:]
    share = order // len(outward)
    for flip, piece in enumerate(outward):
        start = (col_index ^ flip) * share
        for a in range(2 * rows // order):
            picked = both[pl.ds(pl.multiple_of(a * order + start, 8), share), :]
            piece[pl.ds(a * share, share), :] = -picked


def partials(pieces, columns, near, receivers):
    rows, span = 2 * pieces[0].shape[1], columns.shape[2]
    outward = (jax.ShapeDtypeStruct((rows // receivers, span), jnp.float32),) * receivers
    both, *outward = pl.pallas_call(
        functools.partial(partials_kernel, len(pieces) // 2),
        out_shape=(jax.ShapeDtypeStruct((rows, span), jnp.float32),) + outward,
        in_specs=[WHOLE] * (len(pieces) + 1) + [pl.BlockSpec(memory_space=pl.ANY)],
        out_specs=(WHOLE,) * (1 + receivers),
        cost_estimate=LIGHT,
        compiler_params=ROOM,
    )(*pieces, columns, near)
    return both, outward


def halves_kernel(tall, own, held, stay, go):
    even, odd = [
        jnp.concatenate([own[:, i : i + tall] for i in range(first, own.shape[1], 2 * tall)], axis=1)
        for first in (0, tall)
    ]
    upper = (lax.axis_index("row") & 1) == 1
    stay[...] = jnp.where(upper, odd, even)
    go[...] = jnp.where(upper, even, odd)


def halves(own, held, tall):
    rows, width = own.shape
    part = jax.ShapeDtypeStruct((rows, width // 2), jnp.float32)
    return pl.pallas_call(
        functools.partial(halves_kernel, tall),
        out_shape=(part, part),
        in_specs=[WHOLE, pl.BlockSpec(memory_space=pl.ANY)],
        out_specs=(WHOLE, WHOLE),
        cost_estimate=LIGHT,
        compiler_params=ROOM,
    )(own, held)


def finish_kernel(flips, both, got, stay, near, dinv, *refs):
    along, update, terms = refs[:-2], refs[-2], refs[-1]
    rows = stay.shape[0]
    row_index = lax.axis_index("row")
    here = (row_index & 1) * rows
    update[...] = both[...] + got[...]
    mine = update[pl.ds(pl.multiple_of(here, 8), rows), :]
    other = update[pl.ds(pl.multiple_of(rows - here, 8), rows), :]
    factors = jnp.concatenate([stay[...], near[...]], axis=0)
    terms[...] = product(factors, jnp.concatenate([mine, other], axis=0), ((0,), (0,)))
    tall = dinv.shape[0]
    for flip, piece in zip(flips, along):
        slot = ((row_index ^ flip) >> 1) * tall
        piece[...] = terms[pl.ds(pl.multiple_of(slot, 8), tall), :]
    along[0][...] = along[0][...] + dinv[...]


def finish(both, got, stay, near, dinv, flips):
    rows, half = stay.shape
    span = both.shape[1]
    return pl.pallas_call(
        functools.partial(finish_kernel, flips),
        out_shape=(jax.ShapeDtypeStruct(dinv.shape, jnp.float32),) * len(flips),
        in_specs=[WHOLE] * 5,
        out_specs=(WHOLE,) * len(flips),
        scratch_shapes=[
            pltpu.VMEM((2 * rows, span), jnp.float32),
            pltpu.VMEM((half, span), jnp.float32),
        ],
        cost_estimate=LIGHT,
        compiler_params=ROOM,
    )(both, got, stay, near, dinv)


def collect_kernel(*refs):
    keep, send = refs[-2:]
    share = keep.shape[0]
    span = refs[0].shape[1]
    here = (lax.axis_index("row") & 1) * share
    for flip, piece in enumerate(refs[:-2]):
        spot = pl.ds(pl.multiple_of((lax.axis_index("col") ^ flip) * span, LANES), span)
        keep[:, spot] = piece[pl.ds(pl.multiple_of(here, 8), share), :]
        send[:, spot] = piece[pl.ds(pl.multiple_of(share - here, 8), share), :]


def collect(arrived):
    flips = len(arrived)
    share, span = arrived[0].shape[0] // 2, arrived[0].shape[1]
    if span % LANES:
        me = lax.axis_index("col")
        row_bit = lax.axis_index("row") & 1
        laid = jnp.concatenate([lax.select_n(me ^ j, *arrived) for j in range(flips)], axis=1)
        laid = laid.reshape(2, share, span * flips)
        return [lax.dynamic_index_in_dim(laid, row_bit ^ k, 0, keepdims=False) for k in range(2)]
    part = jax.ShapeDtypeStruct((share, span * flips), jnp.float32)
    return pl.pallas_call(
        collect_kernel,
        out_shape=(part, part),
        in_specs=[WHOLE] * flips,
        out_specs=(WHOLE, WHOLE),
        cost_estimate=LIGHT,
        compiler_params=ROOM,
    )(*arrived)


def pair_rows(masked):
    groups_row = lax.axis_size("row")
    groups_col = lax.axis_size("col")
    cross = []
    for r in range(groups_row):
        for c in range(groups_col):
            odd = (r ^ c) & 1
            cross.append((r * groups_col + c, (r ^ odd) * groups_col + (c ^ odd)))
    held = lax.ppermute(masked, ("row", "col"), cross)
    held = [held] + [flipped(held, "col", flip) for flip in range(2, groups_col, 2)]
    return held + [flipped(piece, "col", 1) for piece in held]


def along_line(mine):
    strips = mine[None]
    bit = lax.axis_size("row") // 2
    while bit > 1:
        strips = joined(strips, flipped(strips, "row", bit), bit)
        bit //= 2
    return strips


def local(inverse_set, presence, factor, dinv):
    groups_row = lax.axis_size("row")
    groups_col = lax.axis_size("col")
    block_rows, _, order, width = factor.shape
    block_cols = inverse_set.shape[3]
    span = width // groups_col
    rows = block_rows * order
    share = order // groups_col

    own = factor.reshape(rows, width)
    blocks = inverse_set.reshape(rows * block_cols, order)
    masked, mine = prepare(presence.reshape(-1), blocks, own, span)
    columns = along_line(mine).reshape(-1, block_rows, order, span).transpose(1, 0, 2, 3)
    columns = columns.reshape(-1, order, span)
    pieces = pair_rows(masked)
    stay, go = halves(own, pieces[0], width // groups_row)
    near = flipped(go, "row", 1)

    both, outward = partials(pieces, columns, near, groups_col)
    got = flipped(both, "row", 1)
    arrived = [outward[0]] + [flipped(outward[f], "col", f) for f in range(1, groups_col)]
    keep, send = collect(arrived)
    off_diag = keep + flipped(send, "row", 1)

    flips = tuple(range(0, groups_row, 2))
    along = finish(both, got, stay, near, dinv, flips)
    diag_block = along[0]
    for flip, piece in zip(flips[1:], along[1:]):
        diag_block = diag_block + flipped(piece, "row", flip)
    return (off_diag.reshape(block_rows, 1, share, width), diag_block)


def solution(mesh):
    in_specs = (
        P(None, "row", None, None, "col", None),
        P(None, "row", None, "col"),
        P(None, "row", None, None),
        P("row", "col"),
    )
    out_specs = (P(None, "row", "col", None), P("row", "col"))
    return jax.shard_map(local, mesh=mesh, in_specs=in_specs, out_specs=out_specs, check_vma=False)
```

```python
import functools

import jax
import jax.numpy as jnp
from jax import lax
from jax.experimental import pallas as pl
from jax.experimental.pallas import tpu as pltpu
from jax.sharding import PartitionSpec as P

LANES = 128
WHOLE = pl.BlockSpec(memory_space=pltpu.VMEM)
ROOM = pltpu.CompilerParams(vmem_limit_bytes=16 * 1024 * 1024)
HEAVY = 10**9
LIGHT = pl.CostEstimate(flops=1000, bytes_accessed=1000, transcendentals=0)


def flipped(value, axis, flip):
    return lax.ppermute(value, axis, [(i, i ^ flip) for i in range(lax.axis_size(axis))])


def two_parts(value):
    high = value.astype(jnp.bfloat16)
    return high, (value - high.astype(jnp.float32)).astype(jnp.bfloat16)


def product(left, right, contract):
    left_high, left_low = two_parts(left)
    right_high, right_low = two_parts(right)

    def once(a, b):
        return lax.dot_general(a, b, (contract, ((), ())), preferred_element_type=jnp.float32)

    return once(left_high, right_high) + (once(left_high, right_low) + once(left_low, right_high))


def prepare_kernel(presence, blocks, factor, masked, mine):
    rows, span = mine.shape
    mine[...] = factor[:, pl.ds(pl.multiple_of(lax.axis_index("col") * span, LANES), span)]
    block_cols, _, order = masked.shape
    for a in range(rows // order):
        for b in range(block_cols):
            weight = presence[a * block_cols + b].astype(jnp.float32)
            picked = blocks[pl.ds(a * order * block_cols + b, order, stride=block_cols), :]
            masked[b, pl.ds(a * order, order), :] = picked * weight


def prepare(presence, blocks, own, span):
    rows, width = own.shape
    block_cols = blocks.shape[0] // rows
    order = blocks.shape[1]
    if span % LANES:
        first = lax.axis_index("col") * span
        mine = lax.dynamic_slice_in_dim(own, first, span, 1)
        weights = presence.reshape(-1, 1, block_cols, 1).astype(jnp.float32)
        picked = blocks.reshape(-1, order, block_cols, order) * weights
        return picked.transpose(2, 0, 1, 3).reshape(block_cols, rows, order), mine
    return pl.pallas_call(
        prepare_kernel,
        out_shape=(
            jax.ShapeDtypeStruct((block_cols, rows, order), jnp.float32),
            jax.ShapeDtypeStruct((rows, span), jnp.float32),
        ),
        in_specs=[pl.BlockSpec(memory_space=pltpu.SMEM), WHOLE, WHOLE],
        out_specs=(WHOLE, WHOLE),
        cost_estimate=LIGHT,
    )(presence, blocks, own)


def joined_kernel(bit, first, second, out):
    here = jnp.where((lax.axis_index("row") & bit) == 0, 0, 1)
    if first.ndim == 2:
        span = out.shape[3]
        spot = pl.ds(pl.multiple_of(lax.axis_index("col") * span, LANES), span)
        out[0, here] = first[:, spot]
    else:
        out[:, here] = first[...]
    out[:, 1 - here] = second[...]


def joined(first, second, bit):
    count, rows, span = second.shape
    both = pl.pallas_call(
        functools.partial(joined_kernel, bit),
        out_shape=jax.ShapeDtypeStruct((count, 2, rows, span), jnp.float32),
        in_specs=[WHOLE, WHOLE],
        out_specs=WHOLE,
        cost_estimate=pl.CostEstimate(flops=HEAVY, bytes_accessed=1000, transcendentals=0),
        compiler_params=ROOM,
    )(first, second)
    return both.reshape(2 * count, rows, span)


def partials_kernel(count, *refs):
    pieces = refs[: 2 * count]
    columns, _, both, *outward = refs[2 * count :]
    block_cols, rows, order = pieces[0].shape
    col_index = lax.axis_index("col")
    left, right = [], []
    for t in range(count):
        for b in range(block_cols):
            left.append(jnp.concatenate([pieces[t][b], pieces[count + t][b]], axis=0))
            right.append(columns[b * count + ((col_index >> 1) ^ t)])
    summed = product(jnp.concatenate(left, axis=1), jnp.concatenate(right, axis=0), ((1,), (0,)))
    here = (col_index & 1) * rows
    both[pl.ds(pl.multiple_of(here, 8), rows), :] = summed[:rows]
    both[pl.ds(pl.multiple_of(rows - here, 8), rows), :] = summed[rows:]
    share = order // len(outward)
    for flip, piece in enumerate(outward):
        start = (col_index ^ flip) * share
        for a in range(2 * rows // order):
            picked = both[pl.ds(pl.multiple_of(a * order + start, 8), share), :]
            piece[pl.ds(a * share, share), :] = -picked


def partials(pieces, columns, near, receivers):
    rows, span = 2 * pieces[0].shape[1], columns.shape[2]
    outward = (jax.ShapeDtypeStruct((rows // receivers, span), jnp.float32),) * receivers
    both, *outward = pl.pallas_call(
        functools.partial(partials_kernel, len(pieces) // 2),
        out_shape=(jax.ShapeDtypeStruct((rows, span), jnp.float32),) + outward,
        in_specs=[WHOLE] * (len(pieces) + 1) + [pl.BlockSpec(memory_space=pl.ANY)],
        out_specs=(WHOLE,) * (1 + receivers),
        cost_estimate=LIGHT,
        compiler_params=ROOM,
    )(*pieces, columns, near)
    return both, outward


def halves_kernel(tall, own, held, stay, go):
    even, odd = [
        jnp.concatenate([own[:, i : i + tall] for i in range(first, own.shape[1], 2 * tall)], axis=1)
        for first in (0, tall)
    ]
    upper = (lax.axis_index("row") & 1) == 1
    stay[...] = jnp.where(upper, odd, even)
    go[...] = jnp.where(upper, even, odd)


def halves(own, held, tall):
    rows, width = own.shape
    part = jax.ShapeDtypeStruct((rows, width // 2), jnp.float32)
    return pl.pallas_call(
        functools.partial(halves_kernel, tall),
        out_shape=(part, part),
        in_specs=[WHOLE, pl.BlockSpec(memory_space=pl.ANY)],
        out_specs=(WHOLE, WHOLE),
        cost_estimate=LIGHT,
        compiler_params=ROOM,
    )(own, held)


def finish_kernel(flips, both, got, stay, near, dinv, *refs):
    along, update, terms = refs[:-2], refs[-2], refs[-1]
    rows = stay.shape[0]
    row_index = lax.axis_index("row")
    here = (row_index & 1) * rows
    update[...] = both[...] + got[...]
    mine = update[pl.ds(pl.multiple_of(here, 8), rows), :]
    other = update[pl.ds(pl.multiple_of(rows - here, 8), rows), :]
    factors = jnp.concatenate([stay[...], near[...]], axis=0)
    terms[...] = product(factors, jnp.concatenate([mine, other], axis=0), ((0,), (0,)))
    tall = dinv.shape[0]
    for flip, piece in zip(flips, along):
        slot = ((row_index ^ flip) >> 1) * tall
        piece[...] = terms[pl.ds(pl.multiple_of(slot, 8), tall), :]
    along[0][...] = along[0][...] + dinv[...]


def finish(both, got, stay, near, dinv, flips):
    rows, half = stay.shape
    span = both.shape[1]
    return pl.pallas_call(
        functools.partial(finish_kernel, flips),
        out_shape=(jax.ShapeDtypeStruct(dinv.shape, jnp.float32),) * len(flips),
        in_specs=[WHOLE] * 5,
        out_specs=(WHOLE,) * len(flips),
        scratch_shapes=[
            pltpu.VMEM((2 * rows, span), jnp.float32),
            pltpu.VMEM((half, span), jnp.float32),
        ],
        cost_estimate=LIGHT,
        compiler_params=ROOM,
    )(both, got, stay, near, dinv)


def collect_kernel(*refs):
    arrived, (_, keep, send) = refs[:-3], refs[-3:]
    share = keep.shape[0]
    span = refs[0].shape[1]
    here = (lax.axis_index("row") & 1) * share
    for flip, piece in enumerate(arrived):
        spot = pl.ds(pl.multiple_of((lax.axis_index("col") ^ flip) * span, LANES), span)
        keep[:, spot] = piece[pl.ds(pl.multiple_of(here, 8), share), :]
        send[:, spot] = piece[pl.ds(pl.multiple_of(share - here, 8), share), :]


def collect(arrived, along):
    flips = len(arrived)
    share, span = arrived[0].shape[0] // 2, arrived[0].shape[1]
    if span % LANES:
        me = lax.axis_index("col")
        row_bit = lax.axis_index("row") & 1
        laid = jnp.concatenate([lax.select_n(me ^ j, *arrived) for j in range(flips)], axis=1)
        laid = laid.reshape(2, share, span * flips)
        return [lax.dynamic_index_in_dim(laid, row_bit ^ k, 0, keepdims=False) for k in range(2)]
    part = jax.ShapeDtypeStruct((share, span * flips), jnp.float32)
    return pl.pallas_call(
        collect_kernel,
        out_shape=(part, part),
        in_specs=[WHOLE] * flips + [pl.BlockSpec(memory_space=pl.ANY)],
        out_specs=(WHOLE, WHOLE),
        cost_estimate=LIGHT,
        compiler_params=ROOM,
    )(*arrived, along)


def pair_rows(masked):
    groups_row = lax.axis_size("row")
    groups_col = lax.axis_size("col")
    cross = []
    for r in range(groups_row):
        for c in range(groups_col):
            odd = (r ^ c) & 1
            cross.append((r * groups_col + c, (r ^ odd) * groups_col + (c ^ odd)))
    held = lax.ppermute(masked, ("row", "col"), cross)
    held = [held] + [flipped(held, "col", flip) for flip in range(2, groups_col, 2)]
    return held + [flipped(piece, "col", 1) for piece in held]


def along_line(mine, own):
    strips = mine[None]
    bit = lax.axis_size("row") // 2
    while bit > 1:
        whole = strips.shape[0] == 1 and mine.shape[1] % LANES == 0
        strips = joined(own if whole else strips, flipped(strips, "row", bit), bit)
        bit //= 2
    return strips


def local(inverse_set, presence, factor, dinv):
    groups_row = lax.axis_size("row")
    groups_col = lax.axis_size("col")
    block_rows, _, order, width = factor.shape
    block_cols = inverse_set.shape[3]
    span = width // groups_col
    rows = block_rows * order
    share = order // groups_col

    own = factor.reshape(rows, width)
    blocks = inverse_set.reshape(rows * block_cols, order)
    masked, mine = prepare(presence.reshape(-1), blocks, own, span)
    columns = along_line(mine, own).reshape(-1, block_rows, order, span).transpose(1, 0, 2, 3)
    columns = columns.reshape(-1, order, span)
    pieces = pair_rows(masked)
    stay, go = halves(own, pieces[0], width // groups_row)
    near = flipped(go, "row", 1)

    both, outward = partials(pieces, columns, near, groups_col)
    got = flipped(both, "row", 1)
    arrived = [outward[0]] + [flipped(outward[f], "col", f) for f in range(1, groups_col)]
    flips = tuple(range(0, groups_row, 2))
    along = finish(both, got, stay, near, dinv, flips)
    keep, send = collect(arrived, along[0])
    off_diag = keep + flipped(send, "row", 1)
    diag_block = along[0]
    for flip, piece in zip(flips[1:], along[1:]):
        diag_block = diag_block + flipped(piece, "row", flip)
    return (off_diag.reshape(block_rows, 1, share, width), diag_block)


def solution(mesh):
    in_specs = (
        P(None, "row", None, None, "col", None),
        P(None, "row", None, "col"),
        P(None, "row", None, None),
        P("row", "col"),
    )
    out_specs = (P(None, "row", "col", None), P("row", "col"))
    return jax.shard_map(local, mesh=mesh, in_specs=in_specs, out_specs=out_specs, check_vma=False)
```

```python
import functools

import jax
import jax.numpy as jnp
from jax import lax
from jax.experimental import pallas as pl
from jax.experimental.pallas import tpu as pltpu
from jax.sharding import PartitionSpec as P

LANES = 128
WHOLE = pl.BlockSpec(memory_space=pltpu.VMEM)
ROOM = pltpu.CompilerParams(vmem_limit_bytes=16 * 1024 * 1024)
HEAVY = 10**9
LIGHT = pl.CostEstimate(flops=1000, bytes_accessed=1000, transcendentals=0)


def flipped(value, axis, flip):
    return lax.ppermute(value, axis, [(i, i ^ flip) for i in range(lax.axis_size(axis))])


def two_parts(value):
    high = value.astype(jnp.bfloat16)
    return high, (value - high.astype(jnp.float32)).astype(jnp.bfloat16)


def product(left, right, contract):
    left_high, left_low = two_parts(left)
    right_high, right_low = two_parts(right)

    def once(a, b):
        return lax.dot_general(a, b, (contract, ((), ())), preferred_element_type=jnp.float32)

    return once(left_high, right_high) + (once(left_high, right_low) + once(left_low, right_high))


def prepare_kernel(presence, blocks, factor, masked, mine):
    rows, span = mine.shape
    mine[...] = factor[:, pl.ds(pl.multiple_of(lax.axis_index("col") * span, LANES), span)]
    block_cols, _, order = masked.shape
    for a in range(rows // order):
        for b in range(block_cols):
            weight = presence[a * block_cols + b].astype(jnp.float32)
            picked = blocks[pl.ds(a * order * block_cols + b, order, stride=block_cols), :]
            masked[b, pl.ds(a * order, order), :] = picked * weight


def prepare(presence, blocks, own, span):
    rows, width = own.shape
    block_cols = blocks.shape[0] // rows
    order = blocks.shape[1]
    if span % LANES:
        first = lax.axis_index("col") * span
        mine = lax.dynamic_slice_in_dim(own, first, span, 1)
        weights = presence.reshape(-1, 1, block_cols, 1).astype(jnp.float32)
        picked = blocks.reshape(-1, order, block_cols, order) * weights
        return picked.transpose(2, 0, 1, 3).reshape(block_cols, rows, order), mine
    return pl.pallas_call(
        prepare_kernel,
        out_shape=(
            jax.ShapeDtypeStruct((block_cols, rows, order), jnp.float32),
            jax.ShapeDtypeStruct((rows, span), jnp.float32),
        ),
        in_specs=[pl.BlockSpec(memory_space=pltpu.SMEM), WHOLE, WHOLE],
        out_specs=(WHOLE, WHOLE),
        cost_estimate=LIGHT,
    )(presence, blocks, own)


def joined_kernel(bit, first, second, near, out):
    here = jnp.where((lax.axis_index("row") & bit) == 0, 0, 1)
    if first.ndim == 2:
        span = out.shape[3]
        spot = pl.ds(pl.multiple_of(lax.axis_index("col") * span, LANES), span)
        out[0, here] = first[:, spot]
    else:
        out[:, here] = first[...]
    out[:, 1 - here] = second[...]


def joined(first, second, bit, near):
    count, rows, span = second.shape
    both = pl.pallas_call(
        functools.partial(joined_kernel, bit),
        out_shape=jax.ShapeDtypeStruct((count, 2, rows, span), jnp.float32),
        in_specs=[WHOLE, WHOLE, pl.BlockSpec(memory_space=pl.ANY)],
        out_specs=WHOLE,
        cost_estimate=pl.CostEstimate(flops=HEAVY, bytes_accessed=1000, transcendentals=0),
        compiler_params=ROOM,
    )(first, second, near)
    return both.reshape(2 * count, rows, span)


def partials_kernel(count, *refs):
    pieces = refs[: 2 * count]
    columns, both, *outward = refs[2 * count :]
    block_cols, rows, order = pieces[0].shape
    col_index = lax.axis_index("col")
    left, right = [], []
    for t in range(count):
        for b in range(block_cols):
            left.append(jnp.concatenate([pieces[t][b], pieces[count + t][b]], axis=0))
            right.append(columns[b * count + ((col_index >> 1) ^ t)])
    summed = product(jnp.concatenate(left, axis=1), jnp.concatenate(right, axis=0), ((1,), (0,)))
    here = (col_index & 1) * rows
    both[pl.ds(pl.multiple_of(here, 8), rows), :] = summed[:rows]
    both[pl.ds(pl.multiple_of(rows - here, 8), rows), :] = summed[rows:]
    share = order // len(outward)
    for flip, piece in enumerate(outward):
        start = (col_index ^ flip) * share
        for a in range(2 * rows // order):
            picked = both[pl.ds(pl.multiple_of(a * order + start, 8), share), :]
            piece[pl.ds(a * share, share), :] = -picked


def partials(pieces, columns, receivers):
    rows, span = 2 * pieces[0].shape[1], columns.shape[2]
    outward = (jax.ShapeDtypeStruct((rows // receivers, span), jnp.float32),) * receivers
    both, *outward = pl.pallas_call(
        functools.partial(partials_kernel, len(pieces) // 2),
        out_shape=(jax.ShapeDtypeStruct((rows, span), jnp.float32),) + outward,
        in_specs=[WHOLE] * (len(pieces) + 1),
        out_specs=(WHOLE,) * (1 + receivers),
        cost_estimate=LIGHT,
        compiler_params=ROOM,
    )(*pieces, columns)
    return both, outward


def halves_kernel(tall, own, stay, go):
    even, odd = [
        jnp.concatenate([own[:, i : i + tall] for i in range(first, own.shape[1], 2 * tall)], axis=1)
        for first in (0, tall)
    ]
    upper = (lax.axis_index("row") & 1) == 1
    stay[...] = jnp.where(upper, odd, even)
    go[...] = jnp.where(upper, even, odd)


def halves(own, tall):
    rows, width = own.shape
    part = jax.ShapeDtypeStruct((rows, width // 2), jnp.float32)
    return pl.pallas_call(
        functools.partial(halves_kernel, tall),
        out_shape=(part, part),
        in_specs=[WHOLE],
        out_specs=(WHOLE, WHOLE),
        cost_estimate=LIGHT,
        compiler_params=ROOM,
    )(own)


def finish_kernel(flips, both, got, stay, near, dinv, *refs):
    along, update, terms = refs[:-2], refs[-2], refs[-1]
    rows = stay.shape[0]
    row_index = lax.axis_index("row")
    here = (row_index & 1) * rows
    update[...] = both[...] + got[...]
    mine = update[pl.ds(pl.multiple_of(here, 8), rows), :]
    other = update[pl.ds(pl.multiple_of(rows - here, 8), rows), :]
    factors = jnp.concatenate([stay[...], near[...]], axis=0)
    terms[...] = product(factors, jnp.concatenate([mine, other], axis=0), ((0,), (0,)))
    tall = dinv.shape[0]
    for flip, piece in zip(flips, along):
        slot = ((row_index ^ flip) >> 1) * tall
        piece[...] = terms[pl.ds(pl.multiple_of(slot, 8), tall), :]
    along[0][...] = along[0][...] + dinv[...]


def finish(both, got, stay, near, dinv, flips):
    rows, half = stay.shape
    span = both.shape[1]
    return pl.pallas_call(
        functools.partial(finish_kernel, flips),
        out_shape=(jax.ShapeDtypeStruct(dinv.shape, jnp.float32),) * len(flips),
        in_specs=[WHOLE] * 5,
        out_specs=(WHOLE,) * len(flips),
        scratch_shapes=[
            pltpu.VMEM((2 * rows, span), jnp.float32),
            pltpu.VMEM((half, span), jnp.float32),
        ],
        cost_estimate=LIGHT,
        compiler_params=ROOM,
    )(both, got, stay, near, dinv)


def collect_kernel(*refs):
    arrived, (_, keep, send) = refs[:-3], refs[-3:]
    share = keep.shape[0]
    span = refs[0].shape[1]
    here = (lax.axis_index("row") & 1) * share
    for flip, piece in enumerate(arrived):
        spot = pl.ds(pl.multiple_of((lax.axis_index("col") ^ flip) * span, LANES), span)
        keep[:, spot] = piece[pl.ds(pl.multiple_of(here, 8), share), :]
        send[:, spot] = piece[pl.ds(pl.multiple_of(share - here, 8), share), :]


def collect(arrived, along):
    flips = len(arrived)
    share, span = arrived[0].shape[0] // 2, arrived[0].shape[1]
    if span % LANES:
        me = lax.axis_index("col")
        row_bit = lax.axis_index("row") & 1
        laid = jnp.concatenate([lax.select_n(me ^ j, *arrived) for j in range(flips)], axis=1)
        laid = laid.reshape(2, share, span * flips)
        return [lax.dynamic_index_in_dim(laid, row_bit ^ k, 0, keepdims=False) for k in range(2)]
    part = jax.ShapeDtypeStruct((share, span * flips), jnp.float32)
    return pl.pallas_call(
        collect_kernel,
        out_shape=(part, part),
        in_specs=[WHOLE] * flips + [pl.BlockSpec(memory_space=pl.ANY)],
        out_specs=(WHOLE, WHOLE),
        cost_estimate=LIGHT,
        compiler_params=ROOM,
    )(*arrived, along)


def pair_rows(masked):
    groups_row = lax.axis_size("row")
    groups_col = lax.axis_size("col")
    cross = []
    for r in range(groups_row):
        for c in range(groups_col):
            odd = (r ^ c) & 1
            cross.append((r * groups_col + c, (r ^ odd) * groups_col + (c ^ odd)))
    held = lax.ppermute(masked, ("row", "col"), cross)
    held = [held] + [flipped(held, "col", flip) for flip in range(2, groups_col, 2)]
    return held + [flipped(piece, "col", 1) for piece in held]


def along_line(mine, own, near):
    strips = mine[None]
    bit = lax.axis_size("row") // 2
    while bit > 1:
        whole = strips.shape[0] == 1 and mine.shape[1] % LANES == 0
        first = own if whole else strips
        strips = joined(first, flipped(strips, "row", bit), bit, near if bit == 2 else mine)
        bit //= 2
    return strips


def local(inverse_set, presence, factor, dinv):
    groups_row = lax.axis_size("row")
    groups_col = lax.axis_size("col")
    block_rows, _, order, width = factor.shape
    block_cols = inverse_set.shape[3]
    span = width // groups_col
    rows = block_rows * order
    share = order // groups_col

    own = factor.reshape(rows, width)
    blocks = inverse_set.reshape(rows * block_cols, order)
    masked, mine = prepare(presence.reshape(-1), blocks, own, span)
    stay, go = halves(own, width // groups_row)
    near = flipped(go, "row", 1)
    columns = along_line(mine, own, near).reshape(-1, block_rows, order, span).transpose(1, 0, 2, 3)
    columns = columns.reshape(-1, order, span)
    pieces = pair_rows(masked)

    both, outward = partials(pieces, columns, groups_col)
    got = flipped(both, "row", 1)
    arrived = [outward[0]] + [flipped(outward[f], "col", f) for f in range(1, groups_col)]
    flips = (0,) + tuple(range(groups_row - 2, 0, -2))
    along = finish(both, got, stay, near, dinv, flips)
    keep, send = collect(arrived, along[0])
    off_diag = keep + flipped(send, "row", 1)
    diag_block = along[0]
    for flip, piece in zip(flips[1:], along[1:]):
        diag_block = diag_block + flipped(piece, "row", flip)
    return (off_diag.reshape(block_rows, 1, share, width), diag_block)


def solution(mesh):
    in_specs = (
        P(None, "row", None, None, "col", None),
        P(None, "row", None, "col"),
        P(None, "row", None, None),
        P("row", "col"),
    )
    out_specs = (P(None, "row", "col", None), P("row", "col"))
    return jax.shard_map(local, mesh=mesh, in_specs=in_specs, out_specs=out_specs, check_vma=False)
```

```python
import functools

import jax
import jax.numpy as jnp
from jax import lax
from jax.experimental import pallas as pl
from jax.experimental.pallas import tpu as pltpu
from jax.sharding import PartitionSpec as P

LANES = 128
WHOLE = pl.BlockSpec(memory_space=pltpu.VMEM)
ROOM = pltpu.CompilerParams(vmem_limit_bytes=16 * 1024 * 1024)
HEAVY = 10**9
LIGHT = pl.CostEstimate(flops=1000, bytes_accessed=1000, transcendentals=0)


def flipped(value, axis, flip):
    return lax.ppermute(value, axis, [(i, i ^ flip) for i in range(lax.axis_size(axis))])


def two_parts(value):
    high = value.astype(jnp.bfloat16)
    return high, (value - high.astype(jnp.float32)).astype(jnp.bfloat16)


def product(left, right, contract):
    left_high, left_low = two_parts(left)
    right_high, right_low = two_parts(right)

    def once(a, b):
        return lax.dot_general(a, b, (contract, ((), ())), preferred_element_type=jnp.float32)

    return once(left_high, right_high) + (once(left_high, right_low) + once(left_low, right_high))


def prepare_kernel(presence, blocks, factor, masked, mine):
    rows, span = mine.shape
    mine[...] = factor[:, pl.ds(pl.multiple_of(lax.axis_index("col") * span, LANES), span)]
    block_cols, _, order = masked.shape
    for a in range(rows // order):
        for b in range(block_cols):
            weight = presence[a * block_cols + b].astype(jnp.float32)
            picked = blocks[pl.ds(a * order * block_cols + b, order, stride=block_cols), :]
            masked[b, pl.ds(a * order, order), :] = picked * weight


def prepare(presence, blocks, own, span):
    rows, width = own.shape
    block_cols = blocks.shape[0] // rows
    order = blocks.shape[1]
    if span % LANES:
        first = lax.axis_index("col") * span
        mine = lax.dynamic_slice_in_dim(own, first, span, 1)
        weights = presence.reshape(-1, 1, block_cols, 1).astype(jnp.float32)
        picked = blocks.reshape(-1, order, block_cols, order) * weights
        return picked.transpose(2, 0, 1, 3).reshape(block_cols, rows, order), mine
    return pl.pallas_call(
        prepare_kernel,
        out_shape=(
            jax.ShapeDtypeStruct((block_cols, rows, order), jnp.float32),
            jax.ShapeDtypeStruct((rows, span), jnp.float32),
        ),
        in_specs=[pl.BlockSpec(memory_space=pltpu.SMEM), WHOLE, WHOLE],
        out_specs=(WHOLE, WHOLE),
        cost_estimate=LIGHT,
    )(presence, blocks, own)


def joined_kernel(bit, first, second, near, out):
    here = jnp.where((lax.axis_index("row") & bit) == 0, 0, 1)
    if first.ndim == 2:
        span = out.shape[3]
        spot = pl.ds(pl.multiple_of(lax.axis_index("col") * span, LANES), span)
        out[0, here] = first[:, spot]
    else:
        out[:, here] = first[...]
    out[:, 1 - here] = second[...]


def joined(first, second, bit, near):
    count, rows, span = second.shape
    both = pl.pallas_call(
        functools.partial(joined_kernel, bit),
        out_shape=jax.ShapeDtypeStruct((count, 2, rows, span), jnp.float32),
        in_specs=[WHOLE, WHOLE, pl.BlockSpec(memory_space=pl.ANY)],
        out_specs=WHOLE,
        cost_estimate=pl.CostEstimate(flops=HEAVY, bytes_accessed=1000, transcendentals=0),
        compiler_params=ROOM,
    )(first, second, near)
    return both.reshape(2 * count, rows, span)


def partials_kernel(count, *refs):
    pieces = refs[: 2 * count]
    columns, both, *outward = refs[2 * count :]
    block_cols, rows, order = pieces[0].shape
    col_index = lax.axis_index("col")
    left, right = [], []
    for t in range(count):
        for b in range(block_cols):
            left.append(jnp.concatenate([pieces[t][b], pieces[count + t][b]], axis=0))
            right.append(columns[b * count + ((col_index >> 1) ^ t)])
    summed = product(jnp.concatenate(left, axis=1), jnp.concatenate(right, axis=0), ((1,), (0,)))
    here = (col_index & 1) * rows
    both[pl.ds(pl.multiple_of(here, 8), rows), :] = summed[:rows]
    both[pl.ds(pl.multiple_of(rows - here, 8), rows), :] = summed[rows:]
    share = order // len(outward)
    for flip, piece in enumerate(outward):
        start = (col_index ^ flip) * share
        for a in range(2 * rows // order):
            picked = both[pl.ds(pl.multiple_of(a * order + start, 8), share), :]
            piece[pl.ds(a * share, share), :] = -picked


def partials(pieces, columns, receivers):
    rows, span = 2 * pieces[0].shape[1], columns.shape[2]
    outward = (jax.ShapeDtypeStruct((rows // receivers, span), jnp.float32),) * receivers
    both, *outward = pl.pallas_call(
        functools.partial(partials_kernel, len(pieces) // 2),
        out_shape=(jax.ShapeDtypeStruct((rows, span), jnp.float32),) + outward,
        in_specs=[WHOLE] * (len(pieces) + 1),
        out_specs=(WHOLE,) * (1 + receivers),
        cost_estimate=LIGHT,
        compiler_params=ROOM,
    )(*pieces, columns)
    return both, outward


def halves_kernel(tall, own, stay, go):
    even, odd = [
        jnp.concatenate([own[:, i : i + tall] for i in range(first, own.shape[1], 2 * tall)], axis=1)
        for first in (0, tall)
    ]
    upper = (lax.axis_index("row") & 1) == 1
    stay[...] = jnp.where(upper, odd, even)
    go[...] = jnp.where(upper, even, odd)


def halves(own, tall):
    rows, width = own.shape
    part = jax.ShapeDtypeStruct((rows, width // 2), jnp.float32)
    return pl.pallas_call(
        functools.partial(halves_kernel, tall),
        out_shape=(part, part),
        in_specs=[WHOLE],
        out_specs=(WHOLE, WHOLE),
        cost_estimate=LIGHT,
        compiler_params=ROOM,
    )(own)


def finish_kernel(flips, both, got, stay, near, dinv, *refs):
    along, update, terms = refs[:-2], refs[-2], refs[-1]
    rows = stay.shape[0]
    row_index = lax.axis_index("row")
    here = (row_index & 1) * rows
    update[...] = both[...] + got[...]
    mine = update[pl.ds(pl.multiple_of(here, 8), rows), :]
    other = update[pl.ds(pl.multiple_of(rows - here, 8), rows), :]
    factors = jnp.concatenate([stay[...], near[...]], axis=0)
    terms[...] = product(factors, jnp.concatenate([mine, other], axis=0), ((0,), (0,)))
    tall = dinv.shape[0]
    for flip, piece in zip(flips, along):
        slot = ((row_index ^ flip) >> 1) * tall
        piece[...] = terms[pl.ds(pl.multiple_of(slot, 8), tall), :]
    along[0][...] = along[0][...] + dinv[...]


def finish(both, got, stay, near, dinv, flips):
    rows, half = stay.shape
    span = both.shape[1]
    return pl.pallas_call(
        functools.partial(finish_kernel, flips),
        out_shape=(jax.ShapeDtypeStruct(dinv.shape, jnp.float32),) * len(flips),
        in_specs=[WHOLE] * 5,
        out_specs=(WHOLE,) * len(flips),
        scratch_shapes=[
            pltpu.VMEM((2 * rows, span), jnp.float32),
            pltpu.VMEM((half, span), jnp.float32),
        ],
        cost_estimate=LIGHT,
        compiler_params=ROOM,
    )(both, got, stay, near, dinv)


def collect_kernel(*refs):
    arrived, (keep, send) = refs[:-2], refs[-2:]
    share = keep.shape[0]
    span = refs[0].shape[1]
    here = (lax.axis_index("row") & 1) * share
    for flip, piece in enumerate(arrived):
        spot = pl.ds(pl.multiple_of((lax.axis_index("col") ^ flip) * span, LANES), span)
        keep[:, spot] = piece[pl.ds(pl.multiple_of(here, 8), share), :]
        send[:, spot] = piece[pl.ds(pl.multiple_of(share - here, 8), share), :]


def collect(arrived):
    flips = len(arrived)
    share, span = arrived[0].shape[0] // 2, arrived[0].shape[1]
    if span % LANES:
        me = lax.axis_index("col")
        row_bit = lax.axis_index("row") & 1
        laid = jnp.concatenate([lax.select_n(me ^ j, *arrived) for j in range(flips)], axis=1)
        laid = laid.reshape(2, share, span * flips)
        return [lax.dynamic_index_in_dim(laid, row_bit ^ k, 0, keepdims=False) for k in range(2)]
    part = jax.ShapeDtypeStruct((share, span * flips), jnp.float32)
    return pl.pallas_call(
        collect_kernel,
        out_shape=(part, part),
        in_specs=[WHOLE] * flips,
        out_specs=(WHOLE, WHOLE),
        cost_estimate=LIGHT,
        compiler_params=ROOM,
    )(*arrived)


def close_kernel(keep, came, *refs):
    along, (off_diag, diag_block) = refs[:-2], refs[-2:]
    off_diag[...] = keep[...] + came[...]
    total = along[0][...]
    for piece in along[1:]:
        total = total + piece[...]
    diag_block[...] = total


def close(keep, came, along):
    return pl.pallas_call(
        close_kernel,
        out_shape=[jax.ShapeDtypeStruct(x.shape, jnp.float32) for x in (keep, along[0])],
        in_specs=[WHOLE] * (2 + len(along)),
        out_specs=[WHOLE, WHOLE],
        cost_estimate=LIGHT,
        compiler_params=ROOM,
    )(keep, came, *along)


def pick_kernel(masked, swapped, held):
    same = (lax.axis_index("row") & 1) == (lax.axis_index("col") & 1)
    held[...] = jnp.where(same, masked[...], swapped[...])


def pair_rows(masked):
    groups_row = lax.axis_size("row")
    groups_col = lax.axis_size("col")
    cross = [
        (r * groups_col + c, (r ^ 1) * groups_col + (c ^ 1))
        for r in range(groups_row)
        for c in range(groups_col)
        if (r ^ c) & 1
    ]
    held = pl.pallas_call(
        pick_kernel,
        out_shape=jax.ShapeDtypeStruct(masked.shape, jnp.float32),
        in_specs=[WHOLE, WHOLE],
        out_specs=WHOLE,
        cost_estimate=LIGHT,
        compiler_params=ROOM,
    )(masked, lax.ppermute(masked, ("row", "col"), cross))
    held = [held] + [flipped(held, "col", flip) for flip in range(2, groups_col, 2)]
    return held + [flipped(piece, "col", 1) for piece in held]


def along_line(mine, own, near):
    strips = mine[None]
    bit = lax.axis_size("row") // 2
    while bit > 1:
        whole = strips.shape[0] == 1 and mine.shape[1] % LANES == 0
        first = own if whole else strips
        strips = joined(first, flipped(strips, "row", bit), bit, near if bit == 2 else mine)
        bit //= 2
    return strips


def local(inverse_set, presence, factor, dinv):
    groups_row = lax.axis_size("row")
    groups_col = lax.axis_size("col")
    block_rows, _, order, width = factor.shape
    block_cols = inverse_set.shape[3]
    span = width // groups_col
    rows = block_rows * order
    share = order // groups_col

    own = factor.reshape(rows, width)
    blocks = inverse_set.reshape(rows * block_cols, order)
    masked, mine = prepare(presence.reshape(-1), blocks, own, span)
    stay, go = halves(own, width // groups_row)
    near = flipped(go, "row", 1)
    columns = along_line(mine, own, near).reshape(-1, block_rows, order, span).transpose(1, 0, 2, 3)
    columns = columns.reshape(-1, order, span)
    pieces = pair_rows(masked)

    both, outward = partials(pieces, columns, groups_col)
    got = flipped(both, "row", 1)
    arrived = [outward[0]] + [flipped(outward[f], "col", f) for f in range(1, groups_col)]
    keep, send = collect(arrived)
    came = flipped(send, "row", 1)

    flips = (0,) + tuple(range(groups_row - 2, 0, -2))
    along = finish(both, got, stay, near, dinv, flips)
    met = [flipped(piece, "row", flip) if flip else piece for flip, piece in zip(flips, along)]
    off_diag, diag_block = close(keep, came, met)
    return (off_diag.reshape(block_rows, 1, share, width), diag_block)


def solution(mesh):
    in_specs = (
        P(None, "row", None, None, "col", None),
        P(None, "row", None, "col"),
        P(None, "row", None, None),
        P("row", "col"),
    )
    out_specs = (P(None, "row", "col", None), P("row", "col"))
    return jax.shard_map(local, mesh=mesh, in_specs=in_specs, out_specs=out_specs, check_vma=False)
```

```python
import functools

import jax
import jax.numpy as jnp
from jax import lax
from jax.experimental import pallas as pl
from jax.experimental.pallas import tpu as pltpu
from jax.sharding import PartitionSpec as P

LANES = 128
WHOLE = pl.BlockSpec(memory_space=pltpu.VMEM)
ROOM = pltpu.CompilerParams(vmem_limit_bytes=16 * 1024 * 1024)
HEAVY = 10**9
LIGHT = pl.CostEstimate(flops=1000, bytes_accessed=1000, transcendentals=0)


def flipped(value, axis, flip):
    return lax.ppermute(value, axis, [(i, i ^ flip) for i in range(lax.axis_size(axis))])


def two_parts(value):
    high = value.astype(jnp.bfloat16)
    return high, (value - high.astype(jnp.float32)).astype(jnp.bfloat16)


def product(left, right, contract):
    left_high, left_low = two_parts(left)
    right_high, right_low = two_parts(right)

    def once(a, b):
        return lax.dot_general(a, b, (contract, ((), ())), preferred_element_type=jnp.float32)

    return once(left_high, right_high) + (once(left_high, right_low) + once(left_low, right_high))


def parity_half(factor, tall, parity):
    even, odd = [
        jnp.concatenate(
            [factor[:, i : i + tall] for i in range(first, factor.shape[1], 2 * tall)], axis=1
        )
        for first in (0, tall)
    ]
    return jnp.where(parity == 1, odd, even)


def prepare_kernel(tall, presence, blocks, factor, masked, swap, mine):
    rows, span = mine.shape
    mine[...] = factor[:, pl.ds(pl.multiple_of(lax.axis_index("col") * span, LANES), span)]
    row_bit = lax.axis_index("row") & 1
    same = row_bit == (lax.axis_index("col") & 1)
    block_cols, _, order = masked.shape
    for a in range(rows // order):
        for b in range(block_cols):
            weight = presence[a * block_cols + b].astype(jnp.float32)
            picked = blocks[pl.ds(a * order * block_cols + b, order, stride=block_cols), :]
            masked[b, pl.ds(a * order, order), :] = picked * weight
    half = parity_half(factor[...], tall, 1 - row_bit)
    for b in range(swap.shape[0]):
        part = half[:, b * order : (b + 1) * order]
        if part.shape[1] and b < block_cols:
            swap[b] = jnp.where(same, part, masked[b])
        else:
            swap[b] = part if part.shape[1] else masked[b]


def prepare(presence, blocks, own, span, tall):
    rows, width = own.shape
    block_cols = blocks.shape[0] // rows
    order = blocks.shape[1]
    depth = max(block_cols, width // 2 // order)
    if span % LANES:
        first = lax.axis_index("col") * span
        row_bit = lax.axis_index("row") & 1
        same = row_bit == (lax.axis_index("col") & 1)
        mine = lax.dynamic_slice_in_dim(own, first, span, 1)
        weights = presence.reshape(-1, 1, block_cols, 1).astype(jnp.float32)
        picked = blocks.reshape(-1, order, block_cols, order) * weights
        masked = picked.transpose(2, 0, 1, 3).reshape(block_cols, rows, order)
        half = parity_half(own, tall, 1 - row_bit).reshape(rows, -1, order).transpose(1, 0, 2)
        half = jnp.pad(half, ((0, depth - half.shape[0]), (0, 0), (0, 0)))
        padded = jnp.pad(masked, ((0, depth - block_cols), (0, 0), (0, 0)))
        return masked, jnp.where(same, half, padded), mine
    return pl.pallas_call(
        functools.partial(prepare_kernel, tall),
        out_shape=(
            jax.ShapeDtypeStruct((block_cols, rows, order), jnp.float32),
            jax.ShapeDtypeStruct((depth, rows, order), jnp.float32),
            jax.ShapeDtypeStruct((rows, span), jnp.float32),
        ),
        in_specs=[pl.BlockSpec(memory_space=pltpu.SMEM), WHOLE, WHOLE],
        out_specs=(WHOLE,) * 3,
        cost_estimate=LIGHT,
    )(presence, blocks, own)


def joined_kernel(bit, first, second, out):
    here = jnp.where((lax.axis_index("row") & bit) == 0, 0, 1)
    if first.ndim == 2:
        span = out.shape[3]
        spot = pl.ds(pl.multiple_of(lax.axis_index("col") * span, LANES), span)
        out[0, here] = first[:, spot]
    else:
        out[:, here] = first[...]
    out[:, 1 - here] = second[...]


def joined(first, second, bit):
    count, rows, span = second.shape
    both = pl.pallas_call(
        functools.partial(joined_kernel, bit),
        out_shape=jax.ShapeDtypeStruct((count, 2, rows, span), jnp.float32),
        in_specs=[WHOLE, WHOLE],
        out_specs=WHOLE,
        cost_estimate=pl.CostEstimate(flops=HEAVY, bytes_accessed=1000, transcendentals=0),
        compiler_params=ROOM,
    )(first, second)
    return both.reshape(2 * count, rows, span)


def partials_kernel(count, *refs):
    masked, mate, swapped, mate_swapped = refs[:4]
    pieces, refs = refs[4 : 2 * count + 2], refs[2 * count + 2 :]
    columns, both, *outward = refs
    block_cols, rows, order = masked.shape
    col_index = lax.axis_index("col")
    row_bit = lax.axis_index("row") & 1
    same = row_bit == (col_index & 1)
    left, right = [], []
    for t in range(count):
        for b in range(block_cols):
            if t:
                ours, theirs = pieces[t - 1][b], pieces[count + t - 2][b]
                mine = jnp.where(same, ours, theirs)
                other = jnp.where(same, theirs, ours)
            else:
                mine = jnp.where(same, masked[b], mate[b])
                other = jnp.where(same, mate_swapped[b], swapped[b])
            left.append(jnp.concatenate([mine, other], axis=0))
            right.append(columns[b * count + ((col_index >> 1) ^ t)])
    summed = product(jnp.concatenate(left, axis=1), jnp.concatenate(right, axis=0), ((1,), (0,)))
    here = row_bit * rows
    both[pl.ds(pl.multiple_of(here, 8), rows), :] = summed[:rows]
    both[pl.ds(pl.multiple_of(rows - here, 8), rows), :] = summed[rows:]
    share = order // len(outward)
    for flip, piece in enumerate(outward):
        start = (col_index ^ flip) * share
        for a in range(2 * rows // order):
            picked = both[pl.ds(pl.multiple_of(a * order + start, 8), share), :]
            piece[pl.ds(a * share, share), :] = -picked


def partials(pieces, columns, receivers):
    rows, span = 2 * pieces[0].shape[1], columns.shape[2]
    outward = (jax.ShapeDtypeStruct((rows // receivers, span), jnp.float32),) * receivers
    both, *outward = pl.pallas_call(
        functools.partial(partials_kernel, len(pieces) // 2 - 1),
        out_shape=(jax.ShapeDtypeStruct((rows, span), jnp.float32),) + outward,
        in_specs=[WHOLE] * (len(pieces) + 1),
        out_specs=(WHOLE,) * (1 + receivers),
        cost_estimate=LIGHT,
        compiler_params=ROOM,
    )(*pieces, columns)
    return both, outward


def stay_kernel(tall, own, stay):
    stay[...] = parity_half(own[...], tall, lax.axis_index("row") & 1)


def stay_half(own, tall):
    rows, width = own.shape
    return pl.pallas_call(
        functools.partial(stay_kernel, tall),
        out_shape=jax.ShapeDtypeStruct((rows, width // 2), jnp.float32),
        in_specs=[WHOLE],
        out_specs=WHOLE,
        cost_estimate=LIGHT,
        compiler_params=ROOM,
    )(own)


def finish_kernel(flips, both, got, stay, swapped, mate_swapped, dinv, *refs):
    along, update, terms = refs[:-2], refs[-2], refs[-1]
    rows = stay.shape[0]
    row_index = lax.axis_index("row")
    here = (row_index & 1) * rows
    update[...] = both[...] + got[...]
    mine = update[pl.ds(pl.multiple_of(here, 8), rows), :]
    other = update[pl.ds(pl.multiple_of(rows - here, 8), rows), :]
    same = (row_index & 1) == (lax.axis_index("col") & 1)
    depth = stay.shape[1] // swapped.shape[2]
    near = [jnp.where(same, swapped[j], mate_swapped[j]) for j in range(depth)]
    factors = jnp.concatenate([stay[...], jnp.concatenate(near, axis=1)], axis=0)
    terms[...] = product(factors, jnp.concatenate([mine, other], axis=0), ((0,), (0,)))
    tall = dinv.shape[0]
    for flip, piece in zip(flips, along):
        slot = ((row_index ^ flip) >> 1) * tall
        piece[...] = terms[pl.ds(pl.multiple_of(slot, 8), tall), :]
    along[0][...] = along[0][...] + dinv[...]


def finish(both, got, stay, swapped, mate_swapped, dinv, flips):
    rows, half = stay.shape
    span = both.shape[1]
    return pl.pallas_call(
        functools.partial(finish_kernel, flips),
        out_shape=(jax.ShapeDtypeStruct(dinv.shape, jnp.float32),) * len(flips),
        in_specs=[WHOLE] * 6,
        out_specs=(WHOLE,) * len(flips),
        scratch_shapes=[
            pltpu.VMEM((2 * rows, span), jnp.float32),
            pltpu.VMEM((half, span), jnp.float32),
        ],
        cost_estimate=LIGHT,
        compiler_params=ROOM,
    )(both, got, stay, swapped, mate_swapped, dinv)


def collect_kernel(*refs):
    arrived, (keep, send) = refs[:-2], refs[-2:]
    share = keep.shape[0]
    span = refs[0].shape[1]
    here = (lax.axis_index("row") & 1) * share
    for flip, piece in enumerate(arrived):
        spot = pl.ds(pl.multiple_of((lax.axis_index("col") ^ flip) * span, LANES), span)
        keep[:, spot] = piece[pl.ds(pl.multiple_of(here, 8), share), :]
        send[:, spot] = piece[pl.ds(pl.multiple_of(share - here, 8), share), :]


def collect(arrived):
    flips = len(arrived)
    share, span = arrived[0].shape[0] // 2, arrived[0].shape[1]
    if span % LANES:
        me = lax.axis_index("col")
        row_bit = lax.axis_index("row") & 1
        laid = jnp.concatenate([lax.select_n(me ^ j, *arrived) for j in range(flips)], axis=1)
        laid = laid.reshape(2, share, span * flips)
        return [lax.dynamic_index_in_dim(laid, row_bit ^ k, 0, keepdims=False) for k in range(2)]
    part = jax.ShapeDtypeStruct((share, span * flips), jnp.float32)
    return pl.pallas_call(
        collect_kernel,
        out_shape=(part, part),
        in_specs=[WHOLE] * flips,
        out_specs=(WHOLE, WHOLE),
        cost_estimate=LIGHT,
        compiler_params=ROOM,
    )(*arrived)


def close_kernel(keep, came, *refs):
    along, (off_diag, diag_block) = refs[:-2], refs[-2:]
    off_diag[...] = keep[...] + came[...]
    total = along[0][...]
    for piece in along[1:]:
        total = total + piece[...]
    diag_block[...] = total


def close(keep, came, along):
    return pl.pallas_call(
        close_kernel,
        out_shape=[jax.ShapeDtypeStruct(x.shape, jnp.float32) for x in (keep, along[0])],
        in_specs=[WHOLE] * (2 + len(along)),
        out_specs=[WHOLE, WHOLE],
        cost_estimate=LIGHT,
        compiler_params=ROOM,
    )(keep, came, *along)


def pick_kernel(masked, swapped, held):
    same = (lax.axis_index("row") & 1) == (lax.axis_index("col") & 1)
    for b in range(held.shape[0]):
        held[b] = jnp.where(same, masked[b], swapped[b])


def pair_rows(masked, swap):
    groups_row = lax.axis_size("row")
    groups_col = lax.axis_size("col")
    cross = [
        (r * groups_col + c, (r ^ 1) * groups_col + (c ^ 1))
        for r in range(groups_row)
        for c in range(groups_col)
    ]
    swapped = lax.ppermute(swap, ("row", "col"), cross)
    held = pl.pallas_call(
        pick_kernel,
        out_shape=jax.ShapeDtypeStruct(masked.shape, jnp.float32),
        in_specs=[WHOLE, WHOLE],
        out_specs=WHOLE,
        cost_estimate=LIGHT,
        compiler_params=ROOM,
    )(masked, swapped)
    ours = [flipped(held, "col", flip) for flip in range(2, groups_col, 2)]
    theirs = [flipped(piece, "col", 1) for piece in ours]
    mates = [flipped(masked, "col", 1), flipped(swapped, "col", 1)]
    return [masked, mates[0], swapped, mates[1]] + ours + theirs


def along_line(mine, own):
    strips = mine[None]
    bit = lax.axis_size("row") // 2
    while bit > 1:
        whole = strips.shape[0] == 1 and mine.shape[1] % LANES == 0
        first = own if whole else strips
        strips = joined(first, flipped(strips, "row", bit), bit)
        bit //= 2
    return strips


def local(inverse_set, presence, factor, dinv):
    groups_row = lax.axis_size("row")
    groups_col = lax.axis_size("col")
    block_rows, _, order, width = factor.shape
    block_cols = inverse_set.shape[3]
    span = width // groups_col
    rows = block_rows * order
    share = order // groups_col

    own = factor.reshape(rows, width)
    blocks = inverse_set.reshape(rows * block_cols, order)
    tall = width // groups_row
    masked, swap, mine = prepare(presence.reshape(-1), blocks, own, span, tall)
    stay = stay_half(own, tall)
    columns = along_line(mine, own).reshape(-1, block_rows, order, span).transpose(1, 0, 2, 3)
    columns = columns.reshape(-1, order, span)
    pieces = pair_rows(masked, swap)

    both, outward = partials(pieces, columns, groups_col)
    got = flipped(both, "row", 1)
    arrived = [outward[0]] + [flipped(outward[f], "col", f) for f in range(1, groups_col)]
    keep, send = collect(arrived)
    came = flipped(send, "row", 1)

    flips = (0,) + tuple(range(groups_row - 2, 0, -2))
    along = finish(both, got, stay, pieces[2], pieces[3], dinv, flips)
    met = [flipped(piece, "row", flip) if flip else piece for flip, piece in zip(flips, along)]
    off_diag, diag_block = close(keep, came, met)
    return (off_diag.reshape(block_rows, 1, share, width), diag_block)


def solution(mesh):
    in_specs = (
        P(None, "row", None, None, "col", None),
        P(None, "row", None, "col"),
        P(None, "row", None, None),
        P("row", "col"),
    )
    out_specs = (P(None, "row", "col", None), P("row", "col"))
    return jax.shard_map(local, mesh=mesh, in_specs=in_specs, out_specs=out_specs, check_vma=False)
```

```python
import functools

import jax
import jax.numpy as jnp
from jax import lax
from jax.experimental import pallas as pl
from jax.experimental.pallas import tpu as pltpu
from jax.sharding import PartitionSpec as P

LANES = 128
WHOLE = pl.BlockSpec(memory_space=pltpu.VMEM)
ROOM = pltpu.CompilerParams(vmem_limit_bytes=16 * 1024 * 1024)
HEAVY = 10**9
LIGHT = pl.CostEstimate(flops=1000, bytes_accessed=1000, transcendentals=0)


def flipped(value, axis, flip):
    return lax.ppermute(value, axis, [(i, i ^ flip) for i in range(lax.axis_size(axis))])


def two_parts(value):
    high = value.astype(jnp.bfloat16)
    return high, (value - high.astype(jnp.float32)).astype(jnp.bfloat16)


def product(left, right, contract):
    left_high, left_low = two_parts(left)
    right_high, right_low = two_parts(right)

    def once(a, b):
        return lax.dot_general(a, b, (contract, ((), ())), preferred_element_type=jnp.float32)

    return once(left_high, right_high) + (once(left_high, right_low) + once(left_low, right_high))


def parity_half(factor, tall, parity):
    even, odd = [
        jnp.concatenate(
            [factor[:, i : i + tall] for i in range(first, factor.shape[1], 2 * tall)], axis=1
        )
        for first in (0, tall)
    ]
    return jnp.where(parity == 1, odd, even)


def masked_block(presence, blocks, block_cols, a, b):
    order = blocks.shape[1]
    weight = presence[a * block_cols + b].astype(jnp.float32)
    return blocks[pl.ds(a * order * block_cols + b, order, stride=block_cols), :] * weight


def prepare_kernel(tall, presence, blocks, factor, swap, mine):
    rows, span = mine.shape
    mine[...] = factor[:, pl.ds(pl.multiple_of(lax.axis_index("col") * span, LANES), span)]
    row_bit = lax.axis_index("row") & 1
    same = row_bit == (lax.axis_index("col") & 1)
    order = swap.shape[2]
    block_cols = blocks.shape[0] // rows
    half = parity_half(factor[...], tall, 1 - row_bit)
    for b in range(swap.shape[0]):
        for a in range(rows // order):
            here = pl.ds(a * order, order)
            part = half[a * order : (a + 1) * order, b * order : (b + 1) * order]
            if b >= block_cols:
                swap[b, here, :] = part
                continue
            block = masked_block(presence, blocks, block_cols, a, b)
            swap[b, here, :] = jnp.where(same, part, block) if part.shape[1] else block


def prepare(presence, blocks, own, span, tall):
    rows, width = own.shape
    block_cols = blocks.shape[0] // rows
    order = blocks.shape[1]
    depth = max(block_cols, width // 2 // order)
    if span % LANES:
        first = lax.axis_index("col") * span
        row_bit = lax.axis_index("row") & 1
        same = row_bit == (lax.axis_index("col") & 1)
        mine = lax.dynamic_slice_in_dim(own, first, span, 1)
        weights = presence.reshape(-1, 1, block_cols, 1).astype(jnp.float32)
        picked = blocks.reshape(-1, order, block_cols, order) * weights
        masked = picked.transpose(2, 0, 1, 3).reshape(block_cols, rows, order)
        half = parity_half(own, tall, 1 - row_bit).reshape(rows, -1, order).transpose(1, 0, 2)
        half = jnp.pad(half, ((0, depth - half.shape[0]), (0, 0), (0, 0)))
        padded = jnp.pad(masked, ((0, depth - block_cols), (0, 0), (0, 0)))
        return jnp.where(same, half, padded), mine
    return pl.pallas_call(
        functools.partial(prepare_kernel, tall),
        out_shape=(
            jax.ShapeDtypeStruct((depth, rows, order), jnp.float32),
            jax.ShapeDtypeStruct((rows, span), jnp.float32),
        ),
        in_specs=[pl.BlockSpec(memory_space=pltpu.SMEM), WHOLE, WHOLE],
        out_specs=(WHOLE, WHOLE),
        cost_estimate=LIGHT,
    )(presence, blocks, own)


def joined_kernel(bit, first, second, out):
    here = jnp.where((lax.axis_index("row") & bit) == 0, 0, 1)
    if first.ndim == 2:
        span = out.shape[3]
        spot = pl.ds(pl.multiple_of(lax.axis_index("col") * span, LANES), span)
        out[0, here] = first[:, spot]
    else:
        out[:, here] = first[...]
    out[:, 1 - here] = second[...]


def joined(first, second, bit):
    count, rows, span = second.shape
    both = pl.pallas_call(
        functools.partial(joined_kernel, bit),
        out_shape=jax.ShapeDtypeStruct((count, 2, rows, span), jnp.float32),
        in_specs=[WHOLE, WHOLE],
        out_specs=WHOLE,
        cost_estimate=pl.CostEstimate(flops=HEAVY, bytes_accessed=1000, transcendentals=0),
        compiler_params=ROOM,
    )(first, second)
    return both.reshape(2 * count, rows, span)


def partials_kernel(count, *refs):
    pieces = refs[: 2 * count]
    columns, both, *outward = refs[2 * count :]
    block_cols, rows, order = pieces[0].shape
    col_index = lax.axis_index("col")
    left, right = [], []
    for t in range(count):
        for b in range(block_cols):
            left.append(jnp.concatenate([pieces[t][b], pieces[count + t][b]], axis=0))
            right.append(columns[b * count + ((col_index >> 1) ^ t)])
    summed = product(jnp.concatenate(left, axis=1), jnp.concatenate(right, axis=0), ((1,), (0,)))
    here = (col_index & 1) * rows
    both[pl.ds(pl.multiple_of(here, 8), rows), :] = summed[:rows]
    both[pl.ds(pl.multiple_of(rows - here, 8), rows), :] = summed[rows:]
    share = order // len(outward)
    for flip, piece in enumerate(outward):
        start = (col_index ^ flip) * share
        for a in range(2 * rows // order):
            picked = both[pl.ds(pl.multiple_of(a * order + start, 8), share), :]
            piece[pl.ds(a * share, share), :] = -picked


def partials(pieces, columns, receivers):
    rows, span = 2 * pieces[0].shape[1], columns.shape[2]
    outward = (jax.ShapeDtypeStruct((rows // receivers, span), jnp.float32),) * receivers
    both, *outward = pl.pallas_call(
        functools.partial(partials_kernel, len(pieces) // 2),
        out_shape=(jax.ShapeDtypeStruct((rows, span), jnp.float32),) + outward,
        in_specs=[WHOLE] * (len(pieces) + 1),
        out_specs=(WHOLE,) * (1 + receivers),
        cost_estimate=LIGHT,
        compiler_params=ROOM,
    )(*pieces, columns)
    return both, outward


def stay_kernel(tall, own, stay):
    stay[...] = parity_half(own[...], tall, lax.axis_index("row") & 1)


def stay_half(own, tall):
    rows, width = own.shape
    return pl.pallas_call(
        functools.partial(stay_kernel, tall),
        out_shape=jax.ShapeDtypeStruct((rows, width // 2), jnp.float32),
        in_specs=[WHOLE],
        out_specs=WHOLE,
        cost_estimate=LIGHT,
        compiler_params=ROOM,
    )(own)


def finish_kernel(flips, both, got, stay, swapped, mate_swapped, dinv, *refs):
    along, update, terms = refs[:-2], refs[-2], refs[-1]
    rows = stay.shape[0]
    row_index = lax.axis_index("row")
    here = (row_index & 1) * rows
    update[...] = both[...] + got[...]
    mine = update[pl.ds(pl.multiple_of(here, 8), rows), :]
    other = update[pl.ds(pl.multiple_of(rows - here, 8), rows), :]
    same = (row_index & 1) == (lax.axis_index("col") & 1)
    depth = stay.shape[1] // swapped.shape[2]
    near = [jnp.where(same, swapped[j], mate_swapped[j]) for j in range(depth)]
    factors = jnp.concatenate([stay[...], jnp.concatenate(near, axis=1)], axis=0)
    terms[...] = product(factors, jnp.concatenate([mine, other], axis=0), ((0,), (0,)))
    tall = dinv.shape[0]
    for flip, piece in zip(flips, along):
        slot = ((row_index ^ flip) >> 1) * tall
        piece[...] = terms[pl.ds(pl.multiple_of(slot, 8), tall), :]
    along[0][...] = along[0][...] + dinv[...]


def finish(both, got, stay, swapped, mate_swapped, dinv, flips):
    rows, half = stay.shape
    span = both.shape[1]
    return pl.pallas_call(
        functools.partial(finish_kernel, flips),
        out_shape=(jax.ShapeDtypeStruct(dinv.shape, jnp.float32),) * len(flips),
        in_specs=[WHOLE] * 6,
        out_specs=(WHOLE,) * len(flips),
        scratch_shapes=[
            pltpu.VMEM((2 * rows, span), jnp.float32),
            pltpu.VMEM((half, span), jnp.float32),
        ],
        cost_estimate=LIGHT,
        compiler_params=ROOM,
    )(both, got, stay, swapped, mate_swapped, dinv)


def collect_kernel(*refs):
    arrived, (_, keep, send) = refs[:-3], refs[-3:]
    share = keep.shape[0]
    span = refs[0].shape[1]
    here = (lax.axis_index("row") & 1) * share
    for flip, piece in enumerate(arrived):
        spot = pl.ds(pl.multiple_of((lax.axis_index("col") ^ flip) * span, LANES), span)
        keep[:, spot] = piece[pl.ds(pl.multiple_of(here, 8), share), :]
        send[:, spot] = piece[pl.ds(pl.multiple_of(share - here, 8), share), :]


def collect(arrived, along):
    flips = len(arrived)
    share, span = arrived[0].shape[0] // 2, arrived[0].shape[1]
    if span % LANES:
        me = lax.axis_index("col")
        row_bit = lax.axis_index("row") & 1
        laid = jnp.concatenate([lax.select_n(me ^ j, *arrived) for j in range(flips)], axis=1)
        laid = laid.reshape(2, share, span * flips)
        return [lax.dynamic_index_in_dim(laid, row_bit ^ k, 0, keepdims=False) for k in range(2)]
    part = jax.ShapeDtypeStruct((share, span * flips), jnp.float32)
    return pl.pallas_call(
        collect_kernel,
        out_shape=(part, part),
        in_specs=[WHOLE] * flips + [pl.BlockSpec(memory_space=pl.ANY)],
        out_specs=(WHOLE, WHOLE),
        cost_estimate=LIGHT,
        compiler_params=ROOM,
    )(*arrived, along)


def close_kernel(keep, came, total, off_diag, diag_block):
    off_diag[...] = keep[...] + came[...]
    diag_block[...] = total[...]


def close(keep, came, total):
    return pl.pallas_call(
        close_kernel,
        out_shape=[jax.ShapeDtypeStruct(x.shape, jnp.float32) for x in (keep, total)],
        in_specs=[WHOLE] * 3,
        out_specs=[WHOLE, WHOLE],
        cost_estimate=LIGHT,
        compiler_params=ROOM,
    )(keep, came, total)


def pick_kernel(presence, blocks, swapped, held):
    same = (lax.axis_index("row") & 1) == (lax.axis_index("col") & 1)
    block_cols, rows, order = held.shape
    for b in range(block_cols):
        for a in range(rows // order):
            here = pl.ds(a * order, order)
            block = masked_block(presence, blocks, block_cols, a, b)
            held[b, here, :] = jnp.where(same, block, swapped[b, here, :])


def pick(presence, blocks, swapped):
    rows, order = swapped.shape[1:]
    return pl.pallas_call(
        pick_kernel,
        out_shape=jax.ShapeDtypeStruct((blocks.shape[0] // rows, rows, order), jnp.float32),
        in_specs=[pl.BlockSpec(memory_space=pltpu.SMEM), WHOLE, WHOLE],
        out_specs=WHOLE,
        cost_estimate=LIGHT,
        compiler_params=ROOM,
    )(presence, blocks, swapped)


def crossed(swap):
    groups_row = lax.axis_size("row")
    groups_col = lax.axis_size("col")
    cross = [
        (r * groups_col + c, (r ^ 1) * groups_col + (c ^ 1))
        for r in range(groups_row)
        for c in range(groups_col)
    ]
    return lax.ppermute(swap, ("row", "col"), cross)


def pair_rows(held):
    held = [held] + [flipped(held, "col", flip) for flip in range(2, lax.axis_size("col"), 2)]
    return held + [flipped(piece, "col", 1) for piece in held]


def along_line(mine, own):
    strips = mine[None]
    bit = lax.axis_size("row") // 2
    while bit > 1:
        whole = strips.shape[0] == 1 and mine.shape[1] % LANES == 0
        first = own if whole else strips
        strips = joined(first, flipped(strips, "row", bit), bit)
        bit //= 2
    return strips


def local(inverse_set, presence, factor, dinv):
    groups_row = lax.axis_size("row")
    groups_col = lax.axis_size("col")
    block_rows, _, order, width = factor.shape
    block_cols = inverse_set.shape[3]
    span = width // groups_col
    rows = block_rows * order
    share = order // groups_col

    own = factor.reshape(rows, width)
    blocks = inverse_set.reshape(rows * block_cols, order)
    marks = presence.reshape(-1)
    tall = width // groups_row
    swap, mine = prepare(marks, blocks, own, span, tall)
    swapped = crossed(swap)
    stay = stay_half(own, tall)
    columns = along_line(mine, own).reshape(-1, block_rows, order, span).transpose(1, 0, 2, 3)
    columns = columns.reshape(-1, order, span)
    pieces = pair_rows(pick(marks, blocks, swapped))
    mate_swapped = flipped(swapped, "col", 1)

    both, outward = partials(pieces, columns, groups_col)
    got = flipped(both, "row", 1)
    arrived = [outward[0]] + [flipped(outward[f], "col", f) for f in range(1, groups_col)]
    flips = (0,) + tuple(range(groups_row - 2, 0, -2))
    along = finish(both, got, stay, swapped, mate_swapped, dinv, flips)
    keep, send = collect(arrived, along[0])
    came = flipped(send, "row", 1)
    met = [flipped(piece, "row", flip) if flip else piece for flip, piece in zip(flips, along)]
    off_diag, diag_block = close(keep, came, sum(met[1:], met[0]))
    return (off_diag.reshape(block_rows, 1, share, width), diag_block)


def solution(mesh):
    in_specs = (
        P(None, "row", None, None, "col", None),
        P(None, "row", None, "col"),
        P(None, "row", None, None),
        P("row", "col"),
    )
    out_specs = (P(None, "row", "col", None), P("row", "col"))
    return jax.shard_map(local, mesh=mesh, in_specs=in_specs, out_specs=out_specs, check_vma=False)
```

```python
import functools

import jax
import jax.numpy as jnp
from jax import lax
from jax.experimental import pallas as pl
from jax.experimental.pallas import tpu as pltpu
from jax.sharding import PartitionSpec as P

LANES = 128
WHOLE = pl.BlockSpec(memory_space=pltpu.VMEM)
ROOM = pltpu.CompilerParams(vmem_limit_bytes=16 * 1024 * 1024)
HEAVY = 10**9
LIGHT = pl.CostEstimate(flops=1000, bytes_accessed=1000, transcendentals=0)


def flipped(value, axis, flip):
    return lax.ppermute(value, axis, [(i, i ^ flip) for i in range(lax.axis_size(axis))])


def two_parts(value):
    high = value.astype(jnp.bfloat16)
    return high, (value - high.astype(jnp.float32)).astype(jnp.bfloat16)


def product(left, right, contract):
    left_high, left_low = two_parts(left)
    right_high, right_low = two_parts(right)

    def once(a, b):
        return lax.dot_general(a, b, (contract, ((), ())), preferred_element_type=jnp.float32)

    return once(left_high, right_high) + (once(left_high, right_low) + once(left_low, right_high))


def parity_half(factor, tall, parity):
    even, odd = [
        jnp.concatenate(
            [factor[:, i : i + tall] for i in range(first, factor.shape[1], 2 * tall)], axis=1
        )
        for first in (0, tall)
    ]
    return jnp.where(parity == 1, odd, even)


def masked_block(presence, blocks, block_cols, a, b):
    order = blocks.shape[1]
    at = a * block_cols + b
    weight = presence[:, at : at + 1].astype(jnp.float32)
    return blocks[pl.ds(a * order * block_cols + b, order, stride=block_cols), :] * weight


def prepare_kernel(tall, presence, blocks, factor, swap, mine):
    rows, span = mine.shape
    mine[...] = factor[:, pl.ds(pl.multiple_of(lax.axis_index("col") * span, LANES), span)]
    row_bit = lax.axis_index("row") & 1
    same = row_bit == (lax.axis_index("col") & 1)
    order = swap.shape[2]
    block_cols = blocks.shape[0] // rows
    half = parity_half(factor[...], tall, 1 - row_bit)
    for b in range(swap.shape[0]):
        for a in range(rows // order):
            here = pl.ds(a * order, order)
            part = half[a * order : (a + 1) * order, b * order : (b + 1) * order]
            if b >= block_cols:
                swap[b, here, :] = part
                continue
            block = masked_block(presence, blocks, block_cols, a, b)
            swap[b, here, :] = jnp.where(same, part, block) if part.shape[1] else block


def prepare(presence, blocks, own, span, tall):
    rows, width = own.shape
    block_cols = blocks.shape[0] // rows
    order = blocks.shape[1]
    depth = max(block_cols, width // 2 // order)
    if span % LANES:
        first = lax.axis_index("col") * span
        row_bit = lax.axis_index("row") & 1
        same = row_bit == (lax.axis_index("col") & 1)
        mine = lax.dynamic_slice_in_dim(own, first, span, 1)
        weights = presence.reshape(-1, 1, block_cols, 1).astype(jnp.float32)
        picked = blocks.reshape(-1, order, block_cols, order) * weights
        masked = picked.transpose(2, 0, 1, 3).reshape(block_cols, rows, order)
        half = parity_half(own, tall, 1 - row_bit).reshape(rows, -1, order).transpose(1, 0, 2)
        half = jnp.pad(half, ((0, depth - half.shape[0]), (0, 0), (0, 0)))
        padded = jnp.pad(masked, ((0, depth - block_cols), (0, 0), (0, 0)))
        return jnp.where(same, half, padded), mine
    return pl.pallas_call(
        functools.partial(prepare_kernel, tall),
        out_shape=(
            jax.ShapeDtypeStruct((depth, rows, order), jnp.float32),
            jax.ShapeDtypeStruct((rows, span), jnp.float32),
        ),
        in_specs=[WHOLE] * 3,
        out_specs=(WHOLE, WHOLE),
        cost_estimate=LIGHT,
    )(presence, blocks, own)


def joined_kernel(bit, first, second, out):
    here = jnp.where((lax.axis_index("row") & bit) == 0, 0, 1)
    if first.ndim == 2:
        span = out.shape[3]
        spot = pl.ds(pl.multiple_of(lax.axis_index("col") * span, LANES), span)
        out[0, here] = first[:, spot]
    else:
        out[:, here] = first[...]
    out[:, 1 - here] = second[...]


def joined(first, second, bit):
    count, rows, span = second.shape
    both = pl.pallas_call(
        functools.partial(joined_kernel, bit),
        out_shape=jax.ShapeDtypeStruct((count, 2, rows, span), jnp.float32),
        in_specs=[WHOLE, WHOLE],
        out_specs=WHOLE,
        cost_estimate=pl.CostEstimate(flops=HEAVY, bytes_accessed=1000, transcendentals=0),
        compiler_params=ROOM,
    )(first, second)
    return both.reshape(2 * count, rows, span)


def partials_kernel(count, *refs):
    pieces = refs[: 2 * count]
    columns, both, *outward = refs[2 * count :]
    block_cols, rows, order = pieces[0].shape
    col_index = lax.axis_index("col")
    left, right = [], []
    for t in range(count):
        for b in range(block_cols):
            left.append(jnp.concatenate([pieces[t][b], pieces[count + t][b]], axis=0))
            right.append(columns[b * count + ((col_index >> 1) ^ t)])
    summed = product(jnp.concatenate(left, axis=1), jnp.concatenate(right, axis=0), ((1,), (0,)))
    here = (col_index & 1) * rows
    both[pl.ds(pl.multiple_of(here, 8), rows), :] = summed[:rows]
    both[pl.ds(pl.multiple_of(rows - here, 8), rows), :] = summed[rows:]
    share = order // len(outward)
    for flip, piece in enumerate(outward):
        start = (col_index ^ flip) * share
        for a in range(2 * rows // order):
            picked = both[pl.ds(pl.multiple_of(a * order + start, 8), share), :]
            piece[pl.ds(a * share, share), :] = -picked


def partials(pieces, columns, receivers):
    rows, span = 2 * pieces[0].shape[1], columns.shape[2]
    outward = (jax.ShapeDtypeStruct((rows // receivers, span), jnp.float32),) * receivers
    both, *outward = pl.pallas_call(
        functools.partial(partials_kernel, len(pieces) // 2),
        out_shape=(jax.ShapeDtypeStruct((rows, span), jnp.float32),) + outward,
        in_specs=[WHOLE] * (len(pieces) + 1),
        out_specs=(WHOLE,) * (1 + receivers),
        cost_estimate=LIGHT,
        compiler_params=ROOM,
    )(*pieces, columns)
    return both, outward


def stay_kernel(tall, own, stay):
    stay[...] = parity_half(own[...], tall, lax.axis_index("row") & 1)


def stay_half(own, tall):
    rows, width = own.shape
    return pl.pallas_call(
        functools.partial(stay_kernel, tall),
        out_shape=jax.ShapeDtypeStruct((rows, width // 2), jnp.float32),
        in_specs=[WHOLE],
        out_specs=WHOLE,
        cost_estimate=LIGHT,
        compiler_params=ROOM,
    )(own)


def finish_kernel(flips, both, got, stay, swapped, mate_swapped, dinv, *refs):
    along, update, terms = refs[:-2], refs[-2], refs[-1]
    rows = stay.shape[0]
    row_index = lax.axis_index("row")
    here = (row_index & 1) * rows
    update[...] = both[...] + got[...]
    mine = update[pl.ds(pl.multiple_of(here, 8), rows), :]
    other = update[pl.ds(pl.multiple_of(rows - here, 8), rows), :]
    same = (row_index & 1) == (lax.axis_index("col") & 1)
    depth = stay.shape[1] // swapped.shape[2]
    near = [jnp.where(same, swapped[j], mate_swapped[j]) for j in range(depth)]
    factors = jnp.concatenate([stay[...], jnp.concatenate(near, axis=1)], axis=0)
    terms[...] = product(factors, jnp.concatenate([mine, other], axis=0), ((0,), (0,)))
    tall = dinv.shape[0]
    for flip, piece in zip(flips, along):
        slot = ((row_index ^ flip) >> 1) * tall
        piece[...] = terms[pl.ds(pl.multiple_of(slot, 8), tall), :]
    along[0][...] = along[0][...] + dinv[...]


def finish(both, got, stay, swapped, mate_swapped, dinv, flips):
    rows, half = stay.shape
    span = both.shape[1]
    return pl.pallas_call(
        functools.partial(finish_kernel, flips),
        out_shape=(jax.ShapeDtypeStruct(dinv.shape, jnp.float32),) * len(flips),
        in_specs=[WHOLE] * 6,
        out_specs=(WHOLE,) * len(flips),
        scratch_shapes=[
            pltpu.VMEM((2 * rows, span), jnp.float32),
            pltpu.VMEM((half, span), jnp.float32),
        ],
        cost_estimate=LIGHT,
        compiler_params=ROOM,
    )(both, got, stay, swapped, mate_swapped, dinv)


def collect_kernel(*refs):
    arrived, (_, keep, send) = refs[:-3], refs[-3:]
    share = keep.shape[0]
    span = refs[0].shape[1]
    here = (lax.axis_index("row") & 1) * share
    for flip, piece in enumerate(arrived):
        spot = pl.ds(pl.multiple_of((lax.axis_index("col") ^ flip) * span, LANES), span)
        keep[:, spot] = piece[pl.ds(pl.multiple_of(here, 8), share), :]
        send[:, spot] = piece[pl.ds(pl.multiple_of(share - here, 8), share), :]


def collect(arrived, along):
    flips = len(arrived)
    share, span = arrived[0].shape[0] // 2, arrived[0].shape[1]
    if span % LANES:
        me = lax.axis_index("col")
        row_bit = lax.axis_index("row") & 1
        laid = jnp.concatenate([lax.select_n(me ^ j, *arrived) for j in range(flips)], axis=1)
        laid = laid.reshape(2, share, span * flips)
        return [lax.dynamic_index_in_dim(laid, row_bit ^ k, 0, keepdims=False) for k in range(2)]
    part = jax.ShapeDtypeStruct((share, span * flips), jnp.float32)
    return pl.pallas_call(
        collect_kernel,
        out_shape=(part, part),
        in_specs=[WHOLE] * flips + [pl.BlockSpec(memory_space=pl.ANY)],
        out_specs=(WHOLE, WHOLE),
        cost_estimate=LIGHT,
        compiler_params=ROOM,
    )(*arrived, along)


def close_kernel(keep, came, *refs):
    met, (off_diag, diag_block) = refs[:-2], refs[-2:]
    off_diag[...] = keep[...] + came[...]
    diag_block[...] = sum([piece[...] for piece in met[1:]], met[0][...])


def close(keep, came, met):
    return pl.pallas_call(
        close_kernel,
        out_shape=[jax.ShapeDtypeStruct(x.shape, jnp.float32) for x in (keep, met[0])],
        in_specs=[WHOLE] * (2 + len(met)),
        out_specs=[WHOLE, WHOLE],
        cost_estimate=LIGHT,
        compiler_params=ROOM,
    )(keep, came, *met)


def pick_kernel(presence, blocks, swapped, held):
    same = (lax.axis_index("row") & 1) == (lax.axis_index("col") & 1)
    block_cols, rows, order = held.shape
    for b in range(block_cols):
        for a in range(rows // order):
            here = pl.ds(a * order, order)
            block = masked_block(presence, blocks, block_cols, a, b)
            held[b, here, :] = jnp.where(same, block, swapped[b, here, :])


def pick(presence, blocks, swapped):
    rows, order = swapped.shape[1:]
    return pl.pallas_call(
        pick_kernel,
        out_shape=jax.ShapeDtypeStruct((blocks.shape[0] // rows, rows, order), jnp.float32),
        in_specs=[WHOLE] * 3,
        out_specs=WHOLE,
        cost_estimate=LIGHT,
        compiler_params=ROOM,
    )(presence, blocks, swapped)


def crossed(swap):
    groups_row = lax.axis_size("row")
    groups_col = lax.axis_size("col")
    cross = [
        (r * groups_col + c, (r ^ 1) * groups_col + (c ^ 1))
        for r in range(groups_row)
        for c in range(groups_col)
    ]
    return lax.ppermute(swap, ("row", "col"), cross)


def pair_rows(held):
    held = [held] + [flipped(held, "col", flip) for flip in range(2, lax.axis_size("col"), 2)]
    return held + [flipped(piece, "col", 1) for piece in held]


def along_line(mine, own):
    strips = mine[None]
    bit = lax.axis_size("row") // 2
    while bit > 1:
        whole = strips.shape[0] == 1 and mine.shape[1] % LANES == 0
        first = own if whole else strips
        strips = joined(first, flipped(strips, "row", bit), bit)
        bit //= 2
    return strips


def local(inverse_set, presence, factor, dinv):
    groups_row = lax.axis_size("row")
    groups_col = lax.axis_size("col")
    block_rows, _, order, width = factor.shape
    block_cols = inverse_set.shape[3]
    span = width // groups_col
    rows = block_rows * order
    share = order // groups_col

    own = factor.reshape(rows, width)
    blocks = inverse_set.reshape(rows * block_cols, order)
    marks = presence.reshape(1, -1)
    tall = width // groups_row
    swap, mine = prepare(marks, blocks, own, span, tall)
    swapped = crossed(swap)
    stay = stay_half(own, tall)
    columns = along_line(mine, own).reshape(-1, block_rows, order, span).transpose(1, 0, 2, 3)
    columns = columns.reshape(-1, order, span)
    pieces = pair_rows(pick(marks, blocks, swapped))
    mate_swapped = flipped(swapped, "col", 1)

    both, outward = partials(pieces, columns, groups_col)
    got = flipped(both, "row", 1)
    arrived = [outward[0]] + [flipped(outward[f], "col", f) for f in range(1, groups_col)]
    flips = (0,) + tuple(range(groups_row - 2, 0, -2))
    along = finish(both, got, stay, swapped, mate_swapped, dinv, flips)
    keep, send = collect(arrived, along[0])
    came = flipped(send, "row", 1)
    met = [flipped(piece, "row", flip) if flip else piece for flip, piece in zip(flips, along)]
    off_diag, diag_block = close(keep, came, met)
    return (off_diag.reshape(block_rows, 1, share, width), diag_block)


def solution(mesh):
    in_specs = (
        P(None, "row", None, None, "col", None),
        P(None, "row", None, "col"),
        P(None, "row", None, None),
        P("row", "col"),
    )
    out_specs = (P(None, "row", "col", None), P("row", "col"))
    return jax.shard_map(local, mesh=mesh, in_specs=in_specs, out_specs=out_specs, check_vma=False)
```

```python
import functools

import jax
import jax.numpy as jnp
from jax import lax
from jax.experimental import pallas as pl
from jax.experimental.pallas import tpu as pltpu
from jax.sharding import PartitionSpec as P

LANES = 128
WHOLE = pl.BlockSpec(memory_space=pltpu.VMEM)
ROOM = pltpu.CompilerParams(vmem_limit_bytes=16 * 1024 * 1024)
HEAVY = 10**9
LIGHT = pl.CostEstimate(flops=1000, bytes_accessed=1000, transcendentals=0)


def flipped(value, axis, flip):
    return lax.ppermute(value, axis, [(i, i ^ flip) for i in range(lax.axis_size(axis))])


def two_parts(value):
    high = value.astype(jnp.bfloat16)
    return high, (value - high.astype(jnp.float32)).astype(jnp.bfloat16)


def product(left, right, contract):
    left_high, left_low = two_parts(left)
    right_high, right_low = two_parts(right)

    def once(a, b):
        return lax.dot_general(a, b, (contract, ((), ())), preferred_element_type=jnp.float32)

    return once(left_high, right_high) + (once(left_high, right_low) + once(left_low, right_high))


def parity_half(factor, tall, parity):
    even, odd = [
        jnp.concatenate(
            [factor[:, i : i + tall] for i in range(first, factor.shape[1], 2 * tall)], axis=1
        )
        for first in (0, tall)
    ]
    return jnp.where(parity == 1, odd, even)


def masked_block(presence, blocks, block_cols, a, b):
    order = blocks.shape[1]
    at = a * block_cols + b
    weight = presence[:, at : at + 1].astype(jnp.float32)
    return blocks[pl.ds(a * order * block_cols + b, order, stride=block_cols), :] * weight


def prepare_kernel(tall, presence, blocks, factor, swap, mine):
    rows, span = mine.shape
    mine[...] = factor[:, pl.ds(pl.multiple_of(lax.axis_index("col") * span, LANES), span)]
    row_bit = lax.axis_index("row") & 1
    same = row_bit == (lax.axis_index("col") & 1)
    order = swap.shape[2]
    block_cols = blocks.shape[0] // rows
    half = parity_half(factor[...], tall, 1 - row_bit)
    for b in range(swap.shape[0]):
        for a in range(rows // order):
            here = pl.ds(a * order, order)
            part = half[a * order : (a + 1) * order, b * order : (b + 1) * order]
            if b >= block_cols:
                swap[b, here, :] = part
                continue
            block = masked_block(presence, blocks, block_cols, a, b)
            swap[b, here, :] = jnp.where(same, part, block) if part.shape[1] else block


def prepare(presence, blocks, own, span, tall):
    rows, width = own.shape
    block_cols = blocks.shape[0] // rows
    order = blocks.shape[1]
    depth = max(block_cols, width // 2 // order)
    if span % LANES:
        first = lax.axis_index("col") * span
        row_bit = lax.axis_index("row") & 1
        same = row_bit == (lax.axis_index("col") & 1)
        mine = lax.dynamic_slice_in_dim(own, first, span, 1)
        weights = presence.reshape(-1, 1, block_cols, 1).astype(jnp.float32)
        picked = blocks.reshape(-1, order, block_cols, order) * weights
        masked = picked.transpose(2, 0, 1, 3).reshape(block_cols, rows, order)
        half = parity_half(own, tall, 1 - row_bit).reshape(rows, -1, order).transpose(1, 0, 2)
        half = jnp.pad(half, ((0, depth - half.shape[0]), (0, 0), (0, 0)))
        padded = jnp.pad(masked, ((0, depth - block_cols), (0, 0), (0, 0)))
        return jnp.where(same, half, padded), mine
    return pl.pallas_call(
        functools.partial(prepare_kernel, tall),
        out_shape=(
            jax.ShapeDtypeStruct((depth, rows, order), jnp.float32),
            jax.ShapeDtypeStruct((rows, span), jnp.float32),
        ),
        in_specs=[WHOLE] * 3,
        out_specs=(WHOLE, WHOLE),
        cost_estimate=LIGHT,
    )(presence, blocks, own)


def joined_kernel(bit, first, second, out):
    here = jnp.where((lax.axis_index("row") & bit) == 0, 0, 1)
    if first.ndim == 2:
        span = out.shape[3]
        spot = pl.ds(pl.multiple_of(lax.axis_index("col") * span, LANES), span)
        out[0, here] = first[:, spot]
    else:
        out[:, here] = first[...]
    out[:, 1 - here] = second[...]


def joined(first, second, bit):
    count, rows, span = second.shape
    both = pl.pallas_call(
        functools.partial(joined_kernel, bit),
        out_shape=jax.ShapeDtypeStruct((count, 2, rows, span), jnp.float32),
        in_specs=[WHOLE, WHOLE],
        out_specs=WHOLE,
        cost_estimate=pl.CostEstimate(flops=HEAVY, bytes_accessed=1000, transcendentals=0),
        compiler_params=ROOM,
    )(first, second)
    return both.reshape(2 * count, rows, span)


def partials_kernel(count, *refs):
    pieces = refs[: 2 * count]
    columns, both, *outward = refs[2 * count :]
    block_cols, rows, order = pieces[0].shape
    col_index = lax.axis_index("col")
    left, right = [], []
    for t in range(count):
        for b in range(block_cols):
            left.append(jnp.concatenate([pieces[t][b], pieces[count + t][b]], axis=0))
            right.append(columns[b * count + ((col_index >> 1) ^ t)])
    summed = product(jnp.concatenate(left, axis=1), jnp.concatenate(right, axis=0), ((1,), (0,)))
    here = (col_index & 1) * rows
    both[pl.ds(pl.multiple_of(here, 8), rows), :] = summed[:rows]
    both[pl.ds(pl.multiple_of(rows - here, 8), rows), :] = summed[rows:]
    share = order // len(outward)
    for flip, piece in enumerate(outward):
        start = (col_index ^ flip) * share
        for a in range(2 * rows // order):
            picked = both[pl.ds(pl.multiple_of(a * order + start, 8), share), :]
            piece[pl.ds(a * share, share), :] = -picked


def partials(pieces, columns, receivers):
    rows, span = 2 * pieces[0].shape[1], columns.shape[2]
    outward = (jax.ShapeDtypeStruct((rows // receivers, span), jnp.float32),) * receivers
    both, *outward = pl.pallas_call(
        functools.partial(partials_kernel, len(pieces) // 2),
        out_shape=(jax.ShapeDtypeStruct((rows, span), jnp.float32),) + outward,
        in_specs=[WHOLE] * (len(pieces) + 1),
        out_specs=(WHOLE,) * (1 + receivers),
        cost_estimate=LIGHT,
        compiler_params=ROOM,
    )(*pieces, columns)
    return both, outward


def stay_kernel(tall, own, stay):
    stay[...] = parity_half(own[...], tall, lax.axis_index("row") & 1)


def stay_half(own, tall):
    rows, width = own.shape
    return pl.pallas_call(
        functools.partial(stay_kernel, tall),
        out_shape=jax.ShapeDtypeStruct((rows, width // 2), jnp.float32),
        in_specs=[WHOLE],
        out_specs=WHOLE,
        cost_estimate=LIGHT,
        compiler_params=ROOM,
    )(own)


def finish_kernel(flips, both, got, stay, swapped, mate_swapped, dinv, *refs):
    along, update, terms = refs[:-2], refs[-2], refs[-1]
    rows = stay.shape[0]
    row_index = lax.axis_index("row")
    here = (row_index & 1) * rows
    update[...] = both[...] + got[...]
    mine = update[pl.ds(pl.multiple_of(here, 8), rows), :]
    other = update[pl.ds(pl.multiple_of(rows - here, 8), rows), :]
    same = (row_index & 1) == (lax.axis_index("col") & 1)
    depth = stay.shape[1] // swapped.shape[2]
    near = [jnp.where(same, swapped[j], mate_swapped[j]) for j in range(depth)]
    factors = jnp.concatenate([stay[...], jnp.concatenate(near, axis=1)], axis=0)
    terms[...] = product(factors, jnp.concatenate([mine, other], axis=0), ((0,), (0,)))
    tall = dinv.shape[0]
    for flip, piece in zip(flips, along):
        slot = ((row_index ^ flip) >> 1) * tall
        piece[...] = terms[pl.ds(pl.multiple_of(slot, 8), tall), :]
    along[0][...] = along[0][...] + dinv[...]


def finish(both, got, stay, swapped, mate_swapped, dinv, flips):
    rows, half = stay.shape
    span = both.shape[1]
    return pl.pallas_call(
        functools.partial(finish_kernel, flips),
        out_shape=(jax.ShapeDtypeStruct(dinv.shape, jnp.float32),) * len(flips),
        in_specs=[WHOLE] * 6,
        out_specs=(WHOLE,) * len(flips),
        scratch_shapes=[
            pltpu.VMEM((2 * rows, span), jnp.float32),
            pltpu.VMEM((half, span), jnp.float32),
        ],
        cost_estimate=LIGHT,
        compiler_params=ROOM,
    )(both, got, stay, swapped, mate_swapped, dinv)


def collect_kernel(*refs):
    arrived, (_, keep, send) = refs[:-3], refs[-3:]
    share = keep.shape[0]
    span = refs[0].shape[1]
    here = (lax.axis_index("row") & 1) * share
    for flip, piece in enumerate(arrived):
        spot = pl.ds(pl.multiple_of((lax.axis_index("col") ^ flip) * span, LANES), span)
        keep[:, spot] = piece[pl.ds(pl.multiple_of(here, 8), share), :]
        send[:, spot] = piece[pl.ds(pl.multiple_of(share - here, 8), share), :]


def collect(arrived, along):
    flips = len(arrived)
    share, span = arrived[0].shape[0] // 2, arrived[0].shape[1]
    if span % LANES:
        me = lax.axis_index("col")
        row_bit = lax.axis_index("row") & 1
        laid = jnp.concatenate([lax.select_n(me ^ j, *arrived) for j in range(flips)], axis=1)
        laid = laid.reshape(2, share, span * flips)
        return [lax.dynamic_index_in_dim(laid, row_bit ^ k, 0, keepdims=False) for k in range(2)]
    part = jax.ShapeDtypeStruct((share, span * flips), jnp.float32)
    return pl.pallas_call(
        collect_kernel,
        out_shape=(part, part),
        in_specs=[WHOLE] * flips + [pl.BlockSpec(memory_space=pl.ANY)],
        out_specs=(WHOLE, WHOLE),
        cost_estimate=LIGHT,
        compiler_params=ROOM,
    )(*arrived, along)


def close_kernel(keep, came, total, off_diag, diag_block):
    off_diag[...] = keep[...] + came[...]
    diag_block[...] = total[...]


def close(keep, came, total):
    return pl.pallas_call(
        close_kernel,
        out_shape=[jax.ShapeDtypeStruct(x.shape, jnp.float32) for x in (keep, total)],
        in_specs=[WHOLE] * 3,
        out_specs=[WHOLE, WHOLE],
        cost_estimate=LIGHT,
        compiler_params=ROOM,
    )(keep, came, total)


def pick_kernel(presence, blocks, swapped, held):
    same = (lax.axis_index("row") & 1) == (lax.axis_index("col") & 1)
    block_cols, rows, order = held.shape
    for b in range(block_cols):
        for a in range(rows // order):
            here = pl.ds(a * order, order)
            block = masked_block(presence, blocks, block_cols, a, b)
            held[b, here, :] = jnp.where(same, block, swapped[b, here, :])


def pick(presence, blocks, swapped):
    rows, order = swapped.shape[1:]
    return pl.pallas_call(
        pick_kernel,
        out_shape=jax.ShapeDtypeStruct((blocks.shape[0] // rows, rows, order), jnp.float32),
        in_specs=[WHOLE] * 3,
        out_specs=WHOLE,
        cost_estimate=LIGHT,
        compiler_params=ROOM,
    )(presence, blocks, swapped)


def crossed(swap):
    groups_row = lax.axis_size("row")
    groups_col = lax.axis_size("col")
    cross = [
        (r * groups_col + c, (r ^ 1) * groups_col + (c ^ 1))
        for r in range(groups_row)
        for c in range(groups_col)
    ]
    return lax.ppermute(swap, ("row", "col"), cross)


def pair_rows(held):
    held = [held] + [flipped(held, "col", flip) for flip in range(2, lax.axis_size("col"), 2)]
    return held + [flipped(piece, "col", 1) for piece in held]


def along_line(mine, own):
    strips = mine[None]
    bit = lax.axis_size("row") // 2
    while bit > 1:
        whole = strips.shape[0] == 1 and mine.shape[1] % LANES == 0
        first = own if whole else strips
        strips = joined(first, flipped(strips, "row", bit), bit)
        bit //= 2
    return strips


def local(inverse_set, presence, factor, dinv):
    groups_row = lax.axis_size("row")
    groups_col = lax.axis_size("col")
    block_rows, _, order, width = factor.shape
    block_cols = inverse_set.shape[3]
    span = width // groups_col
    rows = block_rows * order
    share = order // groups_col

    own = factor.reshape(rows, width)
    blocks = inverse_set.reshape(rows * block_cols, order)
    marks = presence.reshape(1, -1)
    tall = width // groups_row
    swap, mine = prepare(marks, blocks, own, span, tall)
    swapped = crossed(swap)
    stay = stay_half(own, tall)
    columns = along_line(mine, own).reshape(-1, block_rows, order, span).transpose(1, 0, 2, 3)
    columns = columns.reshape(-1, order, span)
    pieces = pair_rows(pick(marks, blocks, swapped))
    mate_swapped = flipped(swapped, "col", 1)

    both, outward = partials(pieces, columns, groups_col)
    got = flipped(both, "row", 1)
    arrived = [outward[0]] + [flipped(outward[f], "col", f) for f in range(1, groups_col)]
    flips = (0,) + tuple(range(groups_row - 2, 0, -2))
    along = finish(both, got, stay, swapped, mate_swapped, dinv, flips)
    keep, send = collect(arrived, along[0])
    came = flipped(send, "row", 1)
    met = [flipped(piece, "row", flip) if flip else piece for flip, piece in zip(flips, along)]
    off_diag, diag_block = close(keep, came, sum(met[1:], met[0]))
    return (off_diag.reshape(block_rows, 1, share, width), diag_block)


def solution(mesh):
    in_specs = (
        P(None, "row", None, None, "col", None),
        P(None, "row", None, "col"),
        P(None, "row", None, None),
        P("row", "col"),
    )
    out_specs = (P(None, "row", "col", None), P("row", "col"))
    return jax.shard_map(local, mesh=mesh, in_specs=in_specs, out_specs=out_specs, check_vma=False)
```

```python
import functools

import jax
import jax.numpy as jnp
from jax import lax
from jax.experimental import pallas as pl
from jax.experimental.pallas import tpu as pltpu
from jax.sharding import PartitionSpec as P

LANES = 128
WHOLE = pl.BlockSpec(memory_space=pltpu.VMEM)
ROOM = pltpu.CompilerParams(vmem_limit_bytes=16 * 1024 * 1024)
HEAVY = 10**9
LIGHT = pl.CostEstimate(flops=1000, bytes_accessed=1000, transcendentals=0)


def flipped(value, axis, flip):
    return lax.ppermute(value, axis, [(i, i ^ flip) for i in range(lax.axis_size(axis))])


def two_parts(value):
    high = value.astype(jnp.bfloat16)
    return high, (value - high.astype(jnp.float32)).astype(jnp.bfloat16)


def product(left, right, contract):
    left_high, left_low = two_parts(left)
    right_high, right_low = two_parts(right)

    def once(a, b):
        return lax.dot_general(a, b, (contract, ((), ())), preferred_element_type=jnp.float32)

    return once(left_high, right_high) + (once(left_high, right_low) + once(left_low, right_high))


def parity_half(factor, tall, parity):
    even, odd = [
        jnp.concatenate(
            [factor[:, i : i + tall] for i in range(first, factor.shape[1], 2 * tall)], axis=1
        )
        for first in (0, tall)
    ]
    return jnp.where(parity == 1, odd, even)


def masked_block(presence, blocks, block_cols, a, b):
    order = blocks.shape[1]
    at = a * block_cols + b
    weight = presence[:, at : at + 1].astype(jnp.float32)
    return blocks[pl.ds(a * order * block_cols + b, order, stride=block_cols), :] * weight


def prepare_kernel(tall, presence, blocks, factor, mine, *swaps):
    rows, span = mine.shape
    mine[...] = factor[:, pl.ds(pl.multiple_of(lax.axis_index("col") * span, LANES), span)]
    row_bit = lax.axis_index("row") & 1
    same = row_bit == (lax.axis_index("col") & 1)
    order = blocks.shape[1]
    block_cols = blocks.shape[0] // rows
    half = parity_half(factor[...], tall, 1 - row_bit)
    for b, swap in enumerate(swaps):
        for a in range(rows // order):
            here = pl.ds(a * order, order)
            part = half[a * order : (a + 1) * order, b * order : (b + 1) * order]
            if b >= block_cols:
                swap[here, :] = part
                continue
            block = masked_block(presence, blocks, block_cols, a, b)
            swap[here, :] = jnp.where(same, part, block) if part.shape[1] else block


def prepare(presence, blocks, own, span, tall):
    rows, width = own.shape
    block_cols = blocks.shape[0] // rows
    order = blocks.shape[1]
    depth = max(block_cols, width // 2 // order)
    if span % LANES:
        first = lax.axis_index("col") * span
        row_bit = lax.axis_index("row") & 1
        same = row_bit == (lax.axis_index("col") & 1)
        mine = lax.dynamic_slice_in_dim(own, first, span, 1)
        weights = presence.reshape(-1, 1, block_cols, 1).astype(jnp.float32)
        picked = blocks.reshape(-1, order, block_cols, order) * weights
        masked = picked.transpose(2, 0, 1, 3).reshape(block_cols, rows, order)
        half = parity_half(own, tall, 1 - row_bit).reshape(rows, -1, order).transpose(1, 0, 2)
        half = jnp.pad(half, ((0, depth - half.shape[0]), (0, 0), (0, 0)))
        padded = jnp.pad(masked, ((0, depth - block_cols), (0, 0), (0, 0)))
        return mine, list(jnp.where(same, half, padded))
    mine, *swaps = pl.pallas_call(
        functools.partial(prepare_kernel, tall),
        out_shape=(jax.ShapeDtypeStruct((rows, span), jnp.float32),)
        + (jax.ShapeDtypeStruct((rows, order), jnp.float32),) * depth,
        in_specs=[WHOLE] * 3,
        out_specs=(WHOLE,) * (1 + depth),
        cost_estimate=LIGHT,
    )(presence, blocks, own)
    return mine, swaps


def ordered_kernel(flips, *refs):
    columns = refs[-1]
    _, order, _ = columns.shape
    for flip, strip in zip(flips, refs[:-1]):
        at = (lax.axis_index("row") ^ flip) >> 1
        for a in range(strip.shape[0] // order):
            columns[a * len(flips) + at] = strip[pl.ds(a * order, order), :]


def ordered(strips, flips, order):
    rows, span = strips[0].shape
    return pl.pallas_call(
        functools.partial(ordered_kernel, flips),
        out_shape=jax.ShapeDtypeStruct((rows // order * len(strips), order, span), jnp.float32),
        in_specs=[WHOLE] * len(strips),
        out_specs=WHOLE,
        cost_estimate=pl.CostEstimate(flops=HEAVY, bytes_accessed=1000, transcendentals=0),
        compiler_params=ROOM,
    )(*strips)


def partials_kernel(count, *refs):
    held, mate = refs[:2]
    block_cols, rows, order = held.shape
    far = (count - 1) * block_cols
    ours, theirs, refs = refs[2 : 2 + far], refs[2 + far : 2 + 2 * far], refs[2 + 2 * far :]
    columns, both, *outward = refs
    col_index = lax.axis_index("col")
    left, right = [], []
    for t in range(count):
        for b in range(block_cols):
            if t:
                at = (t - 1) * block_cols + b
                pair = [ours[at][...], theirs[at][...]]
            else:
                pair = [held[b], mate[b]]
            left.append(jnp.concatenate(pair, axis=0))
            right.append(columns[b * count + ((col_index >> 1) ^ t)])
    summed = product(jnp.concatenate(left, axis=1), jnp.concatenate(right, axis=0), ((1,), (0,)))
    here = (col_index & 1) * rows
    both[pl.ds(pl.multiple_of(here, 8), rows), :] = summed[:rows]
    both[pl.ds(pl.multiple_of(rows - here, 8), rows), :] = summed[rows:]
    share = order // len(outward)
    for flip, piece in enumerate(outward):
        start = (col_index ^ flip) * share
        for a in range(2 * rows // order):
            picked = both[pl.ds(pl.multiple_of(a * order + start, 8), share), :]
            piece[pl.ds(a * share, share), :] = -picked


def partials(held, mate, ours, theirs, columns, receivers):
    block_cols, rows, _ = held.shape
    rows, span = 2 * rows, columns.shape[2]
    operands = (held, mate, *ours, *theirs, columns)
    outward = (jax.ShapeDtypeStruct((rows // receivers, span), jnp.float32),) * receivers
    both, *outward = pl.pallas_call(
        functools.partial(partials_kernel, 1 + len(ours) // block_cols),
        out_shape=(jax.ShapeDtypeStruct((rows, span), jnp.float32),) + outward,
        in_specs=[WHOLE] * len(operands),
        out_specs=(WHOLE,) * (1 + receivers),
        cost_estimate=LIGHT,
        compiler_params=ROOM,
    )(*operands)
    return both, outward


def stay_kernel(tall, own, stay):
    stay[...] = parity_half(own[...], tall, lax.axis_index("row") & 1)


def stay_half(own, tall):
    rows, width = own.shape
    return pl.pallas_call(
        functools.partial(stay_kernel, tall),
        out_shape=jax.ShapeDtypeStruct((rows, width // 2), jnp.float32),
        in_specs=[WHOLE],
        out_specs=WHOLE,
        cost_estimate=LIGHT,
        compiler_params=ROOM,
    )(own)


def finish_kernel(flips, both, got, stay, swapped, mate_swapped, dinv, *refs):
    along, update, terms = refs[:-2], refs[-2], refs[-1]
    rows = stay.shape[0]
    row_index = lax.axis_index("row")
    here = (row_index & 1) * rows
    update[...] = both[...] + got[...]
    mine = update[pl.ds(pl.multiple_of(here, 8), rows), :]
    other = update[pl.ds(pl.multiple_of(rows - here, 8), rows), :]
    same = (row_index & 1) == (lax.axis_index("col") & 1)
    depth = stay.shape[1] // swapped.shape[2]
    near = [jnp.where(same, swapped[j], mate_swapped[j]) for j in range(depth)]
    factors = jnp.concatenate([stay[...], jnp.concatenate(near, axis=1)], axis=0)
    terms[...] = product(factors, jnp.concatenate([mine, other], axis=0), ((0,), (0,)))
    tall = dinv.shape[0]
    for flip, piece in zip(flips, along):
        slot = ((row_index ^ flip) >> 1) * tall
        piece[...] = terms[pl.ds(pl.multiple_of(slot, 8), tall), :]
    along[0][...] = along[0][...] + dinv[...]


def finish(both, got, stay, swapped, mate_swapped, dinv, flips):
    rows, half = stay.shape
    span = both.shape[1]
    return pl.pallas_call(
        functools.partial(finish_kernel, flips),
        out_shape=(jax.ShapeDtypeStruct(dinv.shape, jnp.float32),) * len(flips),
        in_specs=[WHOLE] * 6,
        out_specs=(WHOLE,) * len(flips),
        scratch_shapes=[
            pltpu.VMEM((2 * rows, span), jnp.float32),
            pltpu.VMEM((half, span), jnp.float32),
        ],
        cost_estimate=LIGHT,
        compiler_params=ROOM,
    )(both, got, stay, swapped, mate_swapped, dinv)


def collect_kernel(*refs):
    arrived, (_, keep, send) = refs[:-3], refs[-3:]
    share = keep.shape[0]
    span = refs[0].shape[1]
    here = (lax.axis_index("row") & 1) * share
    for flip, piece in enumerate(arrived):
        spot = pl.ds(pl.multiple_of((lax.axis_index("col") ^ flip) * span, LANES), span)
        keep[:, spot] = piece[pl.ds(pl.multiple_of(here, 8), share), :]
        send[:, spot] = piece[pl.ds(pl.multiple_of(share - here, 8), share), :]


def collect(arrived, along):
    flips = len(arrived)
    share, span = arrived[0].shape[0] // 2, arrived[0].shape[1]
    if span % LANES:
        me = lax.axis_index("col")
        row_bit = lax.axis_index("row") & 1
        laid = jnp.concatenate([lax.select_n(me ^ j, *arrived) for j in range(flips)], axis=1)
        laid = laid.reshape(2, share, span * flips)
        return [lax.dynamic_index_in_dim(laid, row_bit ^ k, 0, keepdims=False) for k in range(2)]
    part = jax.ShapeDtypeStruct((share, span * flips), jnp.float32)
    return pl.pallas_call(
        collect_kernel,
        out_shape=(part, part),
        in_specs=[WHOLE] * flips + [pl.BlockSpec(memory_space=pl.ANY)],
        out_specs=(WHOLE, WHOLE),
        cost_estimate=LIGHT,
        compiler_params=ROOM,
    )(*arrived, along)


def close_kernel(keep, came, total, off_diag, diag_block):
    off_diag[...] = keep[...] + came[...]
    diag_block[...] = total[...]


def close(keep, came, total):
    return pl.pallas_call(
        close_kernel,
        out_shape=[jax.ShapeDtypeStruct(x.shape, jnp.float32) for x in (keep, total)],
        in_specs=[WHOLE] * 3,
        out_specs=[WHOLE, WHOLE],
        cost_estimate=LIGHT,
        compiler_params=ROOM,
    )(keep, came, total)


def pick_kernel(block_cols, b, presence, blocks, swapped, held):
    same = (lax.axis_index("row") & 1) == (lax.axis_index("col") & 1)
    rows, order = held.shape
    for a in range(rows // order):
        here = pl.ds(a * order, order)
        block = masked_block(presence, blocks, block_cols, a, b)
        held[here, :] = jnp.where(same, block, swapped[here, :])


def pick(presence, blocks, swapped, b):
    return pl.pallas_call(
        functools.partial(pick_kernel, blocks.shape[0] // swapped.shape[0], b),
        out_shape=jax.ShapeDtypeStruct(swapped.shape, jnp.float32),
        in_specs=[WHOLE] * 3,
        out_specs=WHOLE,
        cost_estimate=LIGHT,
        compiler_params=ROOM,
    )(presence, blocks, swapped)


def stacked_kernel(*refs):
    for at, piece in enumerate(refs[:-1]):
        refs[-1][at] = piece[...]


def stacked(pieces):
    return pl.pallas_call(
        stacked_kernel,
        out_shape=jax.ShapeDtypeStruct((len(pieces),) + pieces[0].shape, jnp.float32),
        in_specs=[WHOLE] * len(pieces),
        out_specs=WHOLE,
        cost_estimate=LIGHT,
        compiler_params=ROOM,
    )(*pieces)


def crossed(swap):
    groups_row = lax.axis_size("row")
    groups_col = lax.axis_size("col")
    cross = [
        (r * groups_col + c, (r ^ 1) * groups_col + (c ^ 1))
        for r in range(groups_row)
        for c in range(groups_col)
    ]
    return lax.ppermute(swap, ("row", "col"), cross)


def along_line(mine, order):
    strips, flips = [mine], [0]
    bit = lax.axis_size("row") // 2
    while bit > 1:
        strips = strips + [flipped(strip, "row", bit) for strip in strips]
        flips = flips + [flip ^ bit for flip in flips]
        bit //= 2
    return ordered(strips, tuple(flips), order)


def local(inverse_set, presence, factor, dinv):
    groups_row = lax.axis_size("row")
    groups_col = lax.axis_size("col")
    block_rows, _, order, width = factor.shape
    block_cols = inverse_set.shape[3]
    span = width // groups_col
    rows = block_rows * order
    share = order // groups_col

    own = factor.reshape(rows, width)
    blocks = inverse_set.reshape(rows * block_cols, order)
    marks = presence.reshape(1, -1)
    tall = width // groups_row
    mine, swaps = prepare(marks, blocks, own, span, tall)
    swapped = [crossed(swap) for swap in swaps]
    stay = stay_half(own, tall)
    columns = along_line(mine, order)
    held = [pick(marks, blocks, swapped[b], b) for b in range(block_cols)]
    far = [(flip, piece) for flip in range(2, groups_col, 2) for piece in held]
    ours = [flipped(piece, "col", flip) for flip, piece in far]
    theirs = [flipped(piece, "col", 1) for piece in ours]
    held, swapped = stacked(held), stacked(swapped)
    mate, mate_swapped = flipped(held, "col", 1), flipped(swapped, "col", 1)

    both, outward = partials(held, mate, ours, theirs, columns, groups_col)
    got = flipped(both, "row", 1)
    arrived = [outward[0]] + [flipped(outward[f], "col", f) for f in range(1, groups_col)]
    flips = (0,) + tuple(range(groups_row - 2, 0, -2))
    along = finish(both, got, stay, swapped, mate_swapped, dinv, flips)
    keep, send = collect(arrived, along[0])
    came = flipped(send, "row", 1)
    met = [flipped(piece, "row", flip) if flip else piece for flip, piece in zip(flips, along)]
    off_diag, diag_block = close(keep, came, sum(met[1:], met[0]))
    return (off_diag.reshape(block_rows, 1, share, width), diag_block)


def solution(mesh):
    in_specs = (
        P(None, "row", None, None, "col", None),
        P(None, "row", None, "col"),
        P(None, "row", None, None),
        P("row", "col"),
    )
    out_specs = (P(None, "row", "col", None), P("row", "col"))
    return jax.shard_map(local, mesh=mesh, in_specs=in_specs, out_specs=out_specs, check_vma=False)
```

```python
import functools

import jax
import jax.numpy as jnp
from jax import lax
from jax.experimental import pallas as pl
from jax.experimental.pallas import tpu as pltpu
from jax.sharding import PartitionSpec as P

LANES = 128
WHOLE = pl.BlockSpec(memory_space=pltpu.VMEM)
ROOM = pltpu.CompilerParams(vmem_limit_bytes=16 * 1024 * 1024)
HEAVY = 10**9
LIGHT = pl.CostEstimate(flops=1000, bytes_accessed=1000, transcendentals=0)


def flipped(value, axis, flip):
    return lax.ppermute(value, axis, [(i, i ^ flip) for i in range(lax.axis_size(axis))])


def two_parts(value):
    high = value.astype(jnp.bfloat16)
    return high, (value - high.astype(jnp.float32)).astype(jnp.bfloat16)


def product(left, right, contract):
    left_high, left_low = two_parts(left)
    right_high, right_low = two_parts(right)

    def once(a, b):
        return lax.dot_general(a, b, (contract, ((), ())), preferred_element_type=jnp.float32)

    return once(left_high, right_high) + (once(left_high, right_low) + once(left_low, right_high))


def parity_half(factor, tall, parity):
    even, odd = [
        jnp.concatenate(
            [factor[:, i : i + tall] for i in range(first, factor.shape[1], 2 * tall)], axis=1
        )
        for first in (0, tall)
    ]
    return jnp.where(parity == 1, odd, even)


def masked_block(presence, blocks, block_cols, a, b):
    order = blocks.shape[1]
    at = a * block_cols + b
    weight = presence[:, at : at + 1].astype(jnp.float32)
    return blocks[pl.ds(a * order * block_cols + b, order, stride=block_cols), :] * weight


def prepare_kernel(tall, presence, blocks, factor, mine, *swaps):
    rows, span = mine.shape
    mine[...] = factor[:, pl.ds(pl.multiple_of(lax.axis_index("col") * span, LANES), span)]
    row_bit = lax.axis_index("row") & 1
    same = row_bit == (lax.axis_index("col") & 1)
    order = blocks.shape[1]
    block_cols = blocks.shape[0] // rows
    half = parity_half(factor[...], tall, 1 - row_bit)
    for b, swap in enumerate(swaps):
        for a in range(rows // order):
            here = pl.ds(a * order, order)
            part = half[a * order : (a + 1) * order, b * order : (b + 1) * order]
            if b >= block_cols:
                swap[here, :] = part
                continue
            block = masked_block(presence, blocks, block_cols, a, b)
            swap[here, :] = jnp.where(same, part, block) if part.shape[1] else block


def prepare(presence, blocks, own, span, tall):
    rows, width = own.shape
    block_cols = blocks.shape[0] // rows
    order = blocks.shape[1]
    depth = max(block_cols, width // 2 // order)
    if span % LANES:
        first = lax.axis_index("col") * span
        row_bit = lax.axis_index("row") & 1
        same = row_bit == (lax.axis_index("col") & 1)
        mine = lax.dynamic_slice_in_dim(own, first, span, 1)
        weights = presence.reshape(-1, 1, block_cols, 1).astype(jnp.float32)
        picked = blocks.reshape(-1, order, block_cols, order) * weights
        masked = picked.transpose(2, 0, 1, 3).reshape(block_cols, rows, order)
        half = parity_half(own, tall, 1 - row_bit).reshape(rows, -1, order).transpose(1, 0, 2)
        half = jnp.pad(half, ((0, depth - half.shape[0]), (0, 0), (0, 0)))
        padded = jnp.pad(masked, ((0, depth - block_cols), (0, 0), (0, 0)))
        return mine, list(jnp.where(same, half, padded))
    mine, *swaps = pl.pallas_call(
        functools.partial(prepare_kernel, tall),
        out_shape=(jax.ShapeDtypeStruct((rows, span), jnp.float32),)
        + (jax.ShapeDtypeStruct((rows, order), jnp.float32),) * depth,
        in_specs=[WHOLE] * 3,
        out_specs=(WHOLE,) * (1 + depth),
        cost_estimate=LIGHT,
    )(presence, blocks, own)
    return mine, swaps


def ordered_kernel(flips, *refs):
    columns = refs[-1]
    _, order, _ = columns.shape
    for flip, strip in zip(flips, refs[:-1]):
        at = (lax.axis_index("row") ^ flip) >> 1
        for a in range(strip.shape[0] // order):
            columns[a * len(flips) + at] = strip[pl.ds(a * order, order), :]


def ordered(strips, flips, order):
    rows, span = strips[0].shape
    return pl.pallas_call(
        functools.partial(ordered_kernel, flips),
        out_shape=jax.ShapeDtypeStruct((rows // order * len(strips), order, span), jnp.float32),
        in_specs=[WHOLE] * len(strips),
        out_specs=WHOLE,
        cost_estimate=pl.CostEstimate(flops=HEAVY, bytes_accessed=1000, transcendentals=0),
        compiler_params=ROOM,
    )(*strips)


def partials_kernel(count, *refs):
    held, mate = refs[:2]
    block_cols, rows, order = held.shape
    far = (count - 1) * block_cols
    ours, theirs, refs = refs[2 : 2 + far], refs[2 + far : 2 + 2 * far], refs[2 + 2 * far :]
    columns, both, *outward = refs
    col_index = lax.axis_index("col")
    left, right = [], []
    for t in range(count):
        for b in range(block_cols):
            if t:
                at = (t - 1) * block_cols + b
                pair = [ours[at][...], theirs[at][...]]
            else:
                pair = [held[b], mate[b]]
            left.append(jnp.concatenate(pair, axis=0))
            right.append(columns[b * count + ((col_index >> 1) ^ t)])
    summed = product(jnp.concatenate(left, axis=1), jnp.concatenate(right, axis=0), ((1,), (0,)))
    here = (col_index & 1) * rows
    both[pl.ds(pl.multiple_of(here, 8), rows), :] = summed[:rows]
    both[pl.ds(pl.multiple_of(rows - here, 8), rows), :] = summed[rows:]
    share = order // len(outward)
    for flip, piece in enumerate(outward):
        start = (col_index ^ flip) * share
        for a in range(2 * rows // order):
            picked = both[pl.ds(pl.multiple_of(a * order + start, 8), share), :]
            piece[pl.ds(a * share, share), :] = -picked


def partials(held, mate, ours, theirs, columns, receivers):
    block_cols, rows, _ = held.shape
    rows, span = 2 * rows, columns.shape[2]
    operands = (held, mate, *ours, *theirs, columns)
    outward = (jax.ShapeDtypeStruct((rows // receivers, span), jnp.float32),) * receivers
    both, *outward = pl.pallas_call(
        functools.partial(partials_kernel, 1 + len(ours) // block_cols),
        out_shape=(jax.ShapeDtypeStruct((rows, span), jnp.float32),) + outward,
        in_specs=[WHOLE] * len(operands),
        out_specs=(WHOLE,) * (1 + receivers),
        cost_estimate=LIGHT,
        compiler_params=ROOM,
    )(*operands)
    return both, outward


def stay_kernel(tall, own, stay):
    stay[...] = parity_half(own[...], tall, lax.axis_index("row") & 1)


def stay_half(own, tall):
    rows, width = own.shape
    return pl.pallas_call(
        functools.partial(stay_kernel, tall),
        out_shape=jax.ShapeDtypeStruct((rows, width // 2), jnp.float32),
        in_specs=[WHOLE],
        out_specs=WHOLE,
        cost_estimate=LIGHT,
        compiler_params=ROOM,
    )(own)


def finish_kernel(flips, both, got, stay, swapped, mate_swapped, dinv, *refs):
    along, update, terms = refs[:-2], refs[-2], refs[-1]
    rows = stay.shape[0]
    row_index = lax.axis_index("row")
    here = (row_index & 1) * rows
    update[...] = both[...] + got[...]
    mine = update[pl.ds(pl.multiple_of(here, 8), rows), :]
    other = update[pl.ds(pl.multiple_of(rows - here, 8), rows), :]
    same = (row_index & 1) == (lax.axis_index("col") & 1)
    depth = stay.shape[1] // swapped.shape[2]
    near = [jnp.where(same, swapped[j], mate_swapped[j]) for j in range(depth)]
    factors = jnp.concatenate([stay[...], jnp.concatenate(near, axis=1)], axis=0)
    terms[...] = product(factors, jnp.concatenate([mine, other], axis=0), ((0,), (0,)))
    tall = dinv.shape[0]
    for flip, piece in zip(flips, along):
        slot = ((row_index ^ flip) >> 1) * tall
        piece[...] = terms[pl.ds(pl.multiple_of(slot, 8), tall), :]
    along[0][...] = along[0][...] + dinv[...]


def finish(both, got, stay, swapped, mate_swapped, dinv, flips):
    rows, half = stay.shape
    span = both.shape[1]
    return pl.pallas_call(
        functools.partial(finish_kernel, flips),
        out_shape=(jax.ShapeDtypeStruct(dinv.shape, jnp.float32),) * len(flips),
        in_specs=[WHOLE] * 6,
        out_specs=(WHOLE,) * len(flips),
        scratch_shapes=[
            pltpu.VMEM((2 * rows, span), jnp.float32),
            pltpu.VMEM((half, span), jnp.float32),
        ],
        cost_estimate=LIGHT,
        compiler_params=ROOM,
    )(both, got, stay, swapped, mate_swapped, dinv)


def collect_kernel(flips, *refs):
    arrived, (keep, send) = refs[:-2], refs[-2:]
    share = keep.shape[0]
    span = refs[0].shape[1]
    here = (lax.axis_index("row") & 1) * share
    for flip, piece in zip(flips, arrived):
        spot = pl.ds(pl.multiple_of((lax.axis_index("col") ^ flip) * span, LANES), span)
        keep[:, spot] = piece[pl.ds(pl.multiple_of(here, 8), share), :]
        send[:, spot] = piece[pl.ds(pl.multiple_of(share - here, 8), share), :]


def collect(arrived, flips):
    share, span = arrived[0].shape[0] // 2, arrived[0].shape[1]
    if span % LANES:
        me = lax.axis_index("col")
        by_flip = [arrived[flips.index(flip)] for flip in range(len(flips))]
        row_bit = lax.axis_index("row") & 1
        laid = jnp.concatenate([lax.select_n(me ^ j, *by_flip) for j in range(len(flips))], axis=1)
        laid = laid.reshape(2, share, span * len(flips))
        return [lax.dynamic_index_in_dim(laid, row_bit ^ k, 0, keepdims=False) for k in range(2)]
    part = jax.ShapeDtypeStruct((share, span * len(flips)), jnp.float32)
    return pl.pallas_call(
        functools.partial(collect_kernel, flips),
        out_shape=(part, part),
        in_specs=[WHOLE] * len(flips),
        out_specs=(WHOLE, WHOLE),
        cost_estimate=LIGHT,
        compiler_params=ROOM,
    )(*arrived)


def close_kernel(keep, came, *refs):
    along, (off_diag, diag_block) = refs[:-2], refs[-2:]
    off_diag[...] = keep[...] + came[...]
    total = along[0][...]
    for piece in along[1:]:
        total = total + piece[...]
    diag_block[...] = total


def close(keep, came, along):
    return pl.pallas_call(
        close_kernel,
        out_shape=[jax.ShapeDtypeStruct(x.shape, jnp.float32) for x in (keep, along[0])],
        in_specs=[WHOLE] * (2 + len(along)),
        out_specs=[WHOLE, WHOLE],
        cost_estimate=LIGHT,
        compiler_params=ROOM,
    )(keep, came, *along)


def pick_kernel(block_cols, b, presence, blocks, swapped, held):
    same = (lax.axis_index("row") & 1) == (lax.axis_index("col") & 1)
    rows, order = held.shape
    for a in range(rows // order):
        here = pl.ds(a * order, order)
        block = masked_block(presence, blocks, block_cols, a, b)
        held[here, :] = jnp.where(same, block, swapped[here, :])


def pick(presence, blocks, swapped, b):
    return pl.pallas_call(
        functools.partial(pick_kernel, blocks.shape[0] // swapped.shape[0], b),
        out_shape=jax.ShapeDtypeStruct(swapped.shape, jnp.float32),
        in_specs=[WHOLE] * 3,
        out_specs=WHOLE,
        cost_estimate=LIGHT,
        compiler_params=ROOM,
    )(presence, blocks, swapped)


def stacked_kernel(*refs):
    for at, piece in enumerate(refs[:-1]):
        refs[-1][at] = piece[...]


def stacked(pieces):
    return pl.pallas_call(
        stacked_kernel,
        out_shape=jax.ShapeDtypeStruct((len(pieces),) + pieces[0].shape, jnp.float32),
        in_specs=[WHOLE] * len(pieces),
        out_specs=WHOLE,
        cost_estimate=LIGHT,
        compiler_params=ROOM,
    )(*pieces)


def crossed(swap):
    groups_row = lax.axis_size("row")
    groups_col = lax.axis_size("col")
    cross = [
        (r * groups_col + c, (r ^ 1) * groups_col + (c ^ 1))
        for r in range(groups_row)
        for c in range(groups_col)
    ]
    return lax.ppermute(swap, ("row", "col"), cross)


def along_line(mine, order):
    strips, flips = [mine], [0]
    bit = lax.axis_size("row") // 2
    while bit > 1:
        strips = strips + [flipped(strip, "row", bit) for strip in strips]
        flips = flips + [flip ^ bit for flip in flips]
        bit //= 2
    return ordered(strips, tuple(flips), order)


def local(inverse_set, presence, factor, dinv):
    groups_row = lax.axis_size("row")
    groups_col = lax.axis_size("col")
    block_rows, _, order, width = factor.shape
    block_cols = inverse_set.shape[3]
    span = width // groups_col
    rows = block_rows * order
    share = order // groups_col

    own = factor.reshape(rows, width)
    blocks = inverse_set.reshape(rows * block_cols, order)
    marks = presence.reshape(1, -1)
    tall = width // groups_row
    mine, swaps = prepare(marks, blocks, own, span, tall)
    swapped = [crossed(swap) for swap in swaps]
    stay = stay_half(own, tall)
    columns = along_line(mine, order)
    held = [pick(marks, blocks, swapped[b], b) for b in range(block_cols)]
    far = [(flip, piece) for flip in range(2, groups_col, 2) for piece in held]
    ours = [flipped(piece, "col", flip) for flip, piece in far]
    theirs = [flipped(piece, "col", 1) for piece in ours]
    held, swapped = stacked(held), stacked(swapped)
    mate, mate_swapped = flipped(held, "col", 1), flipped(swapped, "col", 1)

    both, outward = partials(held, mate, ours, theirs, columns, groups_col)
    got = flipped(both, "row", 1)
    far_first = (0, *range(groups_col - 1, 0, -1))
    arrived = [flipped(outward[f], "col", f) if f else outward[f] for f in far_first]
    keep, send = collect(arrived, far_first)
    came = flipped(send, "row", 1)
    flips = (0,) + tuple(range(groups_row - 2, 0, -2))
    along = finish(both, got, stay, swapped, mate_swapped, dinv, flips)
    met = [flipped(piece, "row", flip) if flip else piece for flip, piece in zip(flips, along)]
    off_diag, diag_block = close(keep, came, met)
    return (off_diag.reshape(block_rows, 1, share, width), diag_block)


def solution(mesh):
    in_specs = (
        P(None, "row", None, None, "col", None),
        P(None, "row", None, "col"),
        P(None, "row", None, None),
        P("row", "col"),
    )
    out_specs = (P(None, "row", "col", None), P("row", "col"))
    return jax.shard_map(local, mesh=mesh, in_specs=in_specs, out_specs=out_specs, check_vma=False)
```

```python
import functools

import jax
import jax.numpy as jnp
from jax import lax
from jax.experimental import pallas as pl
from jax.experimental.pallas import tpu as pltpu
from jax.sharding import PartitionSpec as P

LANES = 128
WHOLE = pl.BlockSpec(memory_space=pltpu.VMEM)
ROOM = pltpu.CompilerParams(vmem_limit_bytes=16 * 1024 * 1024)
HEAVY = 10**9
LIGHT = pl.CostEstimate(flops=1000, bytes_accessed=1000, transcendentals=0)


def flipped(value, axis, flip):
    return lax.ppermute(value, axis, [(i, i ^ flip) for i in range(lax.axis_size(axis))])


def two_parts(value):
    high = value.astype(jnp.bfloat16)
    return high, (value - high.astype(jnp.float32)).astype(jnp.bfloat16)


def product(left, right, contract):
    left_high, left_low = two_parts(left)
    right_high, right_low = two_parts(right)

    def once(a, b):
        return lax.dot_general(a, b, (contract, ((), ())), preferred_element_type=jnp.float32)

    return once(left_high, right_high) + (once(left_high, right_low) + once(left_low, right_high))


def parity_half(factor, tall, parity):
    even, odd = [
        jnp.concatenate(
            [factor[:, i : i + tall] for i in range(first, factor.shape[1], 2 * tall)], axis=1
        )
        for first in (0, tall)
    ]
    return jnp.where(parity == 1, odd, even)


def masked_block(presence, blocks, block_cols, a, b):
    order = blocks.shape[1]
    at = a * block_cols + b
    weight = presence[:, at : at + 1].astype(jnp.float32)
    return blocks[pl.ds(a * order * block_cols + b, order, stride=block_cols), :] * weight


def prepare_kernel(tall, presence, blocks, factor, mine, *swaps):
    rows, span = mine.shape
    mine[...] = factor[:, pl.ds(pl.multiple_of(lax.axis_index("col") * span, LANES), span)]
    row_bit = lax.axis_index("row") & 1
    same = row_bit == (lax.axis_index("col") & 1)
    order = blocks.shape[1]
    block_cols = blocks.shape[0] // rows
    half = parity_half(factor[...], tall, 1 - row_bit)
    for b, swap in enumerate(swaps):
        for a in range(rows // order):
            here = pl.ds(a * order, order)
            part = half[a * order : (a + 1) * order, b * order : (b + 1) * order]
            if b >= block_cols:
                swap[here, :] = part
                continue
            block = masked_block(presence, blocks, block_cols, a, b)
            swap[here, :] = jnp.where(same, part, block) if part.shape[1] else block


def prepare(presence, blocks, own, span, tall):
    rows, width = own.shape
    block_cols = blocks.shape[0] // rows
    order = blocks.shape[1]
    depth = max(block_cols, width // 2 // order)
    if span % LANES:
        first = lax.axis_index("col") * span
        row_bit = lax.axis_index("row") & 1
        same = row_bit == (lax.axis_index("col") & 1)
        mine = lax.dynamic_slice_in_dim(own, first, span, 1)
        weights = presence.reshape(-1, 1, block_cols, 1).astype(jnp.float32)
        picked = blocks.reshape(-1, order, block_cols, order) * weights
        masked = picked.transpose(2, 0, 1, 3).reshape(block_cols, rows, order)
        half = parity_half(own, tall, 1 - row_bit).reshape(rows, -1, order).transpose(1, 0, 2)
        half = jnp.pad(half, ((0, depth - half.shape[0]), (0, 0), (0, 0)))
        padded = jnp.pad(masked, ((0, depth - block_cols), (0, 0), (0, 0)))
        return mine, list(jnp.where(same, half, padded))
    mine, *swaps = pl.pallas_call(
        functools.partial(prepare_kernel, tall),
        out_shape=(jax.ShapeDtypeStruct((rows, span), jnp.float32),)
        + (jax.ShapeDtypeStruct((rows, order), jnp.float32),) * depth,
        in_specs=[WHOLE] * 3,
        out_specs=(WHOLE,) * (1 + depth),
        cost_estimate=LIGHT,
    )(presence, blocks, own)
    return mine, swaps


def ordered_kernel(flips, *refs):
    columns = refs[-1]
    _, order, _ = columns.shape
    for flip, strip in zip(flips, refs[:-1]):
        at = (lax.axis_index("row") ^ flip) >> 1
        for a in range(strip.shape[0] // order):
            columns[a * len(flips) + at] = strip[pl.ds(a * order, order), :]


def ordered(strips, flips, order):
    rows, span = strips[0].shape
    return pl.pallas_call(
        functools.partial(ordered_kernel, flips),
        out_shape=jax.ShapeDtypeStruct((rows // order * len(strips), order, span), jnp.float32),
        in_specs=[WHOLE] * len(strips),
        out_specs=WHOLE,
        cost_estimate=pl.CostEstimate(flops=HEAVY, bytes_accessed=1000, transcendentals=0),
        compiler_params=ROOM,
    )(*strips)


def partials_kernel(count, *refs):
    held, mate = refs[:2]
    block_cols, rows, order = held.shape
    far = (count - 1) * block_cols
    ours, theirs, refs = refs[2 : 2 + far], refs[2 + far : 2 + 2 * far], refs[2 + 2 * far :]
    columns, both = refs
    col_index = lax.axis_index("col")
    left, right = [], []
    for t in range(count):
        for b in range(block_cols):
            if t:
                at = (t - 1) * block_cols + b
                pair = [ours[at][...], theirs[at][...]]
            else:
                pair = [held[b], mate[b]]
            left.append(jnp.concatenate(pair, axis=0))
            right.append(columns[b * count + ((col_index >> 1) ^ t)])
    summed = product(jnp.concatenate(left, axis=1), jnp.concatenate(right, axis=0), ((1,), (0,)))
    here = (col_index & 1) * rows
    both[pl.ds(pl.multiple_of(here, 8), rows), :] = summed[:rows]
    both[pl.ds(pl.multiple_of(rows - here, 8), rows), :] = summed[rows:]


def partials(held, mate, ours, theirs, columns):
    block_cols, rows, _ = held.shape
    operands = (held, mate, *ours, *theirs, columns)
    return pl.pallas_call(
        functools.partial(partials_kernel, 1 + len(ours) // block_cols),
        out_shape=jax.ShapeDtypeStruct((2 * rows, columns.shape[2]), jnp.float32),
        in_specs=[WHOLE] * len(operands),
        out_specs=WHOLE,
        cost_estimate=LIGHT,
        compiler_params=ROOM,
    )(*operands)


def stay_kernel(tall, own, stay):
    stay[...] = parity_half(own[...], tall, lax.axis_index("row") & 1)


def stay_half(own, tall):
    rows, width = own.shape
    return pl.pallas_call(
        functools.partial(stay_kernel, tall),
        out_shape=jax.ShapeDtypeStruct((rows, width // 2), jnp.float32),
        in_specs=[WHOLE],
        out_specs=WHOLE,
        cost_estimate=LIGHT,
        compiler_params=ROOM,
    )(own)


def finish_kernel(order, flips, both, got, stay, swapped, mate_swapped, dinv, *refs):
    update, terms = refs[-2:]
    along, outward = refs[: len(flips)], refs[len(flips) : -2]
    rows = stay.shape[0]
    row_index = lax.axis_index("row")
    col_index = lax.axis_index("col")
    here = (row_index & 1) * rows
    update[...] = both[...] + got[...]
    mine = update[pl.ds(pl.multiple_of(here, 8), rows), :]
    other = update[pl.ds(pl.multiple_of(rows - here, 8), rows), :]
    same = (row_index & 1) == (col_index & 1)
    depth = stay.shape[1] // swapped.shape[2]
    near = [jnp.where(same, swapped[j], mate_swapped[j]) for j in range(depth)]
    factors = jnp.concatenate([stay[...], jnp.concatenate(near, axis=1)], axis=0)
    terms[...] = product(factors, jnp.concatenate([mine, other], axis=0), ((0,), (0,)))
    tall = dinv.shape[0]
    for flip, piece in zip(flips, along):
        slot = ((row_index ^ flip) >> 1) * tall
        piece[...] = terms[pl.ds(pl.multiple_of(slot, 8), tall), :]
    along[0][...] = along[0][...] + dinv[...]
    share = order // len(outward)
    for flip, piece in enumerate(outward):
        start = here + (col_index ^ flip) * share
        for a in range(rows // order):
            picked = update[pl.ds(pl.multiple_of(a * order + start, 8), share), :]
            piece[pl.ds(a * share, share), :] = -picked


def finish(both, got, stay, swapped, mate_swapped, dinv, order, flips, receivers):
    rows, half = stay.shape
    span = both.shape[1]
    along = (jax.ShapeDtypeStruct(dinv.shape, jnp.float32),) * len(flips)
    outward = (jax.ShapeDtypeStruct((rows // receivers, span), jnp.float32),) * receivers
    outs = pl.pallas_call(
        functools.partial(finish_kernel, order, flips),
        out_shape=along + outward,
        in_specs=[WHOLE] * 6,
        out_specs=(WHOLE,) * (len(flips) + receivers),
        scratch_shapes=[
            pltpu.VMEM((2 * rows, span), jnp.float32),
            pltpu.VMEM((half, span), jnp.float32),
        ],
        cost_estimate=LIGHT,
        compiler_params=ROOM,
    )(both, got, stay, swapped, mate_swapped, dinv)
    return outs[: len(flips)], outs[len(flips) :]


def close_kernel(count, *refs):
    met, arrived = refs[:count], refs[count:-2]
    off_diag, diag_block = refs[-2:]
    span = arrived[0].shape[1]
    for flip, piece in enumerate(arrived):
        first = pl.multiple_of((lax.axis_index("col") ^ flip) * span, LANES)
        off_diag[:, pl.ds(first, span)] = piece[...]
    diag_block[...] = sum([piece[...] for piece in met[1:]], met[0][...])


def close(arrived, met):
    share, span = arrived[0].shape
    if span % LANES:
        me = lax.axis_index("col")
        laid = [lax.select_n(me ^ j, *arrived) for j in range(len(arrived))]
        return jnp.concatenate(laid, axis=1), sum(met[1:], met[0])
    return pl.pallas_call(
        functools.partial(close_kernel, len(met)),
        out_shape=(
            jax.ShapeDtypeStruct((share, span * len(arrived)), jnp.float32),
            jax.ShapeDtypeStruct(met[0].shape, jnp.float32),
        ),
        in_specs=[WHOLE] * (len(arrived) + len(met)),
        out_specs=(WHOLE, WHOLE),
        cost_estimate=LIGHT,
        compiler_params=ROOM,
    )(*met, *arrived)


def pick_kernel(block_cols, b, presence, blocks, swapped, held):
    same = (lax.axis_index("row") & 1) == (lax.axis_index("col") & 1)
    rows, order = held.shape
    for a in range(rows // order):
        here = pl.ds(a * order, order)
        block = masked_block(presence, blocks, block_cols, a, b)
        held[here, :] = jnp.where(same, block, swapped[here, :])


def pick(presence, blocks, swapped, b):
    return pl.pallas_call(
        functools.partial(pick_kernel, blocks.shape[0] // swapped.shape[0], b),
        out_shape=jax.ShapeDtypeStruct(swapped.shape, jnp.float32),
        in_specs=[WHOLE] * 3,
        out_specs=WHOLE,
        cost_estimate=LIGHT,
        compiler_params=ROOM,
    )(presence, blocks, swapped)


def stacked_kernel(*refs):
    for at, piece in enumerate(refs[:-1]):
        refs[-1][at] = piece[...]


def stacked(pieces):
    return pl.pallas_call(
        stacked_kernel,
        out_shape=jax.ShapeDtypeStruct((len(pieces),) + pieces[0].shape, jnp.float32),
        in_specs=[WHOLE] * len(pieces),
        out_specs=WHOLE,
        cost_estimate=LIGHT,
        compiler_params=ROOM,
    )(*pieces)


def crossed(swap):
    groups_row = lax.axis_size("row")
    groups_col = lax.axis_size("col")
    cross = [
        (r * groups_col + c, (r ^ 1) * groups_col + (c ^ 1))
        for r in range(groups_row)
        for c in range(groups_col)
    ]
    return lax.ppermute(swap, ("row", "col"), cross)


def along_line(mine, order):
    strips, flips = [mine], [0]
    bit = lax.axis_size("row") // 2
    while bit > 1:
        strips = strips + [flipped(strip, "row", bit) for strip in strips]
        flips = flips + [flip ^ bit for flip in flips]
        bit //= 2
    return ordered(strips, tuple(flips), order)


def local(inverse_set, presence, factor, dinv):
    groups_row = lax.axis_size("row")
    groups_col = lax.axis_size("col")
    block_rows, _, order, width = factor.shape
    block_cols = inverse_set.shape[3]
    span = width // groups_col
    rows = block_rows * order
    share = order // groups_col

    own = factor.reshape(rows, width)
    blocks = inverse_set.reshape(rows * block_cols, order)
    marks = presence.reshape(1, -1)
    tall = width // groups_row
    mine, swaps = prepare(marks, blocks, own, span, tall)
    swapped = [crossed(swap) for swap in swaps]
    stay = stay_half(own, tall)
    columns = along_line(mine, order)
    held = [pick(marks, blocks, swapped[b], b) for b in range(block_cols)]
    far = [(flip, piece) for flip in range(2, groups_col, 2) for piece in held]
    ours = [flipped(piece, "col", flip) for flip, piece in far]
    theirs = [flipped(piece, "col", 1) for piece in ours]
    held, swapped = stacked(held), stacked(swapped)
    mate, mate_swapped = flipped(held, "col", 1), flipped(swapped, "col", 1)

    both = partials(held, mate, ours, theirs, columns)
    got = flipped(both, "row", 1)
    flips = (0, *range(groups_row - 2, 0, -2))
    along, outward = finish(
        both, got, stay, swapped, mate_swapped, dinv, order, flips, groups_col
    )
    met = [flipped(piece, "row", flip) if flip else piece for flip, piece in zip(flips, along)]
    arrived = [flipped(piece, "col", f) if f else piece for f, piece in enumerate(outward)]
    off_diag, diag_block = close(arrived, met)
    return (off_diag.reshape(block_rows, 1, share, width), diag_block)


def solution(mesh):
    in_specs = (
        P(None, "row", None, None, "col", None),
        P(None, "row", None, "col"),
        P(None, "row", None, None),
        P("row", "col"),
    )
    out_specs = (P(None, "row", "col", None), P("row", "col"))
    return jax.shard_map(local, mesh=mesh, in_specs=in_specs, out_specs=out_specs, check_vma=False)
```

```python
import functools

import jax
import jax.numpy as jnp
from jax import lax
from jax.experimental import pallas as pl
from jax.experimental.pallas import tpu as pltpu
from jax.sharding import PartitionSpec as P

LANES = 128
WHOLE = pl.BlockSpec(memory_space=pltpu.VMEM)
ROOM = pltpu.CompilerParams(vmem_limit_bytes=16 * 1024 * 1024)
HEAVY = 10**9
LIGHT = pl.CostEstimate(flops=1000, bytes_accessed=1000, transcendentals=0)


def flipped(value, axis, flip):
    return lax.ppermute(value, axis, [(i, i ^ flip) for i in range(lax.axis_size(axis))])


def two_parts(value):
    high = value.astype(jnp.bfloat16)
    return high, (value - high.astype(jnp.float32)).astype(jnp.bfloat16)


def product(left, right, contract):
    left_high, left_low = two_parts(left)
    right_high, right_low = two_parts(right)

    def once(a, b):
        return lax.dot_general(a, b, (contract, ((), ())), preferred_element_type=jnp.float32)

    return once(left_high, right_high) + (once(left_high, right_low) + once(left_low, right_high))


def parity_half(factor, tall, parity):
    even, odd = [
        jnp.concatenate(
            [factor[:, i : i + tall] for i in range(first, factor.shape[1], 2 * tall)], axis=1
        )
        for first in (0, tall)
    ]
    return jnp.where(parity == 1, odd, even)


def masked_block(presence, blocks, block_cols, a, b):
    order = blocks.shape[1]
    at = a * block_cols + b
    weight = presence[:, at : at + 1].astype(jnp.float32)
    return blocks[pl.ds(a * order * block_cols + b, order, stride=block_cols), :] * weight


def prepare_kernel(tall, presence, blocks, factor, mine, *swaps):
    rows, span = mine.shape
    mine[...] = factor[:, pl.ds(pl.multiple_of(lax.axis_index("col") * span, LANES), span)]
    row_bit = lax.axis_index("row") & 1
    same = row_bit == (lax.axis_index("col") & 1)
    order = blocks.shape[1]
    block_cols = blocks.shape[0] // rows
    half = parity_half(factor[...], tall, 1 - row_bit)
    for b, swap in enumerate(swaps):
        for a in range(rows // order):
            here = pl.ds(a * order, order)
            part = half[a * order : (a + 1) * order, b * order : (b + 1) * order]
            if b >= block_cols:
                swap[here, :] = part
                continue
            block = masked_block(presence, blocks, block_cols, a, b)
            swap[here, :] = jnp.where(same, part, block) if part.shape[1] else block


def prepare(presence, blocks, own, span, tall):
    rows, width = own.shape
    block_cols = blocks.shape[0] // rows
    order = blocks.shape[1]
    depth = max(block_cols, width // 2 // order)
    if span % LANES:
        first = lax.axis_index("col") * span
        row_bit = lax.axis_index("row") & 1
        same = row_bit == (lax.axis_index("col") & 1)
        mine = lax.dynamic_slice_in_dim(own, first, span, 1)
        weights = presence.reshape(-1, 1, block_cols, 1).astype(jnp.float32)
        picked = blocks.reshape(-1, order, block_cols, order) * weights
        masked = picked.transpose(2, 0, 1, 3).reshape(block_cols, rows, order)
        half = parity_half(own, tall, 1 - row_bit).reshape(rows, -1, order).transpose(1, 0, 2)
        half = jnp.pad(half, ((0, depth - half.shape[0]), (0, 0), (0, 0)))
        padded = jnp.pad(masked, ((0, depth - block_cols), (0, 0), (0, 0)))
        return mine, list(jnp.where(same, half, padded))
    mine, *swaps = pl.pallas_call(
        functools.partial(prepare_kernel, tall),
        out_shape=(jax.ShapeDtypeStruct((rows, span), jnp.float32),)
        + (jax.ShapeDtypeStruct((rows, order), jnp.float32),) * depth,
        in_specs=[WHOLE] * 3,
        out_specs=(WHOLE,) * (1 + depth),
        cost_estimate=LIGHT,
    )(presence, blocks, own)
    return mine, swaps


def ordered_kernel(flips, *refs):
    columns = refs[-1]
    _, order, _ = columns.shape
    for flip, strip in zip(flips, refs[:-1]):
        at = (lax.axis_index("row") ^ flip) >> 1
        for a in range(strip.shape[0] // order):
            columns[a * len(flips) + at] = strip[pl.ds(a * order, order), :]


def ordered(strips, flips, order):
    rows, span = strips[0].shape
    return pl.pallas_call(
        functools.partial(ordered_kernel, flips),
        out_shape=jax.ShapeDtypeStruct((rows // order * len(strips), order, span), jnp.float32),
        in_specs=[WHOLE] * len(strips),
        out_specs=WHOLE,
        cost_estimate=pl.CostEstimate(flops=HEAVY, bytes_accessed=1000, transcendentals=0),
        compiler_params=ROOM,
    )(*strips)


def partials_kernel(count, *refs):
    held, mate = refs[:2]
    block_cols, rows, order = held.shape
    far = (count - 1) * block_cols
    ours, theirs, refs = refs[2 : 2 + far], refs[2 + far : 2 + 2 * far], refs[2 + 2 * far :]
    columns, kept, sent = refs
    col_index = lax.axis_index("col")
    left, right = [], []
    for t in range(count):
        for b in range(block_cols):
            if t:
                at = (t - 1) * block_cols + b
                pair = [ours[at][...], theirs[at][...]]
            else:
                pair = [held[b], mate[b]]
            left.append(jnp.concatenate(pair, axis=0))
            right.append(columns[b * count + ((col_index >> 1) ^ t)])
    summed = product(jnp.concatenate(left, axis=1), jnp.concatenate(right, axis=0), ((1,), (0,)))
    same = (lax.axis_index("row") & 1) == (col_index & 1)
    kept[...] = jnp.where(same, summed[:rows], summed[rows:])
    sent[...] = jnp.where(same, summed[rows:], summed[:rows])


def partials(held, mate, ours, theirs, columns):
    block_cols, rows, _ = held.shape
    operands = (held, mate, *ours, *theirs, columns)
    part = jax.ShapeDtypeStruct((rows, columns.shape[2]), jnp.float32)
    return pl.pallas_call(
        functools.partial(partials_kernel, 1 + len(ours) // block_cols),
        out_shape=(part, part),
        in_specs=[WHOLE] * len(operands),
        out_specs=(WHOLE, WHOLE),
        cost_estimate=LIGHT,
        compiler_params=ROOM,
    )(*operands)


def halves_kernel(tall, own, stay, away, part):
    row_bit = lax.axis_index("row") & 1
    stay[...] = parity_half(own[...], tall, row_bit)
    away[...] = parity_half(own[...], tall, 1 - row_bit)
    share = part.shape[1]
    upper = (lax.axis_index("col") & 1) == 1
    part[...] = jnp.where(upper, stay[:, share:], stay[:, :share])


def halves(own, tall):
    rows, width = own.shape
    half = jax.ShapeDtypeStruct((rows, width // 2), jnp.float32)
    return pl.pallas_call(
        functools.partial(halves_kernel, tall),
        out_shape=(half, half, jax.ShapeDtypeStruct((rows, width // 4), jnp.float32)),
        in_specs=[WHOLE],
        out_specs=(WHOLE,) * 3,
        cost_estimate=LIGHT,
        compiler_params=ROOM,
    )(own)


def terms_kernel(kept, sent, stay, away, swapped, mate_swapped, part, mate_part, dinv, terms):
    row_index = lax.axis_index("row")
    row_bit = row_index & 1
    col_bit = lax.axis_index("col") & 1
    depth = stay.shape[1] // swapped.shape[2]
    near = [
        jnp.where(row_bit == col_bit, swapped[j], mate_swapped[j]) for j in range(depth)
    ]
    far = [
        jnp.where(col_bit == 0, part[...], mate_part[...]),
        jnp.where(col_bit == 0, mate_part[...], part[...]),
    ]
    partial_pair = jnp.concatenate([kept[...], sent[...]], axis=0)
    shape = (terms.shape[0],) + terms.shape[2:]
    for slot, own, other in ((row_bit, stay, near), (1 - row_bit, away, far)):
        factors = jnp.concatenate([own[...], jnp.concatenate(other, axis=1)], axis=0)
        terms[:, slot] = product(factors, partial_pair, ((0,), (0,))).reshape(shape)
    line = row_index >> 1
    terms[line, row_bit] = terms[line, row_bit] + dinv[...]


def diagonal_terms(kept, sent, stay, away, swapped, mate_swapped, part, mate_part, dinv):
    tall, span = dinv.shape[0], kept.shape[1]
    operands = (kept, sent, stay, away, swapped, mate_swapped, part, mate_part, dinv)
    return pl.pallas_call(
        terms_kernel,
        out_shape=jax.ShapeDtypeStruct((stay.shape[1] // tall, 2, tall, span), jnp.float32),
        in_specs=[WHOLE] * len(operands),
        out_specs=WHOLE,
        cost_estimate=pl.CostEstimate(flops=HEAVY, bytes_accessed=1000, transcendentals=0),
        compiler_params=ROOM,
    )(*operands)


def outward_kernel(order, kept, got, *refs):
    outward, update = refs[:-1], refs[-1]
    rows = kept.shape[0]
    update[...] = kept[...] + got[...]
    share = order // len(outward)
    for flip, piece in enumerate(outward):
        start = (lax.axis_index("col") ^ flip) * share
        for a in range(rows // order):
            picked = update[pl.ds(pl.multiple_of(a * order + start, 8), share), :]
            piece[pl.ds(a * share, share), :] = -picked


def outward_pieces(kept, got, order, receivers):
    rows, span = kept.shape
    return pl.pallas_call(
        functools.partial(outward_kernel, order),
        out_shape=(jax.ShapeDtypeStruct((rows // receivers, span), jnp.float32),) * receivers,
        in_specs=[WHOLE] * 2,
        out_specs=(WHOLE,) * receivers,
        scratch_shapes=[pltpu.VMEM((rows, span), jnp.float32)],
        cost_estimate=LIGHT,
        compiler_params=ROOM,
    )(kept, got)


def close_kernel(met, *refs):
    arrived, off_diag, diag_block = refs[:-2], refs[-2], refs[-1]
    span = arrived[0].shape[1]
    for flip, piece in enumerate(arrived):
        first = pl.multiple_of((lax.axis_index("col") ^ flip) * span, LANES)
        off_diag[:, pl.ds(first, span)] = piece[...]
    diag_block[...] = jnp.sum(met[...], axis=0)


def close(arrived, met):
    share, span = arrived[0].shape
    if span % LANES:
        me = lax.axis_index("col")
        laid = [lax.select_n(me ^ j, *arrived) for j in range(len(arrived))]
        return jnp.concatenate(laid, axis=1), met.sum(axis=0)
    return pl.pallas_call(
        close_kernel,
        out_shape=(
            jax.ShapeDtypeStruct((share, span * len(arrived)), jnp.float32),
            jax.ShapeDtypeStruct(met.shape[1:], jnp.float32),
        ),
        in_specs=[WHOLE] * (1 + len(arrived)),
        out_specs=(WHOLE, WHOLE),
        cost_estimate=LIGHT,
        compiler_params=ROOM,
    )(met, *arrived)


def pick_kernel(block_cols, b, presence, blocks, swapped, held):
    same = (lax.axis_index("row") & 1) == (lax.axis_index("col") & 1)
    rows, order = held.shape
    for a in range(rows // order):
        here = pl.ds(a * order, order)
        block = masked_block(presence, blocks, block_cols, a, b)
        held[here, :] = jnp.where(same, block, swapped[here, :])


def pick(presence, blocks, swapped, b):
    return pl.pallas_call(
        functools.partial(pick_kernel, blocks.shape[0] // swapped.shape[0], b),
        out_shape=jax.ShapeDtypeStruct(swapped.shape, jnp.float32),
        in_specs=[WHOLE] * 3,
        out_specs=WHOLE,
        cost_estimate=LIGHT,
        compiler_params=ROOM,
    )(presence, blocks, swapped)


def stacked_kernel(*refs):
    for at, piece in enumerate(refs[:-1]):
        refs[-1][at] = piece[...]


def stacked(pieces):
    return pl.pallas_call(
        stacked_kernel,
        out_shape=jax.ShapeDtypeStruct((len(pieces),) + pieces[0].shape, jnp.float32),
        in_specs=[WHOLE] * len(pieces),
        out_specs=WHOLE,
        cost_estimate=LIGHT,
        compiler_params=ROOM,
    )(*pieces)


def crossed(swap):
    groups_row = lax.axis_size("row")
    groups_col = lax.axis_size("col")
    cross = [
        (r * groups_col + c, (r ^ 1) * groups_col + (c ^ 1))
        for r in range(groups_row)
        for c in range(groups_col)
    ]
    return lax.ppermute(swap, ("row", "col"), cross)


def along_line(mine, order):
    strips, flips = [mine], [0]
    bit = lax.axis_size("row") // 2
    while bit > 1:
        strips = strips + [flipped(strip, "row", bit) for strip in strips]
        flips = flips + [flip ^ bit for flip in flips]
        bit //= 2
    return ordered(strips, tuple(flips), order)


def local(inverse_set, presence, factor, dinv):
    groups_row = lax.axis_size("row")
    groups_col = lax.axis_size("col")
    block_rows, _, order, width = factor.shape
    block_cols = inverse_set.shape[3]
    span = width // groups_col
    rows = block_rows * order
    share = order // groups_col

    own = factor.reshape(rows, width)
    blocks = inverse_set.reshape(rows * block_cols, order)
    marks = presence.reshape(1, -1)
    tall = width // groups_row
    mine, swaps = prepare(marks, blocks, own, span, tall)
    swapped = [crossed(swap) for swap in swaps]
    stay, away, part = halves(own, tall)
    part = flipped(part, "row", 1)
    mate_part = flipped(part, "col", 1)
    columns = along_line(mine, order)
    held = [pick(marks, blocks, swapped[b], b) for b in range(block_cols)]
    far = [(flip, piece) for flip in range(2, groups_col, 2) for piece in held]
    ours = [flipped(piece, "col", flip) for flip, piece in far]
    theirs = [flipped(piece, "col", 1) for piece in ours]
    held, swapped = stacked(held), stacked(swapped)
    mate, mate_swapped = flipped(held, "col", 1), flipped(swapped, "col", 1)

    kept, sent = partials(held, mate, ours, theirs, columns)
    got = flipped(sent, "row", 1)
    terms = diagonal_terms(
        kept, sent, stay, away, swapped, mate_swapped, part, mate_part, dinv
    )
    met = lax.all_to_all(terms.reshape(groups_row, tall, span), "row", 0, 0)
    outward = outward_pieces(kept, got, order, groups_col)
    arrived = [flipped(piece, "col", f) if f else piece for f, piece in enumerate(outward)]
    off_diag, diag_block = close(arrived, met)
    return (off_diag.reshape(block_rows, 1, share, width), diag_block)


def solution(mesh):
    in_specs = (
        P(None, "row", None, None, "col", None),
        P(None, "row", None, "col"),
        P(None, "row", None, None),
        P("row", "col"),
    )
    out_specs = (P(None, "row", "col", None), P("row", "col"))
    return jax.shard_map(local, mesh=mesh, in_specs=in_specs, out_specs=out_specs, check_vma=False)
```

```python
import functools

import jax
import jax.numpy as jnp
from jax import lax
from jax.experimental import pallas as pl
from jax.experimental.pallas import tpu as pltpu
from jax.sharding import PartitionSpec as P

LANES = 128
WHOLE = pl.BlockSpec(memory_space=pltpu.VMEM)
ROOM = pltpu.CompilerParams(vmem_limit_bytes=16 * 1024 * 1024)
HEAVY = 10**8
LIGHT = pl.CostEstimate(flops=1000, bytes_accessed=1000, transcendentals=0)


def flipped(value, axis, flip):
    return lax.ppermute(value, axis, [(i, i ^ flip) for i in range(lax.axis_size(axis))])


def two_parts(value):
    high = value.astype(jnp.bfloat16)
    return high, (value - high.astype(jnp.float32)).astype(jnp.bfloat16)


def product(left, right, contract):
    left_high, left_low = two_parts(left)
    right_high, right_low = two_parts(right)

    def once(a, b):
        return lax.dot_general(a, b, (contract, ((), ())), preferred_element_type=jnp.float32)

    return once(left_high, right_high) + (once(left_high, right_low) + once(left_low, right_high))


def parity_half(factor, tall, parity):
    even, odd = [
        jnp.concatenate(
            [factor[:, i : i + tall] for i in range(first, factor.shape[1], 2 * tall)], axis=1
        )
        for first in (0, tall)
    ]
    return jnp.where(parity == 1, odd, even)


def masked_block(presence, blocks, block_cols, a, b):
    order = blocks.shape[1]
    at = a * block_cols + b
    weight = presence[:, at : at + 1].astype(jnp.float32)
    return blocks[pl.ds(a * order * block_cols + b, order, stride=block_cols), :] * weight


def prepare_kernel(tall, presence, blocks, factor, masked, swap, mine):
    rows, span = mine.shape
    mine[...] = factor[:, pl.ds(pl.multiple_of(lax.axis_index("col") * span, LANES), span)]
    row_bit = lax.axis_index("row") & 1
    same = row_bit == (lax.axis_index("col") & 1)
    block_cols, _, order = masked.shape
    for a in range(rows // order):
        for b in range(block_cols):
            block = masked_block(presence, blocks, block_cols, a, b)
            masked[b, pl.ds(a * order, order), :] = block
    half = parity_half(factor[...], tall, 1 - row_bit)
    for b in range(swap.shape[0]):
        part = half[:, b * order : (b + 1) * order]
        if part.shape[1] and b < block_cols:
            swap[b] = jnp.where(same, part, masked[b])
        else:
            swap[b] = part if part.shape[1] else masked[b]


def prepare(presence, blocks, own, span, tall):
    rows, width = own.shape
    block_cols = blocks.shape[0] // rows
    order = blocks.shape[1]
    depth = max(block_cols, width // 2 // order)
    if span % LANES:
        first = lax.axis_index("col") * span
        row_bit = lax.axis_index("row") & 1
        same = row_bit == (lax.axis_index("col") & 1)
        mine = lax.dynamic_slice_in_dim(own, first, span, 1)
        weights = presence.reshape(-1, 1, block_cols, 1).astype(jnp.float32)
        picked = blocks.reshape(-1, order, block_cols, order) * weights
        masked = picked.transpose(2, 0, 1, 3).reshape(block_cols, rows, order)
        half = parity_half(own, tall, 1 - row_bit).reshape(rows, -1, order).transpose(1, 0, 2)
        half = jnp.pad(half, ((0, depth - half.shape[0]), (0, 0), (0, 0)))
        padded = jnp.pad(masked, ((0, depth - block_cols), (0, 0), (0, 0)))
        return masked, jnp.where(same, half, padded), mine
    return pl.pallas_call(
        functools.partial(prepare_kernel, tall),
        out_shape=(
            jax.ShapeDtypeStruct((block_cols, rows, order), jnp.float32),
            jax.ShapeDtypeStruct((depth, rows, order), jnp.float32),
            jax.ShapeDtypeStruct((rows, span), jnp.float32),
        ),
        in_specs=[WHOLE] * 3,
        out_specs=(WHOLE,) * 3,
        cost_estimate=LIGHT,
    )(presence, blocks, own)


def ordered_kernel(flips, *refs):
    columns = refs[-1]
    _, order, _ = columns.shape
    for flip, strip in zip(flips, refs[:-1]):
        at = (lax.axis_index("row") ^ flip) >> 1
        for a in range(strip.shape[0] // order):
            columns[a * len(flips) + at] = strip[pl.ds(a * order, order), :]


def ordered(strips, flips, order):
    rows, span = strips[0].shape
    return pl.pallas_call(
        functools.partial(ordered_kernel, flips),
        out_shape=jax.ShapeDtypeStruct((rows // order * len(strips), order, span), jnp.float32),
        in_specs=[WHOLE] * len(strips),
        out_specs=WHOLE,
        cost_estimate=pl.CostEstimate(flops=HEAVY, bytes_accessed=1000, transcendentals=0),
        compiler_params=ROOM,
    )(*strips)


def partials_kernel(count, *refs):
    pieces = refs[: 2 * count]
    columns, both = refs[2 * count :]
    block_cols, rows, _ = pieces[0].shape
    col_index = lax.axis_index("col")
    left, right = [], []
    for t in range(count):
        for b in range(block_cols):
            left.append(jnp.concatenate([pieces[t][b], pieces[count + t][b]], axis=0))
            right.append(columns[b * count + ((col_index >> 1) ^ t)])
    summed = product(jnp.concatenate(left, axis=1), jnp.concatenate(right, axis=0), ((1,), (0,)))
    here = (col_index & 1) * rows
    both[pl.ds(pl.multiple_of(here, 8), rows), :] = summed[:rows]
    both[pl.ds(pl.multiple_of(rows - here, 8), rows), :] = summed[rows:]


def partials(pieces, columns):
    rows = pieces[0].shape[1]
    return pl.pallas_call(
        functools.partial(partials_kernel, len(pieces) // 2),
        out_shape=jax.ShapeDtypeStruct((2 * rows, columns.shape[2]), jnp.float32),
        in_specs=[WHOLE] * (len(pieces) + 1),
        out_specs=WHOLE,
        cost_estimate=LIGHT,
        compiler_params=ROOM,
    )(*pieces, columns)


def stay_kernel(tall, own, stay):
    stay[...] = parity_half(own[...], tall, lax.axis_index("row") & 1)


def stay_half(own, tall):
    rows, width = own.shape
    return pl.pallas_call(
        functools.partial(stay_kernel, tall),
        out_shape=jax.ShapeDtypeStruct((rows, width // 2), jnp.float32),
        in_specs=[WHOLE],
        out_specs=WHOLE,
        cost_estimate=LIGHT,
        compiler_params=ROOM,
    )(own)


def finish_kernel(order, flips, both, got, stay, swapped, mate_swapped, dinv, *refs):
    update, terms = refs[-2:]
    along, outward = refs[: len(flips)], refs[len(flips) : -2]
    rows = stay.shape[0]
    row_index = lax.axis_index("row")
    col_index = lax.axis_index("col")
    here = (row_index & 1) * rows
    update[...] = both[...] + got[...]
    mine = update[pl.ds(pl.multiple_of(here, 8), rows), :]
    other = update[pl.ds(pl.multiple_of(rows - here, 8), rows), :]
    same = (row_index & 1) == (col_index & 1)
    depth = stay.shape[1] // swapped.shape[2]
    near = [jnp.where(same, swapped[j], mate_swapped[j]) for j in range(depth)]
    factors = jnp.concatenate([stay[...], jnp.concatenate(near, axis=1)], axis=0)
    terms[...] = product(factors, jnp.concatenate([mine, other], axis=0), ((0,), (0,)))
    tall = dinv.shape[0]
    for flip, piece in zip(flips, along):
        slot = ((row_index ^ flip) >> 1) * tall
        piece[...] = terms[pl.ds(pl.multiple_of(slot, 8), tall), :]
    along[0][...] = along[0][...] + dinv[...]
    share = order // len(outward)
    for flip, piece in enumerate(outward):
        start = here + (col_index ^ flip) * share
        for a in range(rows // order):
            picked = update[pl.ds(pl.multiple_of(a * order + start, 8), share), :]
            piece[pl.ds(a * share, share), :] = -picked


def finish(both, got, stay, swapped, mate_swapped, dinv, order, flips, receivers):
    rows, half = stay.shape
    span = both.shape[1]
    along = (jax.ShapeDtypeStruct(dinv.shape, jnp.float32),) * len(flips)
    outward = (jax.ShapeDtypeStruct((rows // receivers, span), jnp.float32),) * receivers
    outs = pl.pallas_call(
        functools.partial(finish_kernel, order, flips),
        out_shape=along + outward,
        in_specs=[WHOLE] * 6,
        out_specs=(WHOLE,) * (len(flips) + receivers),
        scratch_shapes=[
            pltpu.VMEM((2 * rows, span), jnp.float32),
            pltpu.VMEM((half, span), jnp.float32),
        ],
        cost_estimate=LIGHT,
        compiler_params=ROOM,
    )(both, got, stay, swapped, mate_swapped, dinv)
    return outs[: len(flips)], outs[len(flips) :]


def close_kernel(count, *refs):
    met, arrived = refs[:count], refs[count:-2]
    off_diag, diag_block = refs[-2:]
    span = arrived[0].shape[1]
    for flip, piece in enumerate(arrived):
        first = pl.multiple_of((lax.axis_index("col") ^ flip) * span, LANES)
        off_diag[:, pl.ds(first, span)] = piece[...]
    diag_block[...] = sum([piece[...] for piece in met[1:]], met[0][...])


def close(arrived, met):
    share, span = arrived[0].shape
    if span % LANES:
        me = lax.axis_index("col")
        laid = [lax.select_n(me ^ j, *arrived) for j in range(len(arrived))]
        return jnp.concatenate(laid, axis=1), sum(met[1:], met[0])
    return pl.pallas_call(
        functools.partial(close_kernel, len(met)),
        out_shape=(
            jax.ShapeDtypeStruct((share, span * len(arrived)), jnp.float32),
            jax.ShapeDtypeStruct(met[0].shape, jnp.float32),
        ),
        in_specs=[WHOLE] * (len(arrived) + len(met)),
        out_specs=(WHOLE, WHOLE),
        cost_estimate=LIGHT,
        compiler_params=ROOM,
    )(*met, *arrived)


def pick_kernel(presence, blocks, swapped, held):
    same = (lax.axis_index("row") & 1) == (lax.axis_index("col") & 1)
    block_cols, rows, order = held.shape
    for b in range(block_cols):
        for a in range(rows // order):
            here = pl.ds(a * order, order)
            block = masked_block(presence, blocks, block_cols, a, b)
            held[b, here, :] = jnp.where(same, block, swapped[b, here, :])


def pick(presence, blocks, swapped):
    rows, order = swapped.shape[1:]
    return pl.pallas_call(
        pick_kernel,
        out_shape=jax.ShapeDtypeStruct((blocks.shape[0] // rows, rows, order), jnp.float32),
        in_specs=[WHOLE] * 3,
        out_specs=WHOLE,
        cost_estimate=LIGHT,
        compiler_params=ROOM,
    )(presence, blocks, swapped)


def crossed(swap):
    groups_row = lax.axis_size("row")
    groups_col = lax.axis_size("col")
    cross = [
        (r * groups_col + c, (r ^ 1) * groups_col + (c ^ 1))
        for r in range(groups_row)
        for c in range(groups_col)
    ]
    return lax.ppermute(swap, ("row", "col"), cross)


def routed(masked, turn, flip):
    groups_row = lax.axis_size("row")
    groups_col = lax.axis_size("col")
    pairs = []
    for r in range(groups_row):
        for c in range(groups_col):
            to_row = (r & ~1) | (c & 1)
            to_col = (((c >> 1) ^ turn) << 1) | ((r & 1) ^ flip)
            pairs.append((r * groups_col + c, to_row * groups_col + to_col))
    return lax.ppermute(masked, ("row", "col"), pairs)


def along_line(mine, order):
    strips, flips = [mine], [0]
    bit = lax.axis_size("row") // 2
    while bit > 1:
        strips = strips + [flipped(strip, "row", bit) for strip in strips]
        flips = flips + [flip ^ bit for flip in flips]
        bit //= 2
    return ordered(strips, tuple(flips), order)


def local(inverse_set, presence, factor, dinv):
    groups_row = lax.axis_size("row")
    groups_col = lax.axis_size("col")
    block_rows, _, order, width = factor.shape
    block_cols = inverse_set.shape[3]
    span = width // groups_col
    rows = block_rows * order
    share = order // groups_col

    own = factor.reshape(rows, width)
    blocks = inverse_set.reshape(rows * block_cols, order)
    marks = presence.reshape(1, -1)
    tall = width // groups_row
    masked, swap, mine = prepare(marks, blocks, own, span, tall)
    swapped = crossed(swap)
    stay = stay_half(own, tall)
    columns = along_line(mine, order)
    turns = range(groups_col // 2)
    ours = [routed(masked, turn, 0) for turn in turns if turn]
    theirs = [routed(masked, turn, 1) for turn in turns]
    mate_swapped = flipped(swapped, "col", 1)

    both = partials([pick(marks, blocks, swapped), *ours, *theirs], columns)
    got = flipped(both, "row", 1)
    flips = (0, *range(groups_row - 2, 0, -2))
    along, outward = finish(
        both, got, stay, swapped, mate_swapped, dinv, order, flips, groups_col
    )
    met = [flipped(piece, "row", flip) if flip else piece for flip, piece in zip(flips, along)]
    arrived = [flipped(piece, "col", f) if f else piece for f, piece in enumerate(outward)]
    off_diag, diag_block = close(arrived, met)
    return (off_diag.reshape(block_rows, 1, share, width), diag_block)


def solution(mesh):
    in_specs = (
        P(None, "row", None, None, "col", None),
        P(None, "row", None, "col"),
        P(None, "row", None, None),
        P("row", "col"),
    )
    out_specs = (P(None, "row", "col", None), P("row", "col"))
    return jax.shard_map(local, mesh=mesh, in_specs=in_specs, out_specs=out_specs, check_vma=False)
```

```python
import functools

import jax
import jax.numpy as jnp
from jax import lax
from jax.experimental import pallas as pl
from jax.experimental.pallas import tpu as pltpu
from jax.sharding import PartitionSpec as P

LANES = 128
WHOLE = pl.BlockSpec(memory_space=pltpu.VMEM)
ROOM = pltpu.CompilerParams(vmem_limit_bytes=16 * 1024 * 1024)
HEAVY = 10**8
LIGHT = pl.CostEstimate(flops=1000, bytes_accessed=1000, transcendentals=0)


def flipped(value, axis, flip):
    return lax.ppermute(value, axis, [(i, i ^ flip) for i in range(lax.axis_size(axis))])


def two_parts(value):
    high = value.astype(jnp.bfloat16)
    return high, (value - high.astype(jnp.float32)).astype(jnp.bfloat16)


def product(left, right, contract):
    left_high, left_low = two_parts(left)
    right_high, right_low = two_parts(right)

    def once(a, b):
        return lax.dot_general(a, b, (contract, ((), ())), preferred_element_type=jnp.float32)

    return once(left_high, right_high) + (once(left_high, right_low) + once(left_low, right_high))


def parity_half(factor, tall, parity):
    even, odd = [
        jnp.concatenate(
            [factor[:, i : i + tall] for i in range(first, factor.shape[1], 2 * tall)], axis=1
        )
        for first in (0, tall)
    ]
    return jnp.where(parity == 1, odd, even)


def masked_block(presence, blocks, block_cols, a, b):
    order = blocks.shape[1]
    at = a * block_cols + b
    weight = presence[:, at : at + 1].astype(jnp.float32)
    return blocks[pl.ds(a * order * block_cols + b, order, stride=block_cols), :] * weight


def prepare_kernel(tall, presence, blocks, factor, masked, swap, mine):
    rows, span = mine.shape
    mine[...] = factor[:, pl.ds(pl.multiple_of(lax.axis_index("col") * span, LANES), span)]
    row_bit = lax.axis_index("row") & 1
    same = row_bit == (lax.axis_index("col") & 1)
    block_cols, _, order = masked.shape
    for a in range(rows // order):
        for b in range(block_cols):
            block = masked_block(presence, blocks, block_cols, a, b)
            masked[b, pl.ds(a * order, order), :] = block
    half = parity_half(factor[...], tall, 1 - row_bit)
    for b in range(swap.shape[0]):
        part = half[:, b * order : (b + 1) * order]
        if part.shape[1] and b < block_cols:
            swap[b] = jnp.where(same, part, masked[b])
        else:
            swap[b] = part if part.shape[1] else masked[b]


def prepare(presence, blocks, own, span, tall):
    rows, width = own.shape
    block_cols = blocks.shape[0] // rows
    order = blocks.shape[1]
    depth = max(block_cols, width // 2 // order)
    if span % LANES:
        first = lax.axis_index("col") * span
        row_bit = lax.axis_index("row") & 1
        same = row_bit == (lax.axis_index("col") & 1)
        mine = lax.dynamic_slice_in_dim(own, first, span, 1)
        weights = presence.reshape(-1, 1, block_cols, 1).astype(jnp.float32)
        picked = blocks.reshape(-1, order, block_cols, order) * weights
        masked = picked.transpose(2, 0, 1, 3).reshape(block_cols, rows, order)
        half = parity_half(own, tall, 1 - row_bit).reshape(rows, -1, order).transpose(1, 0, 2)
        half = jnp.pad(half, ((0, depth - half.shape[0]), (0, 0), (0, 0)))
        padded = jnp.pad(masked, ((0, depth - block_cols), (0, 0), (0, 0)))
        return masked, jnp.where(same, half, padded), mine
    return pl.pallas_call(
        functools.partial(prepare_kernel, tall),
        out_shape=(
            jax.ShapeDtypeStruct((block_cols, rows, order), jnp.float32),
            jax.ShapeDtypeStruct((depth, rows, order), jnp.float32),
            jax.ShapeDtypeStruct((rows, span), jnp.float32),
        ),
        in_specs=[WHOLE] * 3,
        out_specs=(WHOLE,) * 3,
        cost_estimate=LIGHT,
    )(presence, blocks, own)


def ordered_kernel(flips, *refs):
    columns = refs[-1]
    _, order, _ = columns.shape
    for flip, strip in zip(flips, refs[:-1]):
        at = (lax.axis_index("row") ^ flip) >> 1
        for a in range(strip.shape[0] // order):
            columns[a * len(flips) + at] = strip[pl.ds(a * order, order), :]


def ordered(strips, flips, order):
    rows, span = strips[0].shape
    return pl.pallas_call(
        functools.partial(ordered_kernel, flips),
        out_shape=jax.ShapeDtypeStruct((rows // order * len(strips), order, span), jnp.float32),
        in_specs=[WHOLE] * len(strips),
        out_specs=WHOLE,
        cost_estimate=pl.CostEstimate(flops=HEAVY, bytes_accessed=1000, transcendentals=0),
        compiler_params=ROOM,
    )(*strips)


def partials_kernel(count, *refs):
    pieces = refs[: 2 * count]
    columns, both = refs[2 * count :]
    block_cols, rows, _ = pieces[0].shape
    col_index = lax.axis_index("col")
    left, right = [], []
    for t in range(count):
        for b in range(block_cols):
            left.append(jnp.concatenate([pieces[t][b], pieces[count + t][b]], axis=0))
            right.append(columns[b * count + ((col_index >> 1) ^ t)])
    summed = product(jnp.concatenate(left, axis=1), jnp.concatenate(right, axis=0), ((1,), (0,)))
    here = (col_index & 1) * rows
    both[pl.ds(pl.multiple_of(here, 8), rows), :] = summed[:rows]
    both[pl.ds(pl.multiple_of(rows - here, 8), rows), :] = summed[rows:]


def partials(pieces, columns):
    rows = pieces[0].shape[1]
    return pl.pallas_call(
        functools.partial(partials_kernel, len(pieces) // 2),
        out_shape=jax.ShapeDtypeStruct((2 * rows, columns.shape[2]), jnp.float32),
        in_specs=[WHOLE] * (len(pieces) + 1),
        out_specs=WHOLE,
        cost_estimate=LIGHT,
        compiler_params=ROOM,
    )(*pieces, columns)


def stay_kernel(tall, own, stay):
    stay[...] = parity_half(own[...], tall, lax.axis_index("row") & 1)


def stay_half(own, tall):
    rows, width = own.shape
    return pl.pallas_call(
        functools.partial(stay_kernel, tall),
        out_shape=jax.ShapeDtypeStruct((rows, width // 2), jnp.float32),
        in_specs=[WHOLE],
        out_specs=WHOLE,
        cost_estimate=LIGHT,
        compiler_params=ROOM,
    )(own)


def finish_kernel(order, flips, both, got, stay, swapped, mate_swapped, dinv, *refs):
    update, terms = refs[-2:]
    along, outward = refs[: len(flips)], refs[len(flips) : -2]
    rows = stay.shape[0]
    row_index = lax.axis_index("row")
    col_index = lax.axis_index("col")
    here = (row_index & 1) * rows
    update[...] = both[...] + got[...]
    mine = update[pl.ds(pl.multiple_of(here, 8), rows), :]
    other = update[pl.ds(pl.multiple_of(rows - here, 8), rows), :]
    same = (row_index & 1) == (col_index & 1)
    depth = stay.shape[1] // swapped.shape[2]
    near = [jnp.where(same, swapped[j], mate_swapped[j]) for j in range(depth)]
    factors = jnp.concatenate([stay[...], jnp.concatenate(near, axis=1)], axis=0)
    terms[...] = product(factors, jnp.concatenate([mine, other], axis=0), ((0,), (0,)))
    tall = dinv.shape[0]
    for flip, piece in zip(flips, along):
        slot = ((row_index ^ flip) >> 1) * tall
        piece[...] = terms[pl.ds(pl.multiple_of(slot, 8), tall), :]
    along[0][...] = along[0][...] + dinv[...]
    share = order // len(outward)
    for flip, piece in enumerate(outward):
        start = here + (col_index ^ flip) * share
        for a in range(rows // order):
            picked = update[pl.ds(pl.multiple_of(a * order + start, 8), share), :]
            piece[pl.ds(a * share, share), :] = -picked


def finish(both, got, stay, swapped, mate_swapped, dinv, order, flips, receivers):
    rows, half = stay.shape
    span = both.shape[1]
    along = (jax.ShapeDtypeStruct(dinv.shape, jnp.float32),) * len(flips)
    outward = (jax.ShapeDtypeStruct((rows // receivers, span), jnp.float32),) * receivers
    outs = pl.pallas_call(
        functools.partial(finish_kernel, order, flips),
        out_shape=along + outward,
        in_specs=[WHOLE] * 6,
        out_specs=(WHOLE,) * (len(flips) + receivers),
        scratch_shapes=[
            pltpu.VMEM((2 * rows, span), jnp.float32),
            pltpu.VMEM((half, span), jnp.float32),
        ],
        cost_estimate=LIGHT,
        compiler_params=ROOM,
    )(both, got, stay, swapped, mate_swapped, dinv)
    return outs[: len(flips)], outs[len(flips) :]


def close_kernel(count, *refs):
    met, arrived = refs[:count], refs[count:-2]
    off_diag, diag_block = refs[-2:]
    span = arrived[0].shape[1]
    for flip, piece in enumerate(arrived):
        first = pl.multiple_of((lax.axis_index("col") ^ flip) * span, LANES)
        off_diag[:, pl.ds(first, span)] = piece[...]
    diag_block[...] = sum([piece[...] for piece in met[1:]], met[0][...])


def close(arrived, met):
    share, span = arrived[0].shape
    if span % LANES:
        me = lax.axis_index("col")
        laid = [lax.select_n(me ^ j, *arrived) for j in range(len(arrived))]
        return jnp.concatenate(laid, axis=1), sum(met[1:], met[0])
    return pl.pallas_call(
        functools.partial(close_kernel, len(met)),
        out_shape=(
            jax.ShapeDtypeStruct((share, span * len(arrived)), jnp.float32),
            jax.ShapeDtypeStruct(met[0].shape, jnp.float32),
        ),
        in_specs=[WHOLE] * (len(arrived) + len(met)),
        out_specs=(WHOLE, WHOLE),
        cost_estimate=LIGHT,
        compiler_params=ROOM,
    )(*met, *arrived)


def pick_kernel(presence, blocks, swapped, held):
    same = (lax.axis_index("row") & 1) == (lax.axis_index("col") & 1)
    block_cols, rows, order = held.shape
    for b in range(block_cols):
        for a in range(rows // order):
            here = pl.ds(a * order, order)
            block = masked_block(presence, blocks, block_cols, a, b)
            held[b, here, :] = jnp.where(same, block, swapped[b, here, :])


def pick(presence, blocks, swapped):
    rows, order = swapped.shape[1:]
    return pl.pallas_call(
        pick_kernel,
        out_shape=jax.ShapeDtypeStruct((blocks.shape[0] // rows, rows, order), jnp.float32),
        in_specs=[WHOLE] * 3,
        out_specs=WHOLE,
        cost_estimate=LIGHT,
        compiler_params=ROOM,
    )(presence, blocks, swapped)


def crossed(swap):
    groups_row = lax.axis_size("row")
    groups_col = lax.axis_size("col")
    cross = [
        (r * groups_col + c, (r ^ 1) * groups_col + (c ^ 1))
        for r in range(groups_row)
        for c in range(groups_col)
    ]
    return lax.ppermute(swap, ("row", "col"), cross)


def routed(masked, turn, flip):
    groups_row = lax.axis_size("row")
    groups_col = lax.axis_size("col")
    pairs = []
    for r in range(groups_row):
        for c in range(groups_col):
            to_row = (r & ~1) | (c & 1)
            to_col = (((c >> 1) ^ turn) << 1) | ((r & 1) ^ flip)
            pairs.append((r * groups_col + c, to_row * groups_col + to_col))
    return lax.ppermute(masked, ("row", "col"), pairs)


def along_line(mine, order):
    strips, flips = [mine], [0]
    bit = lax.axis_size("row") // 2
    while bit > 1:
        strips = strips + [flipped(strip, "row", bit) for strip in strips]
        flips = flips + [flip ^ bit for flip in flips]
        bit //= 2
    return ordered(strips, tuple(flips), order)


def local(inverse_set, presence, factor, dinv):
    groups_row = lax.axis_size("row")
    groups_col = lax.axis_size("col")
    block_rows, _, order, width = factor.shape
    block_cols = inverse_set.shape[3]
    span = width // groups_col
    rows = block_rows * order
    share = order // groups_col

    own = factor.reshape(rows, width)
    blocks = inverse_set.reshape(rows * block_cols, order)
    marks = presence.reshape(1, -1)
    tall = width // groups_row
    masked, swap, mine = prepare(marks, blocks, own, span, tall)
    swapped = crossed(swap)
    stay = stay_half(own, tall)
    columns = along_line(mine, order)
    turns = range(groups_col // 2)
    ours = [routed(masked, turn, 0) for turn in turns if turn]
    theirs = [routed(masked, turn, 1) for turn in turns]
    mate_swapped = flipped(swapped, "col", 1)

    both = partials([pick(marks, blocks, swapped), *ours, *theirs], columns)
    got = flipped(both, "row", 1)
    flips = (0, 2, *range(groups_row - 2, 2, -2))
    along, outward = finish(
        both, got, stay, swapped, mate_swapped, dinv, order, flips, groups_col
    )
    met = [flipped(piece, "row", flip) if flip else piece for flip, piece in zip(flips, along)]
    arrived = [flipped(piece, "col", f) if f else piece for f, piece in enumerate(outward)]
    off_diag, diag_block = close(arrived, met)
    return (off_diag.reshape(block_rows, 1, share, width), diag_block)


def solution(mesh):
    in_specs = (
        P(None, "row", None, None, "col", None),
        P(None, "row", None, "col"),
        P(None, "row", None, None),
        P("row", "col"),
    )
    out_specs = (P(None, "row", "col", None), P("row", "col"))
    return jax.shard_map(local, mesh=mesh, in_specs=in_specs, out_specs=out_specs, check_vma=False)
```

```python
import functools

import jax
import jax.numpy as jnp
from jax import lax
from jax.experimental import pallas as pl
from jax.experimental.pallas import tpu as pltpu
from jax.sharding import PartitionSpec as P

LANES = 128
WHOLE = pl.BlockSpec(memory_space=pltpu.VMEM)
ROOM = pltpu.CompilerParams(vmem_limit_bytes=16 * 1024 * 1024)
HEAVY = 6 * 10**8
LIGHT = pl.CostEstimate(flops=1000, bytes_accessed=1000, transcendentals=0)


def flipped(value, axis, flip):
    return lax.ppermute(value, axis, [(i, i ^ flip) for i in range(lax.axis_size(axis))])


def two_parts(value):
    high = value.astype(jnp.bfloat16)
    return high, (value - high.astype(jnp.float32)).astype(jnp.bfloat16)


def product(left, right, contract):
    left_high, left_low = two_parts(left)
    right_high, right_low = two_parts(right)

    def once(a, b):
        return lax.dot_general(a, b, (contract, ((), ())), preferred_element_type=jnp.float32)

    return once(left_high, right_high) + (once(left_high, right_low) + once(left_low, right_high))


def parity_half(factor, tall, parity):
    even, odd = [
        jnp.concatenate(
            [factor[:, i : i + tall] for i in range(first, factor.shape[1], 2 * tall)], axis=1
        )
        for first in (0, tall)
    ]
    return jnp.where(parity == 1, odd, even)


def masked_block(presence, blocks, block_cols, a, b):
    order = blocks.shape[1]
    at = a * block_cols + b
    weight = presence[:, at : at + 1].astype(jnp.float32)
    return blocks[pl.ds(a * order * block_cols + b, order, stride=block_cols), :] * weight


def prepare_kernel(tall, presence, blocks, factor, mine, *swaps):
    rows, span = mine.shape
    mine[...] = factor[:, pl.ds(pl.multiple_of(lax.axis_index("col") * span, LANES), span)]
    row_bit = lax.axis_index("row") & 1
    same = row_bit == (lax.axis_index("col") & 1)
    order = blocks.shape[1]
    block_cols = blocks.shape[0] // rows
    half = parity_half(factor[...], tall, 1 - row_bit)
    for b, swap in enumerate(swaps):
        for a in range(rows // order):
            here = pl.ds(a * order, order)
            part = half[a * order : (a + 1) * order, b * order : (b + 1) * order]
            if b >= block_cols:
                swap[here, :] = part
                continue
            block = masked_block(presence, blocks, block_cols, a, b)
            swap[here, :] = jnp.where(same, part, block) if part.shape[1] else block


def prepare(presence, blocks, own, span, tall):
    rows, width = own.shape
    block_cols = blocks.shape[0] // rows
    order = blocks.shape[1]
    depth = max(block_cols, width // 2 // order)
    if span % LANES:
        first = lax.axis_index("col") * span
        row_bit = lax.axis_index("row") & 1
        same = row_bit == (lax.axis_index("col") & 1)
        mine = lax.dynamic_slice_in_dim(own, first, span, 1)
        weights = presence.reshape(-1, 1, block_cols, 1).astype(jnp.float32)
        picked = blocks.reshape(-1, order, block_cols, order) * weights
        masked = picked.transpose(2, 0, 1, 3).reshape(block_cols, rows, order)
        half = parity_half(own, tall, 1 - row_bit).reshape(rows, -1, order).transpose(1, 0, 2)
        half = jnp.pad(half, ((0, depth - half.shape[0]), (0, 0), (0, 0)))
        padded = jnp.pad(masked, ((0, depth - block_cols), (0, 0), (0, 0)))
        return mine, list(jnp.where(same, half, padded))
    mine, *swaps = pl.pallas_call(
        functools.partial(prepare_kernel, tall),
        out_shape=(jax.ShapeDtypeStruct((rows, span), jnp.float32),)
        + (jax.ShapeDtypeStruct((rows, order), jnp.float32),) * depth,
        in_specs=[WHOLE] * 3,
        out_specs=(WHOLE,) * (1 + depth),
        cost_estimate=LIGHT,
    )(presence, blocks, own)
    return mine, swaps


def ordered_kernel(flips, *refs):
    columns = refs[-1]
    _, order, _ = columns.shape
    for flip, strip in zip(flips, refs[:-1]):
        at = (lax.axis_index("row") ^ flip) >> 1
        for a in range(strip.shape[0] // order):
            columns[a * len(flips) + at] = strip[pl.ds(a * order, order), :]


def ordered(strips, flips, order):
    rows, span = strips[0].shape
    return pl.pallas_call(
        functools.partial(ordered_kernel, flips),
        out_shape=jax.ShapeDtypeStruct((rows // order * len(strips), order, span), jnp.float32),
        in_specs=[WHOLE] * len(strips),
        out_specs=WHOLE,
        cost_estimate=pl.CostEstimate(flops=HEAVY, bytes_accessed=1000, transcendentals=0),
        compiler_params=ROOM,
    )(*strips)


def passed_kernel(strip, _, out):
    out[...] = strip[...]


def passed(strip, earlier):
    return pl.pallas_call(
        passed_kernel,
        out_shape=jax.ShapeDtypeStruct(strip.shape, strip.dtype),
        in_specs=[WHOLE, pl.BlockSpec(memory_space=pl.ANY)],
        out_specs=WHOLE,
        cost_estimate=LIGHT,
        compiler_params=ROOM,
    )(strip, earlier)


def partials_kernel(count, *refs):
    held, mate = refs[:2]
    block_cols, rows, order = held.shape
    far = (count - 1) * block_cols
    ours, theirs, refs = refs[2 : 2 + far], refs[2 + far : 2 + 2 * far], refs[2 + 2 * far :]
    columns, both = refs
    col_index = lax.axis_index("col")
    left, right = [], []
    for t in range(count):
        for b in range(block_cols):
            if t:
                at = (t - 1) * block_cols + b
                pair = [ours[at][...], theirs[at][...]]
            else:
                pair = [held[b], mate[b]]
            left.append(jnp.concatenate(pair, axis=0))
            right.append(columns[b * count + ((col_index >> 1) ^ t)])
    summed = product(jnp.concatenate(left, axis=1), jnp.concatenate(right, axis=0), ((1,), (0,)))
    here = (col_index & 1) * rows
    both[pl.ds(pl.multiple_of(here, 8), rows), :] = summed[:rows]
    both[pl.ds(pl.multiple_of(rows - here, 8), rows), :] = summed[rows:]


def partials(held, mate, ours, theirs, columns):
    block_cols, rows, _ = held.shape
    operands = (held, mate, *ours, *theirs, columns)
    return pl.pallas_call(
        functools.partial(partials_kernel, 1 + len(ours) // block_cols),
        out_shape=jax.ShapeDtypeStruct((2 * rows, columns.shape[2]), jnp.float32),
        in_specs=[WHOLE] * len(operands),
        out_specs=WHOLE,
        cost_estimate=LIGHT,
        compiler_params=ROOM,
    )(*operands)


def stay_kernel(tall, own, stay):
    stay[...] = parity_half(own[...], tall, lax.axis_index("row") & 1)


def stay_half(own, tall):
    rows, width = own.shape
    return pl.pallas_call(
        functools.partial(stay_kernel, tall),
        out_shape=jax.ShapeDtypeStruct((rows, width // 2), jnp.float32),
        in_specs=[WHOLE],
        out_specs=WHOLE,
        cost_estimate=LIGHT,
        compiler_params=ROOM,
    )(own)


def finish_kernel(order, flips, both, got, stay, swapped, mate_swapped, dinv, *refs):
    update, terms = refs[-2:]
    along, outward = refs[: len(flips)], refs[len(flips) : -2]
    rows = stay.shape[0]
    row_index = lax.axis_index("row")
    col_index = lax.axis_index("col")
    here = (row_index & 1) * rows
    update[...] = both[...] + got[...]
    mine = update[pl.ds(pl.multiple_of(here, 8), rows), :]
    other = update[pl.ds(pl.multiple_of(rows - here, 8), rows), :]
    same = (row_index & 1) == (col_index & 1)
    depth = stay.shape[1] // swapped.shape[2]
    near = [jnp.where(same, swapped[j], mate_swapped[j]) for j in range(depth)]
    factors = jnp.concatenate([stay[...], jnp.concatenate(near, axis=1)], axis=0)
    terms[...] = product(factors, jnp.concatenate([mine, other], axis=0), ((0,), (0,)))
    tall = dinv.shape[0]
    for flip, piece in zip(flips, along):
        slot = ((row_index ^ flip) >> 1) * tall
        piece[...] = terms[pl.ds(pl.multiple_of(slot, 8), tall), :]
    along[0][...] = along[0][...] + dinv[...]
    share = order // len(outward)
    for flip, piece in enumerate(outward):
        start = here + (col_index ^ flip) * share
        for a in range(rows // order):
            picked = update[pl.ds(pl.multiple_of(a * order + start, 8), share), :]
            piece[pl.ds(a * share, share), :] = -picked


def finish(both, got, stay, swapped, mate_swapped, dinv, order, flips, receivers):
    rows, half = stay.shape
    span = both.shape[1]
    along = (jax.ShapeDtypeStruct(dinv.shape, jnp.float32),) * len(flips)
    outward = (jax.ShapeDtypeStruct((rows // receivers, span), jnp.float32),) * receivers
    outs = pl.pallas_call(
        functools.partial(finish_kernel, order, flips),
        out_shape=along + outward,
        in_specs=[WHOLE] * 6,
        out_specs=(WHOLE,) * (len(flips) + receivers),
        scratch_shapes=[
            pltpu.VMEM((2 * rows, span), jnp.float32),
            pltpu.VMEM((half, span), jnp.float32),
        ],
        cost_estimate=LIGHT,
        compiler_params=ROOM,
    )(both, got, stay, swapped, mate_swapped, dinv)
    return outs[: len(flips)], outs[len(flips) :]


def close_kernel(count, *refs):
    met, arrived = refs[:count], refs[count:-2]
    off_diag, diag_block = refs[-2:]
    span = arrived[0].shape[1]
    for flip, piece in enumerate(arrived):
        first = pl.multiple_of((lax.axis_index("col") ^ flip) * span, LANES)
        off_diag[:, pl.ds(first, span)] = piece[...]
    diag_block[...] = sum([piece[...] for piece in met[1:]], met[0][...])


def close(arrived, met):
    share, span = arrived[0].shape
    if span % LANES:
        me = lax.axis_index("col")
        laid = [lax.select_n(me ^ j, *arrived) for j in range(len(arrived))]
        return jnp.concatenate(laid, axis=1), sum(met[1:], met[0])
    return pl.pallas_call(
        functools.partial(close_kernel, len(met)),
        out_shape=(
            jax.ShapeDtypeStruct((share, span * len(arrived)), jnp.float32),
            jax.ShapeDtypeStruct(met[0].shape, jnp.float32),
        ),
        in_specs=[WHOLE] * (len(arrived) + len(met)),
        out_specs=(WHOLE, WHOLE),
        cost_estimate=LIGHT,
        compiler_params=ROOM,
    )(*met, *arrived)


def pick_kernel(block_cols, b, presence, blocks, swapped, held):
    same = (lax.axis_index("row") & 1) == (lax.axis_index("col") & 1)
    rows, order = held.shape
    for a in range(rows // order):
        here = pl.ds(a * order, order)
        block = masked_block(presence, blocks, block_cols, a, b)
        held[here, :] = jnp.where(same, block, swapped[here, :])


def pick(presence, blocks, swapped, b):
    return pl.pallas_call(
        functools.partial(pick_kernel, blocks.shape[0] // swapped.shape[0], b),
        out_shape=jax.ShapeDtypeStruct(swapped.shape, jnp.float32),
        in_specs=[WHOLE] * 3,
        out_specs=WHOLE,
        cost_estimate=LIGHT,
        compiler_params=ROOM,
    )(presence, blocks, swapped)


def stacked_kernel(*refs):
    for at, piece in enumerate(refs[:-1]):
        refs[-1][at] = piece[...]


def stacked(pieces):
    return pl.pallas_call(
        stacked_kernel,
        out_shape=jax.ShapeDtypeStruct((len(pieces),) + pieces[0].shape, jnp.float32),
        in_specs=[WHOLE] * len(pieces),
        out_specs=WHOLE,
        cost_estimate=LIGHT,
        compiler_params=ROOM,
    )(*pieces)


def crossed(swap):
    groups_row = lax.axis_size("row")
    groups_col = lax.axis_size("col")
    cross = [
        (r * groups_col + c, (r ^ 1) * groups_col + (c ^ 1))
        for r in range(groups_row)
        for c in range(groups_col)
    ]
    return lax.ppermute(swap, ("row", "col"), cross)


def along_line(mine, order, earlier):
    strips, flips = [mine], [0]
    bit = lax.axis_size("row") // 2
    while bit > 1:
        strips = strips + [flipped(strip, "row", bit) for strip in strips]
        strips[0] = passed(mine, earlier)
        flips = flips + [flip ^ bit for flip in flips]
        bit //= 2
    return ordered(strips, tuple(flips), order)


def local(inverse_set, presence, factor, dinv):
    groups_row = lax.axis_size("row")
    groups_col = lax.axis_size("col")
    block_rows, _, order, width = factor.shape
    block_cols = inverse_set.shape[3]
    span = width // groups_col
    rows = block_rows * order
    share = order // groups_col

    own = factor.reshape(rows, width)
    blocks = inverse_set.reshape(rows * block_cols, order)
    marks = presence.reshape(1, -1)
    tall = width // groups_row
    mine, swaps = prepare(marks, blocks, own, span, tall)
    swapped = [crossed(swap) for swap in swaps]
    stay = stay_half(own, tall)
    held = [pick(marks, blocks, swapped[b], b) for b in range(block_cols)]
    far = [(flip, piece) for flip in range(2, groups_col, 2) for piece in held]
    ours = [flipped(piece, "col", flip) for flip, piece in far]
    theirs = [flipped(piece, "col", 1) for piece in ours]
    held, swapped = stacked(held), stacked(swapped)
    columns = along_line(mine, order, held)
    mate, mate_swapped = flipped(held, "col", 1), flipped(swapped, "col", 1)

    both = partials(held, mate, ours, theirs, columns)
    got = flipped(both, "row", 1)
    flips = (0, *range(groups_row - 2, 0, -2))
    along, outward = finish(
        both, got, stay, swapped, mate_swapped, dinv, order, flips, groups_col
    )
    met = [flipped(piece, "row", flip) if flip else piece for flip, piece in zip(flips, along)]
    arrived = [flipped(piece, "col", f) if f else piece for f, piece in enumerate(outward)]
    off_diag, diag_block = close(arrived, met)
    return (off_diag.reshape(block_rows, 1, share, width), diag_block)


def solution(mesh):
    in_specs = (
        P(None, "row", None, None, "col", None),
        P(None, "row", None, "col"),
        P(None, "row", None, None),
        P("row", "col"),
    )
    out_specs = (P(None, "row", "col", None), P("row", "col"))
    return jax.shard_map(local, mesh=mesh, in_specs=in_specs, out_specs=out_specs, check_vma=False)
```

```python
import functools

import jax
import jax.numpy as jnp
from jax import lax
from jax.experimental import pallas as pl
from jax.experimental.pallas import tpu as pltpu
from jax.sharding import PartitionSpec as P

LANES = 128
WHOLE = pl.BlockSpec(memory_space=pltpu.VMEM)
ROOM = pltpu.CompilerParams(vmem_limit_bytes=16 * 1024 * 1024)
HEAVY = 10**9
LIGHT = pl.CostEstimate(flops=1000, bytes_accessed=1000, transcendentals=0)


def flipped(value, axis, flip):
    return lax.ppermute(value, axis, [(i, i ^ flip) for i in range(lax.axis_size(axis))])


def two_parts(value):
    high = value.astype(jnp.bfloat16)
    return high, (value - high.astype(jnp.float32)).astype(jnp.bfloat16)


def product(left, right, contract):
    left_high, left_low = two_parts(left)
    right_high, right_low = two_parts(right)

    def once(a, b):
        return lax.dot_general(a, b, (contract, ((), ())), preferred_element_type=jnp.float32)

    return once(left_high, right_high) + (once(left_high, right_low) + once(left_low, right_high))


def parity_half(factor, tall, parity):
    even, odd = [
        jnp.concatenate(
            [factor[:, i : i + tall] for i in range(first, factor.shape[1], 2 * tall)], axis=1
        )
        for first in (0, tall)
    ]
    return jnp.where(parity == 1, odd, even)


def masked_block(presence, blocks, block_cols, a, b):
    order = blocks.shape[1]
    at = a * block_cols + b
    weight = presence[:, at : at + 1].astype(jnp.float32)
    return blocks[pl.ds(a * order * block_cols + b, order, stride=block_cols), :] * weight


def prepare_kernel(tall, presence_at, blocks_at, factor_at, mine_at, *refs):
    count = (len(refs) - 5) // 2
    swaps_at, (presence, blocks, factor, mine) = refs[:count], refs[count : count + 4]
    swaps, sems = refs[count + 4 : -1], refs[-1]
    sources = (presence_at, blocks_at, factor_at, mine, *swaps)
    targets = (presence, blocks, factor, mine_at, *swaps_at)
    moves = [
        pltpu.make_async_copy(source, target, sems.at[i])
        for i, (source, target) in enumerate(zip(sources, targets))
    ]
    for move in moves[:3]:
        move.start()
    rows, span = mine.shape
    row_bit = lax.axis_index("row") & 1
    same = row_bit == (lax.axis_index("col") & 1)
    order = blocks.shape[1]
    block_cols = blocks.shape[0] // rows
    moves[2].wait()
    mine[...] = factor[:, pl.ds(pl.multiple_of(lax.axis_index("col") * span, LANES), span)]
    moves[3].start()
    half = parity_half(factor[...], tall, 1 - row_bit)
    moves[0].wait()
    moves[1].wait()
    for b, swap in enumerate(swaps):
        for a in range(rows // order):
            here = pl.ds(a * order, order)
            part = half[a * order : (a + 1) * order, b * order : (b + 1) * order]
            if b >= block_cols:
                swap[here, :] = part
                continue
            block = masked_block(presence, blocks, block_cols, a, b)
            swap[here, :] = jnp.where(same, part, block) if part.shape[1] else block
        moves[4 + b].start()
    for move in moves[3:]:
        move.wait()


def prepare(presence, blocks, own, span, tall):
    rows, width = own.shape
    block_cols = blocks.shape[0] // rows
    order = blocks.shape[1]
    depth = max(block_cols, width // 2 // order)
    if span % LANES:
        first = lax.axis_index("col") * span
        row_bit = lax.axis_index("row") & 1
        same = row_bit == (lax.axis_index("col") & 1)
        mine = lax.dynamic_slice_in_dim(own, first, span, 1)
        weights = presence.reshape(-1, 1, block_cols, 1).astype(jnp.float32)
        picked = blocks.reshape(-1, order, block_cols, order) * weights
        masked = picked.transpose(2, 0, 1, 3).reshape(block_cols, rows, order)
        half = parity_half(own, tall, 1 - row_bit).reshape(rows, -1, order).transpose(1, 0, 2)
        half = jnp.pad(half, ((0, depth - half.shape[0]), (0, 0), (0, 0)))
        padded = jnp.pad(masked, ((0, depth - block_cols), (0, 0), (0, 0)))
        return mine, list(jnp.where(same, half, padded))
    part = pltpu.VMEM((rows, order), jnp.float32)
    anywhere = pl.BlockSpec(memory_space=pl.ANY)
    mine, *swaps = pl.pallas_call(
        functools.partial(prepare_kernel, tall),
        out_shape=(jax.ShapeDtypeStruct((rows, span), jnp.float32),)
        + (jax.ShapeDtypeStruct((rows, order), jnp.float32),) * depth,
        in_specs=[anywhere] * 3,
        out_specs=(anywhere,) * (1 + depth),
        scratch_shapes=[
            pltpu.VMEM(presence.shape, jnp.int32),
            pltpu.VMEM(blocks.shape, jnp.float32),
            pltpu.VMEM(own.shape, jnp.float32),
            pltpu.VMEM((rows, span), jnp.float32),
            *[part] * depth,
            pltpu.SemaphoreType.DMA((4 + depth,)),
        ],
        cost_estimate=LIGHT,
    )(presence, blocks, own)
    return mine, swaps


def ordered_kernel(flips, *refs):
    columns = refs[-1]
    _, order, _ = columns.shape
    for flip, strip in zip(flips, refs[:-1]):
        at = (lax.axis_index("row") ^ flip) >> 1
        for a in range(strip.shape[0] // order):
            columns[a * len(flips) + at] = strip[pl.ds(a * order, order), :]


def ordered(strips, flips, order):
    rows, span = strips[0].shape
    return pl.pallas_call(
        functools.partial(ordered_kernel, flips),
        out_shape=jax.ShapeDtypeStruct((rows // order * len(strips), order, span), jnp.float32),
        in_specs=[WHOLE] * len(strips),
        out_specs=WHOLE,
        cost_estimate=pl.CostEstimate(flops=HEAVY, bytes_accessed=1000, transcendentals=0),
        compiler_params=ROOM,
    )(*strips)


def partials_kernel(count, *refs):
    held, mate = refs[:2]
    block_cols, rows, order = held.shape
    far = (count - 1) * block_cols
    ours, theirs, refs = refs[2 : 2 + far], refs[2 + far : 2 + 2 * far], refs[2 + 2 * far :]
    columns, both = refs
    col_index = lax.axis_index("col")
    left, right = [], []
    for t in range(count):
        for b in range(block_cols):
            if t:
                at = (t - 1) * block_cols + b
                pair = [ours[at][...], theirs[at][...]]
            else:
                pair = [held[b], mate[b]]
            left.append(jnp.concatenate(pair, axis=0))
            right.append(columns[b * count + ((col_index >> 1) ^ t)])
    summed = product(jnp.concatenate(left, axis=1), jnp.concatenate(right, axis=0), ((1,), (0,)))
    here = (col_index & 1) * rows
    both[pl.ds(pl.multiple_of(here, 8), rows), :] = summed[:rows]
    both[pl.ds(pl.multiple_of(rows - here, 8), rows), :] = summed[rows:]


def partials(held, mate, ours, theirs, columns):
    block_cols, rows, _ = held.shape
    operands = (held, mate, *ours, *theirs, columns)
    return pl.pallas_call(
        functools.partial(partials_kernel, 1 + len(ours) // block_cols),
        out_shape=jax.ShapeDtypeStruct((2 * rows, columns.shape[2]), jnp.float32),
        in_specs=[WHOLE] * len(operands),
        out_specs=WHOLE,
        cost_estimate=LIGHT,
        compiler_params=ROOM,
    )(*operands)


def stay_kernel(tall, own, stay):
    stay[...] = parity_half(own[...], tall, lax.axis_index("row") & 1)


def stay_half(own, tall):
    rows, width = own.shape
    return pl.pallas_call(
        functools.partial(stay_kernel, tall),
        out_shape=jax.ShapeDtypeStruct((rows, width // 2), jnp.float32),
        in_specs=[WHOLE],
        out_specs=WHOLE,
        cost_estimate=LIGHT,
        compiler_params=ROOM,
    )(own)


def finish_kernel(order, flips, both, got, stay, swapped, mate_swapped, dinv, *refs):
    update, terms = refs[-2:]
    along, outward = refs[: len(flips)], refs[len(flips) : -2]
    rows = stay.shape[0]
    row_index = lax.axis_index("row")
    col_index = lax.axis_index("col")
    here = (row_index & 1) * rows
    update[...] = both[...] + got[...]
    mine = update[pl.ds(pl.multiple_of(here, 8), rows), :]
    other = update[pl.ds(pl.multiple_of(rows - here, 8), rows), :]
    same = (row_index & 1) == (col_index & 1)
    depth = stay.shape[1] // swapped.shape[2]
    near = [jnp.where(same, swapped[j], mate_swapped[j]) for j in range(depth)]
    factors = jnp.concatenate([stay[...], jnp.concatenate(near, axis=1)], axis=0)
    terms[...] = product(factors, jnp.concatenate([mine, other], axis=0), ((0,), (0,)))
    tall = dinv.shape[0]
    for flip, piece in zip(flips, along):
        slot = ((row_index ^ flip) >> 1) * tall
        piece[...] = terms[pl.ds(pl.multiple_of(slot, 8), tall), :]
    along[0][...] = along[0][...] + dinv[...]
    share = order // len(outward)
    for flip, piece in enumerate(outward):
        start = here + (col_index ^ flip) * share
        for a in range(rows // order):
            picked = update[pl.ds(pl.multiple_of(a * order + start, 8), share), :]
            piece[pl.ds(a * share, share), :] = -picked


def finish(both, got, stay, swapped, mate_swapped, dinv, order, flips, receivers):
    rows, half = stay.shape
    span = both.shape[1]
    along = (jax.ShapeDtypeStruct(dinv.shape, jnp.float32),) * len(flips)
    outward = (jax.ShapeDtypeStruct((rows // receivers, span), jnp.float32),) * receivers
    outs = pl.pallas_call(
        functools.partial(finish_kernel, order, flips),
        out_shape=along + outward,
        in_specs=[WHOLE] * 6,
        out_specs=(WHOLE,) * (len(flips) + receivers),
        scratch_shapes=[
            pltpu.VMEM((2 * rows, span), jnp.float32),
            pltpu.VMEM((half, span), jnp.float32),
        ],
        cost_estimate=LIGHT,
        compiler_params=ROOM,
    )(both, got, stay, swapped, mate_swapped, dinv)
    return outs[: len(flips)], outs[len(flips) :]


def close_kernel(count, *refs):
    met, arrived = refs[:count], refs[count:-2]
    off_diag, diag_block = refs[-2:]
    span = arrived[0].shape[1]
    for flip, piece in enumerate(arrived):
        first = pl.multiple_of((lax.axis_index("col") ^ flip) * span, LANES)
        off_diag[:, pl.ds(first, span)] = piece[...]
    diag_block[...] = sum([piece[...] for piece in met[1:]], met[0][...])


def close(arrived, met):
    share, span = arrived[0].shape
    if span % LANES:
        me = lax.axis_index("col")
        laid = [lax.select_n(me ^ j, *arrived) for j in range(len(arrived))]
        return jnp.concatenate(laid, axis=1), sum(met[1:], met[0])
    return pl.pallas_call(
        functools.partial(close_kernel, len(met)),
        out_shape=(
            jax.ShapeDtypeStruct((share, span * len(arrived)), jnp.float32),
            jax.ShapeDtypeStruct(met[0].shape, jnp.float32),
        ),
        in_specs=[WHOLE] * (len(arrived) + len(met)),
        out_specs=(WHOLE, WHOLE),
        cost_estimate=LIGHT,
        compiler_params=ROOM,
    )(*met, *arrived)


def pick_kernel(block_cols, b, presence, blocks, swapped, held):
    same = (lax.axis_index("row") & 1) == (lax.axis_index("col") & 1)
    rows, order = held.shape
    for a in range(rows // order):
        here = pl.ds(a * order, order)
        block = masked_block(presence, blocks, block_cols, a, b)
        held[here, :] = jnp.where(same, block, swapped[here, :])


def pick(presence, blocks, swapped, b):
    return pl.pallas_call(
        functools.partial(pick_kernel, blocks.shape[0] // swapped.shape[0], b),
        out_shape=jax.ShapeDtypeStruct(swapped.shape, jnp.float32),
        in_specs=[WHOLE] * 3,
        out_specs=WHOLE,
        cost_estimate=LIGHT,
        compiler_params=ROOM,
    )(presence, blocks, swapped)


def stacked_kernel(*refs):
    for at, piece in enumerate(refs[:-1]):
        refs[-1][at] = piece[...]


def stacked(pieces):
    return pl.pallas_call(
        stacked_kernel,
        out_shape=jax.ShapeDtypeStruct((len(pieces),) + pieces[0].shape, jnp.float32),
        in_specs=[WHOLE] * len(pieces),
        out_specs=WHOLE,
        cost_estimate=LIGHT,
        compiler_params=ROOM,
    )(*pieces)


def crossed(swap):
    groups_row = lax.axis_size("row")
    groups_col = lax.axis_size("col")
    cross = [
        (r * groups_col + c, (r ^ 1) * groups_col + (c ^ 1))
        for r in range(groups_row)
        for c in range(groups_col)
    ]
    return lax.ppermute(swap, ("row", "col"), cross)


def along_line(mine, order):
    strips, flips = [mine], [0]
    bit = lax.axis_size("row") // 2
    while bit > 1:
        strips = strips + [flipped(strip, "row", bit) for strip in strips]
        flips = flips + [flip ^ bit for flip in flips]
        bit //= 2
    return ordered(strips, tuple(flips), order)


def local(inverse_set, presence, factor, dinv):
    groups_row = lax.axis_size("row")
    groups_col = lax.axis_size("col")
    block_rows, _, order, width = factor.shape
    block_cols = inverse_set.shape[3]
    span = width // groups_col
    rows = block_rows * order
    share = order // groups_col

    own = factor.reshape(rows, width)
    blocks = inverse_set.reshape(rows * block_cols, order)
    marks = presence.reshape(1, -1)
    tall = width // groups_row
    mine, swaps = prepare(marks, blocks, own, span, tall)
    swapped = [crossed(swap) for swap in swaps]
    stay = stay_half(own, tall)
    columns = along_line(mine, order)
    held = [pick(marks, blocks, swapped[b], b) for b in range(block_cols)]
    far = [(flip, piece) for flip in range(2, groups_col, 2) for piece in held]
    ours = [flipped(piece, "col", flip) for flip, piece in far]
    theirs = [flipped(piece, "col", 1) for piece in ours]
    held, swapped = stacked(held), stacked(swapped)
    mate, mate_swapped = flipped(held, "col", 1), flipped(swapped, "col", 1)

    both = partials(held, mate, ours, theirs, columns)
    got = flipped(both, "row", 1)
    flips = (0, *range(groups_row - 2, 0, -2))
    along, outward = finish(
        both, got, stay, swapped, mate_swapped, dinv, order, flips, groups_col
    )
    met = [flipped(piece, "row", flip) if flip else piece for flip, piece in zip(flips, along)]
    arrived = [flipped(piece, "col", f) if f else piece for f, piece in enumerate(outward)]
    off_diag, diag_block = close(arrived, met)
    return (off_diag.reshape(block_rows, 1, share, width), diag_block)


def solution(mesh):
    in_specs = (
        P(None, "row", None, None, "col", None),
        P(None, "row", None, "col"),
        P(None, "row", None, None),
        P("row", "col"),
    )
    out_specs = (P(None, "row", "col", None), P("row", "col"))
    return jax.shard_map(local, mesh=mesh, in_specs=in_specs, out_specs=out_specs, check_vma=False)
```

```python
import functools

import jax
import jax.numpy as jnp
from jax import lax
from jax.experimental import pallas as pl
from jax.experimental.pallas import tpu as pltpu
from jax.sharding import PartitionSpec as P

LANES = 128
WHOLE = pl.BlockSpec(memory_space=pltpu.VMEM)
ROOM = pltpu.CompilerParams(vmem_limit_bytes=16 * 1024 * 1024)
HEAVY = 10**9
LIGHT = pl.CostEstimate(flops=1000, bytes_accessed=1000, transcendentals=0)


def flipped(value, axis, flip):
    return lax.ppermute(value, axis, [(i, i ^ flip) for i in range(lax.axis_size(axis))])


def two_parts(value):
    high = value.astype(jnp.bfloat16)
    return high, (value - high.astype(jnp.float32)).astype(jnp.bfloat16)


def product(left, right, contract):
    left_high, left_low = two_parts(left)
    right_high, right_low = two_parts(right)

    def once(a, b):
        return lax.dot_general(a, b, (contract, ((), ())), preferred_element_type=jnp.float32)

    return once(left_high, right_high) + (once(left_high, right_low) + once(left_low, right_high))


def parity_half(factor, tall, parity):
    even, odd = [
        jnp.concatenate(
            [factor[:, i : i + tall] for i in range(first, factor.shape[1], 2 * tall)], axis=1
        )
        for first in (0, tall)
    ]
    return jnp.where(parity == 1, odd, even)


def masked_block(presence, blocks, block_cols, a, b):
    order = blocks.shape[1]
    at = a * block_cols + b
    weight = presence[:, at : at + 1].astype(jnp.float32)
    return blocks[pl.ds(a * order * block_cols + b, order, stride=block_cols), :] * weight


def prepare_kernel(tall, presence, blocks, factor, mine, *swaps):
    rows, span = mine.shape
    mine[...] = factor[:, pl.ds(pl.multiple_of(lax.axis_index("col") * span, LANES), span)]
    row_bit = lax.axis_index("row") & 1
    same = row_bit == (lax.axis_index("col") & 1)
    order = blocks.shape[1]
    block_cols = blocks.shape[0] // rows
    half = parity_half(factor[...], tall, 1 - row_bit)
    for b, swap in enumerate(swaps):
        for a in range(rows // order):
            here = pl.ds(a * order, order)
            part = half[a * order : (a + 1) * order, b * order : (b + 1) * order]
            if b >= block_cols:
                swap[here, :] = part
                continue
            block = masked_block(presence, blocks, block_cols, a, b)
            swap[here, :] = jnp.where(same, part, block) if part.shape[1] else block


def prepare(presence, blocks, own, span, tall):
    rows, width = own.shape
    block_cols = blocks.shape[0] // rows
    order = blocks.shape[1]
    depth = max(block_cols, width // 2 // order)
    if span % LANES:
        first = lax.axis_index("col") * span
        row_bit = lax.axis_index("row") & 1
        same = row_bit == (lax.axis_index("col") & 1)
        mine = lax.dynamic_slice_in_dim(own, first, span, 1)
        weights = presence.reshape(-1, 1, block_cols, 1).astype(jnp.float32)
        picked = blocks.reshape(-1, order, block_cols, order) * weights
        masked = picked.transpose(2, 0, 1, 3).reshape(block_cols, rows, order)
        half = parity_half(own, tall, 1 - row_bit).reshape(rows, -1, order).transpose(1, 0, 2)
        half = jnp.pad(half, ((0, depth - half.shape[0]), (0, 0), (0, 0)))
        padded = jnp.pad(masked, ((0, depth - block_cols), (0, 0), (0, 0)))
        return mine, list(jnp.where(same, half, padded))
    mine, *swaps = pl.pallas_call(
        functools.partial(prepare_kernel, tall),
        out_shape=(jax.ShapeDtypeStruct((rows, span), jnp.float32),)
        + (jax.ShapeDtypeStruct((rows, order), jnp.float32),) * depth,
        in_specs=[WHOLE] * 3,
        out_specs=(WHOLE,) * (1 + depth),
        cost_estimate=LIGHT,
    )(presence, blocks, own)
    return mine, swaps


def ordered_kernel(flips, *refs):
    columns = refs[-1]
    _, order, _ = columns.shape
    for flip, strip in zip(flips, refs[:-1]):
        at = (lax.axis_index("row") ^ flip) >> 1
        for a in range(strip.shape[0] // order):
            columns[a * len(flips) + at] = strip[pl.ds(a * order, order), :]


def ordered(strips, flips, order):
    rows, span = strips[0].shape
    return pl.pallas_call(
        functools.partial(ordered_kernel, flips),
        out_shape=jax.ShapeDtypeStruct((rows // order * len(strips), order, span), jnp.float32),
        in_specs=[WHOLE] * len(strips),
        out_specs=WHOLE,
        cost_estimate=pl.CostEstimate(flops=HEAVY, bytes_accessed=1000, transcendentals=0),
        compiler_params=ROOM,
    )(*strips)


def partials_kernel(count, *refs):
    held, mate = refs[:2]
    block_cols, rows, order = held.shape
    far = (count - 1) * block_cols
    ours, theirs, refs = refs[2 : 2 + far], refs[2 + far : 2 + 2 * far], refs[2 + 2 * far :]
    columns, both = refs
    col_index = lax.axis_index("col")
    left, right = [], []
    for t in range(count):
        for b in range(block_cols):
            if t:
                at = (t - 1) * block_cols + b
                pair = [ours[at][...], theirs[at][...]]
            else:
                pair = [held[b], mate[b]]
            left.append(jnp.concatenate(pair, axis=0))
            right.append(columns[b * count + ((col_index >> 1) ^ t)])
    summed = product(jnp.concatenate(left, axis=1), jnp.concatenate(right, axis=0), ((1,), (0,)))
    here = (col_index & 1) * rows
    both[pl.ds(pl.multiple_of(here, 8), rows), :] = summed[:rows]
    both[pl.ds(pl.multiple_of(rows - here, 8), rows), :] = summed[rows:]


def partials(held, mate, ours, theirs, columns):
    block_cols, rows, _ = held.shape
    operands = (held, mate, *ours, *theirs, columns)
    return pl.pallas_call(
        functools.partial(partials_kernel, 1 + len(ours) // block_cols),
        out_shape=jax.ShapeDtypeStruct((2 * rows, columns.shape[2]), jnp.float32),
        in_specs=[WHOLE] * len(operands),
        out_specs=WHOLE,
        cost_estimate=LIGHT,
        compiler_params=ROOM,
    )(*operands)


def stay_kernel(tall, own, stay):
    stay[...] = parity_half(own[...], tall, lax.axis_index("row") & 1)


def stay_half(own, tall):
    rows, width = own.shape
    return pl.pallas_call(
        functools.partial(stay_kernel, tall),
        out_shape=jax.ShapeDtypeStruct((rows, width // 2), jnp.float32),
        in_specs=[WHOLE],
        out_specs=WHOLE,
        cost_estimate=LIGHT,
        compiler_params=ROOM,
    )(own)


def finish_kernel(order, flips, both, got, stay, swapped, mate_swapped, dinv, *refs):
    update, terms = refs[-2:]
    along, outward = refs[: len(flips)], refs[len(flips) : -2]
    rows = stay.shape[0]
    row_index = lax.axis_index("row")
    col_index = lax.axis_index("col")
    here = (row_index & 1) * rows
    update[...] = both[...] + got[...]
    mine = update[pl.ds(pl.multiple_of(here, 8), rows), :]
    other = update[pl.ds(pl.multiple_of(rows - here, 8), rows), :]
    same = (row_index & 1) == (col_index & 1)
    depth = stay.shape[1] // swapped.shape[2]
    near = [jnp.where(same, swapped[j], mate_swapped[j]) for j in range(depth)]
    factors = jnp.concatenate([stay[...], jnp.concatenate(near, axis=1)], axis=0)
    terms[...] = product(factors, jnp.concatenate([mine, other], axis=0), ((0,), (0,)))
    tall = dinv.shape[0]
    for flip, piece in zip(flips, along):
        slot = ((row_index ^ flip) >> 1) * tall
        piece[...] = terms[pl.ds(pl.multiple_of(slot, 8), tall), :]
    along[0][...] = along[0][...] + dinv[...]
    share = order // len(outward)
    for flip, piece in enumerate(outward):
        start = here + (col_index ^ flip) * share
        for a in range(rows // order):
            picked = update[pl.ds(pl.multiple_of(a * order + start, 8), share), :]
            piece[pl.ds(a * share, share), :] = -picked


def finish(both, got, stay, swapped, mate_swapped, dinv, order, flips, receivers):
    rows, half = stay.shape
    span = both.shape[1]
    along = (jax.ShapeDtypeStruct(dinv.shape, jnp.float32),) * len(flips)
    outward = (jax.ShapeDtypeStruct((rows // receivers, span), jnp.float32),) * receivers
    outs = pl.pallas_call(
        functools.partial(finish_kernel, order, flips),
        out_shape=along + outward,
        in_specs=[WHOLE] * 6,
        out_specs=(WHOLE,) * (len(flips) + receivers),
        scratch_shapes=[
            pltpu.VMEM((2 * rows, span), jnp.float32),
            pltpu.VMEM((half, span), jnp.float32),
        ],
        cost_estimate=LIGHT,
        compiler_params=ROOM,
    )(both, got, stay, swapped, mate_swapped, dinv)
    return outs[: len(flips)], outs[len(flips) :]


def at_place(ref, place):
    return ref[...] if place is None else ref[place]


def joined_kernel(places, *refs):
    for at, (place, ref) in enumerate(zip(places, refs[:-1])):
        refs[-1][at] = at_place(ref, place)


def joined(pieces):
    shape = pieces[0][0].shape[-2:]
    return pl.pallas_call(
        functools.partial(joined_kernel, [place for _, place in pieces]),
        out_shape=jax.ShapeDtypeStruct((len(pieces),) + shape, jnp.float32),
        in_specs=[WHOLE] * len(pieces),
        out_specs=WHOLE,
        cost_estimate=LIGHT,
        compiler_params=ROOM,
    )(*[array for array, _ in pieces])


def swap_over_col(outward):
    pieces = {(0, flip): (piece, None) for flip, piece in enumerate(outward)}
    bit = len(outward) // 2
    while bit:
        keys = [key for key in sorted(pieces) if key[1] & bit]
        came = flipped(joined([pieces.pop(key) for key in keys]), "col", bit)
        for at, (source, flip) in enumerate(keys):
            pieces[source ^ bit, flip ^ bit] = (came, at)
        bit //= 2
    return [pieces[source, 0] for source in range(len(outward))]


def close_kernel(count, places, *refs):
    met, arrived = refs[:count], refs[count:-2]
    off_diag, diag_block = refs[-2:]
    span = arrived[0].shape[-1]
    for flip, (piece, place) in enumerate(zip(arrived, places)):
        first = pl.multiple_of((lax.axis_index("col") ^ flip) * span, LANES)
        off_diag[:, pl.ds(first, span)] = at_place(piece, place)
    diag_block[...] = sum([piece[...] for piece in met[1:]], met[0][...])


def close(arrived, met):
    share, span = arrived[0][0].shape[-2:]
    if span % LANES:
        me = lax.axis_index("col")
        pieces = [array if place is None else array[place] for array, place in arrived]
        laid = [lax.select_n(me ^ j, *pieces) for j in range(len(pieces))]
        return jnp.concatenate(laid, axis=1), sum(met[1:], met[0])
    return pl.pallas_call(
        functools.partial(close_kernel, len(met), [place for _, place in arrived]),
        out_shape=(
            jax.ShapeDtypeStruct((share, span * len(arrived)), jnp.float32),
            jax.ShapeDtypeStruct(met[0].shape, jnp.float32),
        ),
        in_specs=[WHOLE] * (len(arrived) + len(met)),
        out_specs=(WHOLE, WHOLE),
        cost_estimate=LIGHT,
        compiler_params=ROOM,
    )(*met, *[array for array, _ in arrived])


def pick_kernel(block_cols, b, presence, blocks, swapped, held):
    same = (lax.axis_index("row") & 1) == (lax.axis_index("col") & 1)
    rows, order = held.shape
    for a in range(rows // order):
        here = pl.ds(a * order, order)
        block = masked_block(presence, blocks, block_cols, a, b)
        held[here, :] = jnp.where(same, block, swapped[here, :])


def pick(presence, blocks, swapped, b):
    return pl.pallas_call(
        functools.partial(pick_kernel, blocks.shape[0] // swapped.shape[0], b),
        out_shape=jax.ShapeDtypeStruct(swapped.shape, jnp.float32),
        in_specs=[WHOLE] * 3,
        out_specs=WHOLE,
        cost_estimate=LIGHT,
        compiler_params=ROOM,
    )(presence, blocks, swapped)


def stacked_kernel(*refs):
    for at, piece in enumerate(refs[:-1]):
        refs[-1][at] = piece[...]


def stacked(pieces):
    return pl.pallas_call(
        stacked_kernel,
        out_shape=jax.ShapeDtypeStruct((len(pieces),) + pieces[0].shape, jnp.float32),
        in_specs=[WHOLE] * len(pieces),
        out_specs=WHOLE,
        cost_estimate=LIGHT,
        compiler_params=ROOM,
    )(*pieces)


def crossed(swap):
    groups_row = lax.axis_size("row")
    groups_col = lax.axis_size("col")
    cross = [
        (r * groups_col + c, (r ^ 1) * groups_col + (c ^ 1))
        for r in range(groups_row)
        for c in range(groups_col)
    ]
    return lax.ppermute(swap, ("row", "col"), cross)


def along_line(mine, order):
    strips, flips = [mine], [0]
    bit = lax.axis_size("row") // 2
    while bit > 1:
        strips = strips + [flipped(strip, "row", bit) for strip in strips]
        flips = flips + [flip ^ bit for flip in flips]
        bit //= 2
    return ordered(strips, tuple(flips), order)


def local(inverse_set, presence, factor, dinv):
    groups_row = lax.axis_size("row")
    groups_col = lax.axis_size("col")
    block_rows, _, order, width = factor.shape
    block_cols = inverse_set.shape[3]
    span = width // groups_col
    rows = block_rows * order
    share = order // groups_col

    own = factor.reshape(rows, width)
    blocks = inverse_set.reshape(rows * block_cols, order)
    marks = presence.reshape(1, -1)
    tall = width // groups_row
    mine, swaps = prepare(marks, blocks, own, span, tall)
    swapped = [crossed(swap) for swap in swaps]
    stay = stay_half(own, tall)
    columns = along_line(mine, order)
    held = [pick(marks, blocks, swapped[b], b) for b in range(block_cols)]
    far = [(flip, piece) for flip in range(2, groups_col, 2) for piece in held]
    ours = [flipped(piece, "col", flip) for flip, piece in far]
    theirs = [flipped(piece, "col", 1) for piece in ours]
    held, swapped = stacked(held), stacked(swapped)
    mate, mate_swapped = flipped(held, "col", 1), flipped(swapped, "col", 1)

    both = partials(held, mate, ours, theirs, columns)
    got = flipped(both, "row", 1)
    flips = (0, *range(groups_row - 2, 0, -2))
    along, outward = finish(
        both, got, stay, swapped, mate_swapped, dinv, order, flips, groups_col
    )
    met = [flipped(piece, "row", flip) if flip else piece for flip, piece in zip(flips, along)]
    off_diag, diag_block = close(swap_over_col(outward), met)
    return (off_diag.reshape(block_rows, 1, share, width), diag_block)


def solution(mesh):
    in_specs = (
        P(None, "row", None, None, "col", None),
        P(None, "row", None, "col"),
        P(None, "row", None, None),
        P("row", "col"),
    )
    out_specs = (P(None, "row", "col", None), P("row", "col"))
    return jax.shard_map(local, mesh=mesh, in_specs=in_specs, out_specs=out_specs, check_vma=False)
```

```python
import functools

import jax
import jax.numpy as jnp
from jax import lax
from jax.experimental import pallas as pl
from jax.experimental.pallas import tpu as pltpu
from jax.sharding import PartitionSpec as P

LANES = 128
WHOLE = pl.BlockSpec(memory_space=pltpu.VMEM)
ROOM = pltpu.CompilerParams(vmem_limit_bytes=16 * 1024 * 1024)
HEAVY = 10**9
LIGHT = pl.CostEstimate(flops=1000, bytes_accessed=1000, transcendentals=0)


def flipped(value, axis, flip):
    return lax.ppermute(value, axis, [(i, i ^ flip) for i in range(lax.axis_size(axis))])


def two_parts(value):
    high = value.astype(jnp.bfloat16)
    return high, (value - high.astype(jnp.float32)).astype(jnp.bfloat16)


def product(left, right, contract):
    left_high, left_low = two_parts(left)
    right_high, right_low = two_parts(right)

    def once(a, b):
        return lax.dot_general(a, b, (contract, ((), ())), preferred_element_type=jnp.float32)

    return once(left_high, right_high) + (once(left_high, right_low) + once(left_low, right_high))


def parity_half(factor, tall, parity):
    even, odd = [
        jnp.concatenate(
            [factor[:, i : i + tall] for i in range(first, factor.shape[1], 2 * tall)], axis=1
        )
        for first in (0, tall)
    ]
    return jnp.where(parity == 1, odd, even)


def masked_block(presence, blocks, block_cols, a, b):
    order = blocks.shape[1]
    at = a * block_cols + b
    weight = presence[:, at : at + 1].astype(jnp.float32)
    return blocks[pl.ds(a * order * block_cols + b, order, stride=block_cols), :] * weight


def prepare_kernel(tall, presence, blocks, factor, mine, *swaps):
    rows, span = mine.shape
    mine[...] = factor[:, pl.ds(pl.multiple_of(lax.axis_index("col") * span, LANES), span)]
    row_bit = lax.axis_index("row") & 1
    same = row_bit == (lax.axis_index("col") & 1)
    order = blocks.shape[1]
    block_cols = blocks.shape[0] // rows
    half = parity_half(factor[...], tall, 1 - row_bit)
    for b, swap in enumerate(swaps):
        for a in range(rows // order):
            here = pl.ds(a * order, order)
            part = half[a * order : (a + 1) * order, b * order : (b + 1) * order]
            if b >= block_cols:
                swap[here, :] = part
                continue
            block = masked_block(presence, blocks, block_cols, a, b)
            swap[here, :] = jnp.where(same, part, block) if part.shape[1] else block


def prepare(presence, blocks, own, span, tall):
    rows, width = own.shape
    block_cols = blocks.shape[0] // rows
    order = blocks.shape[1]
    depth = max(block_cols, width // 2 // order)
    if span % LANES:
        first = lax.axis_index("col") * span
        row_bit = lax.axis_index("row") & 1
        same = row_bit == (lax.axis_index("col") & 1)
        mine = lax.dynamic_slice_in_dim(own, first, span, 1)
        weights = presence.reshape(-1, 1, block_cols, 1).astype(jnp.float32)
        picked = blocks.reshape(-1, order, block_cols, order) * weights
        masked = picked.transpose(2, 0, 1, 3).reshape(block_cols, rows, order)
        half = parity_half(own, tall, 1 - row_bit).reshape(rows, -1, order).transpose(1, 0, 2)
        half = jnp.pad(half, ((0, depth - half.shape[0]), (0, 0), (0, 0)))
        padded = jnp.pad(masked, ((0, depth - block_cols), (0, 0), (0, 0)))
        return mine, list(jnp.where(same, half, padded))
    mine, *swaps = pl.pallas_call(
        functools.partial(prepare_kernel, tall),
        out_shape=(jax.ShapeDtypeStruct((rows, span), jnp.float32),)
        + (jax.ShapeDtypeStruct((rows, order), jnp.float32),) * depth,
        in_specs=[WHOLE] * 3,
        out_specs=(WHOLE,) * (1 + depth),
        cost_estimate=LIGHT,
    )(presence, blocks, own)
    return mine, swaps


def ordered_kernel(flips, *refs):
    columns = refs[-1]
    _, order, _ = columns.shape
    for flip, strip in zip(flips, refs[:-1]):
        at = (lax.axis_index("row") ^ flip) >> 1
        for a in range(strip.shape[0] // order):
            columns[a * len(flips) + at] = strip[pl.ds(a * order, order), :]


def ordered(strips, flips, order):
    rows, span = strips[0].shape
    return pl.pallas_call(
        functools.partial(ordered_kernel, flips),
        out_shape=jax.ShapeDtypeStruct((rows // order * len(strips), order, span), jnp.float32),
        in_specs=[WHOLE] * len(strips),
        out_specs=WHOLE,
        cost_estimate=pl.CostEstimate(flops=HEAVY, bytes_accessed=1000, transcendentals=0),
        compiler_params=ROOM,
    )(*strips)


def partials_kernel(count, *refs):
    held, mate = refs[:2]
    block_cols, rows, order = held.shape
    far = (count - 1) * block_cols
    ours, theirs, refs = refs[2 : 2 + far], refs[2 + far : 2 + 2 * far], refs[2 + 2 * far :]
    columns, both = refs
    col_index = lax.axis_index("col")
    left, right = [], []
    for t in range(count):
        for b in range(block_cols):
            if t:
                at = (t - 1) * block_cols + b
                pair = [ours[at][...], theirs[at][...]]
            else:
                pair = [held[b], mate[b]]
            left.append(jnp.concatenate(pair, axis=0))
            right.append(columns[b * count + ((col_index >> 1) ^ t)])
    summed = product(jnp.concatenate(left, axis=1), jnp.concatenate(right, axis=0), ((1,), (0,)))
    here = (col_index & 1) * rows
    both[pl.ds(pl.multiple_of(here, 8), rows), :] = summed[:rows]
    both[pl.ds(pl.multiple_of(rows - here, 8), rows), :] = summed[rows:]


def partials(held, mate, ours, theirs, columns):
    block_cols, rows, _ = held.shape
    operands = (held, mate, *ours, *theirs, columns)
    return pl.pallas_call(
        functools.partial(partials_kernel, 1 + len(ours) // block_cols),
        out_shape=jax.ShapeDtypeStruct((2 * rows, columns.shape[2]), jnp.float32),
        in_specs=[WHOLE] * len(operands),
        out_specs=WHOLE,
        cost_estimate=LIGHT,
        compiler_params=ROOM,
    )(*operands)


def stay_kernel(tall, own, stay):
    stay[...] = parity_half(own[...], tall, lax.axis_index("row") & 1)


def stay_half(own, tall):
    rows, width = own.shape
    return pl.pallas_call(
        functools.partial(stay_kernel, tall),
        out_shape=jax.ShapeDtypeStruct((rows, width // 2), jnp.float32),
        in_specs=[WHOLE],
        out_specs=WHOLE,
        cost_estimate=LIGHT,
        compiler_params=ROOM,
    )(own)


def finish_kernel(order, flips, both, got, stay, swapped, mate_swapped, dinv, *refs):
    update, terms = refs[-2:]
    along, outward = refs[: len(flips)], refs[len(flips) : -2]
    rows = stay.shape[0]
    row_index = lax.axis_index("row")
    col_index = lax.axis_index("col")
    here = (row_index & 1) * rows
    update[...] = both[...] + got[...]
    mine = update[pl.ds(pl.multiple_of(here, 8), rows), :]
    other = update[pl.ds(pl.multiple_of(rows - here, 8), rows), :]
    same = (row_index & 1) == (col_index & 1)
    depth = stay.shape[1] // swapped.shape[2]
    near = [jnp.where(same, swapped[j], mate_swapped[j]) for j in range(depth)]
    factors = jnp.concatenate([stay[...], jnp.concatenate(near, axis=1)], axis=0)
    terms[...] = product(factors, jnp.concatenate([mine, other], axis=0), ((0,), (0,)))
    tall = dinv.shape[0]
    for flip, piece in zip(flips, along):
        slot = ((row_index ^ flip) >> 1) * tall
        piece[...] = terms[pl.ds(pl.multiple_of(slot, 8), tall), :]
    along[0][...] = along[0][...] + dinv[...]
    share = order // len(outward)
    for flip, piece in enumerate(outward):
        start = here + (col_index ^ flip) * share
        for a in range(rows // order):
            picked = update[pl.ds(pl.multiple_of(a * order + start, 8), share), :]
            piece[pl.ds(a * share, share), :] = -picked


def finish(both, got, stay, swapped, mate_swapped, dinv, order, flips, receivers):
    rows, half = stay.shape
    span = both.shape[1]
    along = (jax.ShapeDtypeStruct(dinv.shape, jnp.float32),) * len(flips)
    outward = (jax.ShapeDtypeStruct((rows // receivers, span), jnp.float32),) * receivers
    outs = pl.pallas_call(
        functools.partial(finish_kernel, order, flips),
        out_shape=along + outward,
        in_specs=[WHOLE] * 6,
        out_specs=(WHOLE,) * (len(flips) + receivers),
        scratch_shapes=[
            pltpu.VMEM((2 * rows, span), jnp.float32),
            pltpu.VMEM((half, span), jnp.float32),
        ],
        cost_estimate=LIGHT,
        compiler_params=ROOM,
    )(both, got, stay, swapped, mate_swapped, dinv)
    return outs[: len(flips)], outs[len(flips) :]


def at_place(ref, place):
    return ref[...] if place is None else ref[place]


def joined_kernel(places, *refs):
    for at, (place, ref) in enumerate(zip(places, refs[:-1])):
        refs[-1][at] = at_place(ref, place)


def joined(pieces):
    shape = pieces[0][0].shape[-2:]
    return pl.pallas_call(
        functools.partial(joined_kernel, [place for _, place in pieces]),
        out_shape=jax.ShapeDtypeStruct((len(pieces),) + shape, jnp.float32),
        in_specs=[WHOLE] * len(pieces),
        out_specs=WHOLE,
        cost_estimate=LIGHT,
        compiler_params=ROOM,
    )(*[array for array, _ in pieces])


def swap_over_col(outward):
    pieces = {(0, flip): (piece, None) for flip, piece in enumerate(outward)}
    bit = len(outward) // 2
    while bit:
        keys = [key for key in sorted(pieces) if key[1] & bit]
        came = flipped(joined([pieces.pop(key) for key in keys]), "col", bit)
        for at, (source, flip) in enumerate(keys):
            pieces[source ^ bit, flip ^ bit] = (came, at)
        bit //= 2
    return [pieces[source, 0] for source in range(len(outward))]


def close_kernel(count, places, *refs):
    met, arrived = refs[:count], refs[count:-2]
    off_diag, diag_block = refs[-2:]
    span = arrived[0].shape[-1]
    for flip, (piece, place) in enumerate(zip(arrived, places)):
        first = pl.multiple_of((lax.axis_index("col") ^ flip) * span, LANES)
        off_diag[:, pl.ds(first, span)] = at_place(piece, place)
    diag_block[...] = sum([piece[...] for piece in met[1:]], met[0][...])


def close(arrived, met):
    share, span = arrived[0][0].shape[-2:]
    if span % LANES:
        me = lax.axis_index("col")
        pieces = [array if place is None else array[place] for array, place in arrived]
        laid = [lax.select_n(me ^ j, *pieces) for j in range(len(pieces))]
        return jnp.concatenate(laid, axis=1), sum(met[1:], met[0])
    return pl.pallas_call(
        functools.partial(close_kernel, len(met), [place for _, place in arrived]),
        out_shape=(
            jax.ShapeDtypeStruct((share, span * len(arrived)), jnp.float32),
            jax.ShapeDtypeStruct(met[0].shape, jnp.float32),
        ),
        in_specs=[WHOLE] * (len(arrived) + len(met)),
        out_specs=(WHOLE, WHOLE),
        cost_estimate=LIGHT,
        compiler_params=ROOM,
    )(*met, *[array for array, _ in arrived])


def pick_kernel(block_cols, b, presence, blocks, swapped, held):
    same = (lax.axis_index("row") & 1) == (lax.axis_index("col") & 1)
    rows, order = held.shape
    for a in range(rows // order):
        here = pl.ds(a * order, order)
        block = masked_block(presence, blocks, block_cols, a, b)
        held[here, :] = jnp.where(same, block, swapped[here, :])


def pick(presence, blocks, swapped, b):
    return pl.pallas_call(
        functools.partial(pick_kernel, blocks.shape[0] // swapped.shape[0], b),
        out_shape=jax.ShapeDtypeStruct(swapped.shape, jnp.float32),
        in_specs=[WHOLE] * 3,
        out_specs=WHOLE,
        cost_estimate=LIGHT,
        compiler_params=ROOM,
    )(presence, blocks, swapped)


def stacked_kernel(*refs):
    for at, piece in enumerate(refs[:-1]):
        refs[-1][at] = piece[...]


def stacked(pieces):
    return pl.pallas_call(
        stacked_kernel,
        out_shape=jax.ShapeDtypeStruct((len(pieces),) + pieces[0].shape, jnp.float32),
        in_specs=[WHOLE] * len(pieces),
        out_specs=WHOLE,
        cost_estimate=LIGHT,
        compiler_params=ROOM,
    )(*pieces)


def crossed(swap):
    groups_row = lax.axis_size("row")
    groups_col = lax.axis_size("col")
    cross = [
        (r * groups_col + c, (r ^ 1) * groups_col + (c ^ 1))
        for r in range(groups_row)
        for c in range(groups_col)
    ]
    return lax.ppermute(swap, ("row", "col"), cross)


def along_line(mine, order):
    strips, flips = [mine], [0]
    bit = lax.axis_size("row") // 2
    while bit > 1:
        strips = strips + [flipped(strip, "row", bit) for strip in strips]
        flips = flips + [flip ^ bit for flip in flips]
        bit //= 2
    return ordered(strips, tuple(flips), order)


def local(inverse_set, presence, factor, dinv):
    groups_row = lax.axis_size("row")
    groups_col = lax.axis_size("col")
    block_rows, _, order, width = factor.shape
    block_cols = inverse_set.shape[3]
    span = width // groups_col
    rows = block_rows * order
    share = order // groups_col

    own = factor.reshape(rows, width)
    blocks = inverse_set.reshape(rows * block_cols, order)
    marks = presence.reshape(1, -1)
    tall = width // groups_row
    mine, swaps = prepare(marks, blocks, own, span, tall)
    swapped = [crossed(swap) for swap in swaps]
    stay = stay_half(own, tall)
    columns = along_line(mine, order)
    held = [pick(marks, blocks, swapped[b], b) for b in range(block_cols)]
    far = [(flip, piece) for flip in range(2, groups_col, 2) for piece in held]
    ours = [flipped(piece, "col", flip) for flip, piece in far]
    theirs = [flipped(piece, "col", 1) for piece in ours]
    held, swapped = stacked(held), stacked(swapped)
    mate, mate_swapped = flipped(held, "col", 1), flipped(swapped, "col", 1)

    both = partials(held, mate, ours, theirs, columns)
    got = flipped(both, "row", 1)
    flips = (0, *range(4, groups_row, 2), 2)
    along, outward = finish(
        both, got, stay, swapped, mate_swapped, dinv, order, flips, groups_col
    )
    met = [flipped(piece, "row", flip) if flip else piece for flip, piece in zip(flips, along)]
    off_diag, diag_block = close(swap_over_col(outward), met)
    return (off_diag.reshape(block_rows, 1, share, width), diag_block)


def solution(mesh):
    in_specs = (
        P(None, "row", None, None, "col", None),
        P(None, "row", None, "col"),
        P(None, "row", None, None),
        P("row", "col"),
    )
    out_specs = (P(None, "row", "col", None), P("row", "col"))
    return jax.shard_map(local, mesh=mesh, in_specs=in_specs, out_specs=out_specs, check_vma=False)
```

```python
import functools

import jax
import jax.numpy as jnp
from jax import lax
from jax.experimental import pallas as pl
from jax.experimental.pallas import tpu as pltpu
from jax.sharding import PartitionSpec as P

LANES = 128
WHOLE = pl.BlockSpec(memory_space=pltpu.VMEM)
ROOM = pltpu.CompilerParams(vmem_limit_bytes=16 * 1024 * 1024)
HEAVY = 10**9
LIGHT = pl.CostEstimate(flops=1000, bytes_accessed=1000, transcendentals=0)


def flipped(value, axis, flip):
    return lax.ppermute(value, axis, [(i, i ^ flip) for i in range(lax.axis_size(axis))])


def two_parts(value):
    high = value.astype(jnp.bfloat16)
    return high, (value - high.astype(jnp.float32)).astype(jnp.bfloat16)


def product(left, right, contract):
    left_high, left_low = two_parts(left)
    right_high, right_low = two_parts(right)

    def once(a, b):
        return lax.dot_general(a, b, (contract, ((), ())), preferred_element_type=jnp.float32)

    return once(left_high, right_high) + (once(left_high, right_low) + once(left_low, right_high))


def parity_half(factor, tall, parity):
    even, odd = [
        jnp.concatenate(
            [factor[:, i : i + tall] for i in range(first, factor.shape[1], 2 * tall)], axis=1
        )
        for first in (0, tall)
    ]
    return jnp.where(parity == 1, odd, even)


def masked_block(presence, blocks, block_cols, a, b):
    order = blocks.shape[1]
    at = a * block_cols + b
    weight = presence[:, at : at + 1].astype(jnp.float32)
    return blocks[pl.ds(a * order * block_cols + b, order, stride=block_cols), :] * weight


def prepare_kernel(tall, presence, blocks, factor, mine, *swaps):
    rows, span = mine.shape
    mine[...] = factor[:, pl.ds(pl.multiple_of(lax.axis_index("col") * span, LANES), span)]
    row_bit = lax.axis_index("row") & 1
    same = row_bit == (lax.axis_index("col") & 1)
    order = blocks.shape[1]
    block_cols = blocks.shape[0] // rows
    half = parity_half(factor[...], tall, 1 - row_bit)
    for b, swap in enumerate(swaps):
        for a in range(rows // order):
            here = pl.ds(a * order, order)
            part = half[a * order : (a + 1) * order, b * order : (b + 1) * order]
            if b >= block_cols:
                swap[here, :] = part
                continue
            block = masked_block(presence, blocks, block_cols, a, b)
            swap[here, :] = jnp.where(same, part, block) if part.shape[1] else block


def prepare(presence, blocks, own, span, tall):
    rows, width = own.shape
    block_cols = blocks.shape[0] // rows
    order = blocks.shape[1]
    depth = max(block_cols, width // 2 // order)
    if span % LANES:
        first = lax.axis_index("col") * span
        row_bit = lax.axis_index("row") & 1
        same = row_bit == (lax.axis_index("col") & 1)
        mine = lax.dynamic_slice_in_dim(own, first, span, 1)
        weights = presence.reshape(-1, 1, block_cols, 1).astype(jnp.float32)
        picked = blocks.reshape(-1, order, block_cols, order) * weights
        masked = picked.transpose(2, 0, 1, 3).reshape(block_cols, rows, order)
        half = parity_half(own, tall, 1 - row_bit).reshape(rows, -1, order).transpose(1, 0, 2)
        half = jnp.pad(half, ((0, depth - half.shape[0]), (0, 0), (0, 0)))
        padded = jnp.pad(masked, ((0, depth - block_cols), (0, 0), (0, 0)))
        return mine, list(jnp.where(same, half, padded))
    mine, *swaps = pl.pallas_call(
        functools.partial(prepare_kernel, tall),
        out_shape=(jax.ShapeDtypeStruct((rows, span), jnp.float32),)
        + (jax.ShapeDtypeStruct((rows, order), jnp.float32),) * depth,
        in_specs=[WHOLE] * 3,
        out_specs=(WHOLE,) * (1 + depth),
        cost_estimate=LIGHT,
    )(presence, blocks, own)
    return mine, swaps


def ordered_kernel(flips, *refs):
    columns = refs[-1]
    _, order, _ = columns.shape
    for flip, strip in zip(flips, refs[:-1]):
        at = (lax.axis_index("row") ^ flip) >> 1
        for a in range(strip.shape[0] // order):
            columns[a * len(flips) + at] = strip[pl.ds(a * order, order), :]


def ordered(strips, flips, order):
    rows, span = strips[0].shape
    return pl.pallas_call(
        functools.partial(ordered_kernel, flips),
        out_shape=jax.ShapeDtypeStruct((rows // order * len(strips), order, span), jnp.float32),
        in_specs=[WHOLE] * len(strips),
        out_specs=WHOLE,
        cost_estimate=pl.CostEstimate(flops=HEAVY, bytes_accessed=1000, transcendentals=0),
        compiler_params=ROOM,
    )(*strips)


def partials_kernel(count, *refs):
    held, mate = refs[:2]
    block_cols, rows, order = held.shape
    far = (count - 1) * block_cols
    ours, theirs, refs = refs[2 : 2 + far], refs[2 + far : 2 + 2 * far], refs[2 + 2 * far :]
    columns, both = refs
    col_index = lax.axis_index("col")
    left, right = [], []
    for t in range(count):
        for b in range(block_cols):
            if t:
                at = (t - 1) * block_cols + b
                pair = [ours[at][...], theirs[at][...]]
            else:
                pair = [held[b], mate[b]]
            left.append(jnp.concatenate(pair, axis=0))
            right.append(columns[b * count + ((col_index >> 1) ^ t)])
    summed = product(jnp.concatenate(left, axis=1), jnp.concatenate(right, axis=0), ((1,), (0,)))
    here = (col_index & 1) * rows
    both[pl.ds(pl.multiple_of(here, 8), rows), :] = summed[:rows]
    both[pl.ds(pl.multiple_of(rows - here, 8), rows), :] = summed[rows:]


def partials(held, mate, ours, theirs, columns):
    block_cols, rows, _ = held.shape
    operands = (held, mate, *ours, *theirs, columns)
    return pl.pallas_call(
        functools.partial(partials_kernel, 1 + len(ours) // block_cols),
        out_shape=jax.ShapeDtypeStruct((2 * rows, columns.shape[2]), jnp.float32),
        in_specs=[WHOLE] * len(operands),
        out_specs=WHOLE,
        cost_estimate=LIGHT,
        compiler_params=ROOM,
    )(*operands)


def stay_kernel(tall, own, stay):
    stay[...] = parity_half(own[...], tall, lax.axis_index("row") & 1)


def stay_half(own, tall):
    rows, width = own.shape
    return pl.pallas_call(
        functools.partial(stay_kernel, tall),
        out_shape=jax.ShapeDtypeStruct((rows, width // 2), jnp.float32),
        in_specs=[WHOLE],
        out_specs=WHOLE,
        cost_estimate=LIGHT,
        compiler_params=ROOM,
    )(own)


def finish_kernel(order, flips, both, got, stay, swapped, mate_swapped, dinv, *refs):
    update, terms = refs[-2:]
    along, outward = refs[: len(flips)], refs[len(flips) : -2]
    rows = stay.shape[0]
    row_index = lax.axis_index("row")
    col_index = lax.axis_index("col")
    here = (row_index & 1) * rows
    update[...] = both[...] + got[...]
    mine = update[pl.ds(pl.multiple_of(here, 8), rows), :]
    other = update[pl.ds(pl.multiple_of(rows - here, 8), rows), :]
    same = (row_index & 1) == (col_index & 1)
    depth = stay.shape[1] // swapped.shape[2]
    near = [jnp.where(same, swapped[j], mate_swapped[j]) for j in range(depth)]
    factors = jnp.concatenate([stay[...], jnp.concatenate(near, axis=1)], axis=0)
    terms[...] = product(factors, jnp.concatenate([mine, other], axis=0), ((0,), (0,)))
    tall = dinv.shape[0]
    for flip, piece in zip(flips, along):
        slot = ((row_index ^ flip) >> 1) * tall
        piece[...] = terms[pl.ds(pl.multiple_of(slot, 8), tall), :]
    along[0][...] = along[0][...] + dinv[...]
    share = order // len(outward)
    for flip, piece in enumerate(outward):
        start = here + (col_index ^ flip) * share
        for a in range(rows // order):
            picked = update[pl.ds(pl.multiple_of(a * order + start, 8), share), :]
            piece[pl.ds(a * share, share), :] = -picked


def finish(both, got, stay, swapped, mate_swapped, dinv, order, flips, receivers):
    rows, half = stay.shape
    span = both.shape[1]
    along = (jax.ShapeDtypeStruct(dinv.shape, jnp.float32),) * len(flips)
    outward = (jax.ShapeDtypeStruct((rows // receivers, span), jnp.float32),) * receivers
    outs = pl.pallas_call(
        functools.partial(finish_kernel, order, flips),
        out_shape=along + outward,
        in_specs=[WHOLE] * 6,
        out_specs=(WHOLE,) * (len(flips) + receivers),
        scratch_shapes=[
            pltpu.VMEM((2 * rows, span), jnp.float32),
            pltpu.VMEM((half, span), jnp.float32),
        ],
        cost_estimate=LIGHT,
        compiler_params=ROOM,
    )(both, got, stay, swapped, mate_swapped, dinv)
    return outs[: len(flips)], outs[len(flips) :]


def at_place(ref, place):
    return ref[...] if place is None else ref[place]


def joined_kernel(places, *refs):
    for at, (place, ref) in enumerate(zip(places, refs[:-1])):
        refs[-1][at] = at_place(ref, place)


def joined(pieces):
    shape = pieces[0][0].shape[-2:]
    return pl.pallas_call(
        functools.partial(joined_kernel, [place for _, place in pieces]),
        out_shape=jax.ShapeDtypeStruct((len(pieces),) + shape, jnp.float32),
        in_specs=[WHOLE] * len(pieces),
        out_specs=WHOLE,
        cost_estimate=LIGHT,
        compiler_params=ROOM,
    )(*[array for array, _ in pieces])


def swap_over_col(outward):
    pieces = {(0, flip): (piece, None) for flip, piece in enumerate(outward)}
    bit = len(outward) // 2
    while bit:
        keys = [key for key in sorted(pieces) if key[1] & bit]
        came = flipped(joined([pieces.pop(key) for key in keys]), "col", bit)
        for at, (source, flip) in enumerate(keys):
            pieces[source ^ bit, flip ^ bit] = (came, at)
        bit //= 2
    return [pieces[source, 0] for source in range(len(outward))]


def close_kernel(count, places, *refs):
    met, arrived = refs[:count], refs[count:-2]
    off_diag, diag_block = refs[-2:]
    span = arrived[0].shape[-1]
    for flip, (piece, place) in enumerate(zip(arrived, places)):
        first = pl.multiple_of((lax.axis_index("col") ^ flip) * span, LANES)
        off_diag[:, pl.ds(first, span)] = at_place(piece, place)
    diag_block[...] = sum([piece[...] for piece in met[1:]], met[0][...])


def close(arrived, met):
    share, span = arrived[0][0].shape[-2:]
    if span % LANES:
        me = lax.axis_index("col")
        pieces = [array if place is None else array[place] for array, place in arrived]
        laid = [lax.select_n(me ^ j, *pieces) for j in range(len(pieces))]
        return jnp.concatenate(laid, axis=1), sum(met[1:], met[0])
    return pl.pallas_call(
        functools.partial(close_kernel, len(met), [place for _, place in arrived]),
        out_shape=(
            jax.ShapeDtypeStruct((share, span * len(arrived)), jnp.float32),
            jax.ShapeDtypeStruct(met[0].shape, jnp.float32),
        ),
        in_specs=[WHOLE] * (len(arrived) + len(met)),
        out_specs=(WHOLE, WHOLE),
        cost_estimate=LIGHT,
        compiler_params=ROOM,
    )(*met, *[array for array, _ in arrived])


def pick_kernel(block_cols, b, presence, blocks, swapped, held):
    same = (lax.axis_index("row") & 1) == (lax.axis_index("col") & 1)
    rows, order = held.shape
    for a in range(rows // order):
        here = pl.ds(a * order, order)
        block = masked_block(presence, blocks, block_cols, a, b)
        held[here, :] = jnp.where(same, block, swapped[here, :])


def pick(presence, blocks, swapped, b):
    return pl.pallas_call(
        functools.partial(pick_kernel, blocks.shape[0] // swapped.shape[0], b),
        out_shape=jax.ShapeDtypeStruct(swapped.shape, jnp.float32),
        in_specs=[WHOLE] * 3,
        out_specs=WHOLE,
        cost_estimate=LIGHT,
        compiler_params=ROOM,
    )(presence, blocks, swapped)


def stacked_kernel(*refs):
    for at, piece in enumerate(refs[:-1]):
        refs[-1][at] = piece[...]


def stacked(pieces):
    return pl.pallas_call(
        stacked_kernel,
        out_shape=jax.ShapeDtypeStruct((len(pieces),) + pieces[0].shape, jnp.float32),
        in_specs=[WHOLE] * len(pieces),
        out_specs=WHOLE,
        cost_estimate=LIGHT,
        compiler_params=ROOM,
    )(*pieces)


def crossed(swap):
    groups_row = lax.axis_size("row")
    groups_col = lax.axis_size("col")
    cross = [
        (r * groups_col + c, (r ^ 1) * groups_col + (c ^ 1))
        for r in range(groups_row)
        for c in range(groups_col)
    ]
    return lax.ppermute(swap, ("row", "col"), cross)


def along_line(mine, order):
    strips, flips = [mine], [0]
    bit = lax.axis_size("row") // 2
    while bit > 1:
        strips = strips + [flipped(strip, "row", bit) for strip in strips]
        flips = flips + [flip ^ bit for flip in flips]
        bit //= 2
    return ordered(strips, tuple(flips), order)


def local(inverse_set, presence, factor, dinv):
    groups_row = lax.axis_size("row")
    groups_col = lax.axis_size("col")
    block_rows, _, order, width = factor.shape
    block_cols = inverse_set.shape[3]
    span = width // groups_col
    rows = block_rows * order
    share = order // groups_col

    own = factor.reshape(rows, width)
    blocks = inverse_set.reshape(rows * block_cols, order)
    marks = presence.reshape(1, -1)
    tall = width // groups_row
    mine, swaps = prepare(marks, blocks, own, span, tall)
    swapped = [crossed(swap) for swap in swaps]
    stay = stay_half(own, tall)
    columns = along_line(mine, order)
    held = [pick(marks, blocks, swapped[b], b) for b in range(block_cols)]
    far = [(flip, piece) for flip in range(2, groups_col, 2) for piece in held]
    ours = [flipped(piece, "col", flip) for flip, piece in far]
    theirs = [flipped(piece, "col", 1) for piece in ours]
    held, swapped = stacked(held), stacked(swapped)
    mate, mate_swapped = flipped(held, "col", 1), flipped(swapped, "col", 1)

    both = partials(held, mate, ours, theirs, columns)
    got = flipped(both, "row", 1)
    flips = (0, 2, *range(groups_row - 2, 2, -2))
    along, outward = finish(
        both, got, stay, swapped, mate_swapped, dinv, order, flips, groups_col
    )
    met = [flipped(piece, "row", flip) if flip else piece for flip, piece in zip(flips, along)]
    off_diag, diag_block = close(swap_over_col(outward), met)
    return (off_diag.reshape(block_rows, 1, share, width), diag_block)


def solution(mesh):
    in_specs = (
        P(None, "row", None, None, "col", None),
        P(None, "row", None, "col"),
        P(None, "row", None, None),
        P("row", "col"),
    )
    out_specs = (P(None, "row", "col", None), P("row", "col"))
    return jax.shard_map(local, mesh=mesh, in_specs=in_specs, out_specs=out_specs, check_vma=False)
```
